32 devices in a mesh: dp: 2 (over x), sp: 4 (over y, core), tp: 4 (over z).
Axes of the slice: x: 2, y: 2, z: 4, core: 2. Of those that a mesh axis runs over, the one named last changes fastest.
Arguments:
- tokens: bfloat16 [1024, 4, 2048], P(('sp', 'tp'), 'dp'), may hold values from -6 to 6
- lengths: int32 [4, 8], P('dp'), may hold values from 1 to 769, 1024 in all within a row
- self_flags: int32 [4, 8], P('dp'), may hold values from 0 to 1
- episode_weight: float32 [4, 8], P('dp'), may hold values from 0.25 to 2
- ln1_gain: float32 [2048], replicated, may hold values from 0.5 to 1.5
- ln1_bias: float32 [2048], replicated, may hold values from -3 to 3
- w_qkv: bfloat16 [2048, 3, 2048], P(None, None, 'tp'), may hold values from -0.125 to 0.125
- w_out: bfloat16 [2048, 2048], P('tp'), may hold values from -2 to 2
- ln2_gain: float32 [2048], replicated, may hold values from 0.5 to 1.5
- ln2_bias: float32 [2048], replicated, may hold values from -3 to 3
- w_up: bfloat16 [2048, 8192], P(None, 'tp'), may hold values from -0.125 to 0.125
- w_down: bfloat16 [8192, 2048], P('tp'), may hold values from -0.0625 to 0.0625
- out_grad: bfloat16 [1024, 4, 2048], P(('sp', 'tp'), 'dp'), may hold values from -6 to 6
Outputs:
- output: bfloat16 [1024, 4, 2048], P(('sp', 'tp'), 'dp')
- grad_input: float32 [1024, 4, 2048], P(('sp', 'tp'), 'dp')
- grad_qkv: float32 [2048, 3, 2048], P(('dp', 'sp'), None, 'tp')
- grad_out_proj: float32 [2048, 2048], P('tp', ('dp', 'sp'))
- grad_up: float32 [2048, 8192], P(('dp', 'sp'), 'tp')
- grad_down: float32 [8192, 2048], P('tp', ('dp', 'sp'))
- norm_one_grads: float32 [2, 2048], replicated
- norm_two_grads: float32 [2, 2048], replicated
The draws below stay inside these ranges and needn't reach their ends.
Inputs may be any that keep to these rules, and one draw needn't show every extreme that they name: Each row's 8 episode lengths sum to 1024; in every row one episode has exactly the largest length.
All inputs are finite; a program needn't handle non-finite values.
Results may differ from the reference program's by a relative error of at most 0.02.
Values may be sent and summed in bfloat16 or wider, within the bound.
A program may use at most 192 MiB of HBM per device.

```python
import math
import jax
import jax.numpy as jnp
import numpy as np
from jax import lax

D = 2048
HEADS = 16
DH = 128
FF = 8192
SEQ = 1024
EPIS = 8
ROWS = 4
N_SP = 4


def with_ends(result, stream_key, smallest, largest):
    extent = result.shape
    spot = [jax.random.randint(jax.random.fold_in(stream_key, axis), (), 0, extent[axis]) for axis in range(len(extent))]
    result = result.at[tuple(spot)].set(smallest)
    longest = extent.index(max(extent))
    spot[longest] = (spot[longest] + 1) % extent[longest]
    return result.at[tuple(spot)].set(largest)


def level_of(rng, dims, cuts, low, top_value):
    def one(position, parts):
        draws = jax.random.uniform(jax.random.fold_in(jax.random.fold_in(rng, 6), position), (parts,), jnp.float32, low / len(cuts), top_value / len(cuts))
        return jnp.repeat(jnp.exp(draws), dims[position] // parts).reshape((-1,) + (1,) * (len(dims) - position - 1))

    loudness = one(*cuts[0])
    for cut in cuts[1:]:
        loudness = loudness * one(*cut)
    return loudness


def length_profile(amount, total, reach, slope):
    weights = [(1 << 20) // math.isqrt(grade ** slope) + 1 for grade in range(2, amount + 1)]
    rest, counts = total - reach - (amount - 1), [1] * (amount - 1)
    while rest > 0:
        candidates = [i for i in range(amount - 1) if counts[i] < reach]
        whole, budget = sum([weights[i] for i in candidates]), rest
        for i in candidates:
            more = min(reach - counts[i], max(1, budget * weights[i] // whole), rest)
            counts[i] = counts[i] + more
            rest = rest - more
    return np.array([reach] + counts)


def uneven(own_key, amount, total, most, slope):
    if amount == 2:
        one = jax.random.randint(own_key, (), max(1, total - most), min(most, total - 1) + 1)
        return jnp.stack([one, total - one])
    sizes = jnp.asarray(length_profile(amount, total, most, slope), jnp.int32)
    twos = (amount - 1) // 2
    giver, taker = sizes[1:1 + 2 * twos:2], sizes[2:2 + 2 * twos:2]
    room = jnp.minimum(giver - 1, most - taker)
    shifted = jax.random.randint(jax.random.fold_in(own_key, 1), (twos,), 0, 1 << 20) % (room + 1)
    sizes = sizes.at[1:1 + 2 * twos:2].set(giver - shifted).at[2:2 + 2 * twos:2].set(taker + shifted)
    return sizes[jax.random.permutation(jax.random.fold_in(own_key, 2), amount)]


def bell_draw(stream_key, shape, scale, limit, split=(), dtype=jnp.bfloat16):
    entries = scale * jax.random.normal(stream_key, shape, jnp.float32)
    if split:
        entries = entries * level_of(stream_key, shape, split, -0.22, 0.18)
    return jnp.clip(entries, -limit, limit).astype(dtype)


def setup_inputs(seed: int = 0) -> dict:
    streams_of = jax.random.split(jax.random.key(seed), 14)
    tokens = bell_draw(streams_of[0], (SEQ, ROWS, D), 1.0, 6.0, ((0, 16), (1, 2)))
    lengths = jax.vmap(lambda own: uneven(own, EPIS, SEQ, SEQ - SEQ // N_SP + 1, 2))(jax.random.split(streams_of[1], ROWS)).reshape((ROWS, EPIS)).astype(jnp.int32)
    self_flags = with_ends(jax.random.randint(streams_of[2], (ROWS, EPIS), 0, 2), jax.random.fold_in(streams_of[2], 1), 0, 1).astype(jnp.int32)
    episode_weight = jnp.clip(jnp.exp(math.log(2.0) - 2.0794415 * jax.random.uniform(streams_of[3], (ROWS, EPIS), jnp.float32) ** level_of(streams_of[3], (ROWS, EPIS), ((0, 2),), -0.2, 0.2)), 0.25, 2.0)
    ln1_gain = jnp.clip(1.0 + 0.1 * jax.random.normal(streams_of[4], (D,), jnp.float32), 0.5, 1.5)
    ln1_bias = bell_draw(streams_of[5], (D,), 0.5, 3.0, (), jnp.float32)
    w_qkv = bell_draw(streams_of[6], (D, 3, D), D ** -0.5, 0.125, ((2, 4),))
    w_out = bell_draw(streams_of[7], (D, D), (max(D // 256, 1)) ** -0.5, 2.0, ((0, 4),))
    ln2_gain = jnp.clip(1.0 + 0.1 * jax.random.normal(streams_of[8], (D,), jnp.float32), 0.5, 1.5)
    ln2_bias = bell_draw(streams_of[9], (D,), 0.5, 3.0, (), jnp.float32)
    w_up = bell_draw(streams_of[10], (D, FF), D ** -0.5, 0.125, ((1, 4),))
    w_down = bell_draw(streams_of[11], (FF, D), FF ** -0.5, 0.0625, ((0, 4),))
    out_grad = bell_draw(streams_of[12], (SEQ, ROWS, D), 1.0, 6.0, ((0, 16), (1, 2)))
    return {"tokens": tokens, "lengths": lengths, "self_flags": self_flags, "episode_weight": episode_weight, "ln1_gain": ln1_gain, "ln1_bias": ln1_bias, "w_qkv": w_qkv, "w_out": w_out, "ln2_gain": ln2_gain, "ln2_bias": ln2_bias, "w_up": w_up, "w_down": w_down, "out_grad": out_grad}


@jax.custom_vjp
def low(v):
    return lax.optimization_barrier(v.astype(jnp.bfloat16)).astype(jnp.float32)

@jax.custom_vjp
def low_back(v):
    return v

def low_keep(v):
    return (low(v), None)

def low_pass(kept, grad):
    return (grad,)

def back_keep(v):
    return (v, None)

def back_low(kept, grad):
    return (low(grad),)
low.defvjp(low_keep, low_pass)
low_back.defvjp(back_keep, back_low)
HIGH = lax.Precision.HIGHEST
EPSILON = 1e-05

def both_ways(value):
    return low_back(low(value))

def layer_norm(values, gain, bias):
    average = lax.optimization_barrier(jnp.mean(values, axis=-1, keepdims=True))
    centred = values - average
    variance = lax.optimization_barrier(jnp.mean(centred * centred, axis=-1, keepdims=True))
    return centred * lax.rsqrt(variance + EPSILON) * gain + bias

def forward_row(inputs, segment, params):
    ln1_gain, ln1_bias, w_qkv, w_out, ln2_gain, ln2_bias, w_up, w_down = params
    seq_len = inputs.shape[0]
    normed_one = low(layer_norm(inputs, ln1_gain, ln1_bias))
    projected = jnp.dot(normed_one, w_qkv.reshape(D, 3 * D), precision=HIGH).reshape(seq_len, 3, HEADS, DH)
    queries = both_ways(projected[:, 0])
    keys_all = both_ways(projected[:, 1])
    values_all = both_ways(projected[:, 2])
    raw_scores = jnp.einsum('qhd,khd->hqk', queries, keys_all, precision=HIGH) * DH ** (-0.5)
    raw_scores = low_back(raw_scores)
    places = jnp.arange(seq_len)
    allowed = (places[None, :] <= places[:, None]) & (segment[:, None] == segment[None, :])
    masked = jnp.where(allowed[None], raw_scores, -1e+30)
    peak = lax.optimization_barrier(jnp.max(masked, axis=-1, keepdims=True))
    expos = jnp.where(allowed[None], jnp.exp(masked - peak), 0.0)
    probs = low(expos / lax.optimization_barrier(jnp.sum(expos, axis=-1, keepdims=True)))
    attended = jnp.einsum('hqk,khd->qhd', probs, values_all, precision=HIGH).reshape(seq_len, D)
    attended = both_ways(attended)
    attn_out = low_back(jnp.dot(attended, w_out, precision=HIGH))
    middle = inputs + attn_out
    normed_two = low(layer_norm(middle, ln2_gain, ln2_bias))
    hidden_pre = low_back(jnp.dot(normed_two, w_up, precision=HIGH))
    activated = low(jax.nn.gelu(hidden_pre, approximate=False))
    branch = low_back(jnp.dot(activated, w_down, precision=HIGH))
    return middle + branch

def add_trees(first, second):
    return jax.tree.map(jnp.add, first, second)

def reference(tokens, lengths, self_flags, episode_weight, ln1_gain, ln1_bias, w_qkv, w_out, ln2_gain, ln2_bias, w_up, w_down, out_grad):
    params = tuple((item.astype(jnp.float32) for item in (ln1_gain, ln1_bias, w_qkv, w_out, ln2_gain, ln2_bias, w_up, w_down)))
    ends = jnp.cumsum(lengths, axis=1)
    places = jnp.arange(SEQ)
    segment = lax.optimization_barrier(jnp.sum((places[None, :, None] >= ends[:, None, :]).astype(jnp.int32), axis=2))
    factor = episode_weight.astype(jnp.float32) * (1.0 + self_flags.astype(jnp.float32))
    episode_ids = jnp.arange(EPIS)
    onehot = segment[:, :, None] == episode_ids[None, None, :]
    token_scale = lax.optimization_barrier(jnp.sum(jnp.where(onehot, factor[:, None, :], 0.0), axis=2))

    def one_row(totals, row_items):
        row_input, row_segment, row_scale, row_grad = row_items

        def row_forward(inputs, weights):
            return forward_row(inputs, row_segment, weights)
        outputs, pullback = jax.vjp(row_forward, row_input, params)
        grad_in, grad_params = pullback(row_grad * row_scale[:, None])
        return (add_trees(totals, grad_params), (outputs.astype(jnp.bfloat16), grad_in))
    zeros = jax.tree.map(jnp.zeros_like, params)
    row_inputs = jnp.moveaxis(tokens.astype(jnp.float32), 1, 0)
    row_grads = jnp.moveaxis(out_grad.astype(jnp.float32), 1, 0)
    totals, (outputs, grads_in) = lax.scan(one_row, zeros, (row_inputs, segment, token_scale, row_grads))
    g_ln1, b_ln1, g_qkv, g_out, g_ln2, b_ln2, g_up, g_down = totals
    norm_one_grads = jnp.stack([g_ln1, b_ln1])
    norm_two_grads = jnp.stack([g_ln2, b_ln2])
    return (jnp.moveaxis(outputs, 0, 1), jnp.moveaxis(grads_in, 0, 1), g_qkv, g_out, g_up, g_down, norm_one_grads, norm_two_grads)
```

```python
import jax
import jax.numpy as jnp
from jax import lax
from jax.experimental import pallas as pl
from jax.experimental.pallas import tpu as pltpu
from jax.sharding import PartitionSpec as P

DH = 128
EPSILON = 1e-05
NEG = -1e30
f32 = jnp.float32
bf16 = jnp.bfloat16
MESH = pl.DeviceIdType.MESH


def dot(a, b, ca, cb):
    return lax.dot_general(a, b, (((ca,), (cb,)), ((), ())), preferred_element_type=f32)


def lanes(start, size):
    if isinstance(start, int):
        return pl.ds(start, size)
    return pl.ds(pl.multiple_of(start, 128), size)


def rows_at(start, size):
    if isinstance(start, int):
        return pl.ds(start, size)
    return pl.ds(pl.multiple_of(start, 64), size)


def norm_parts(values):
    average = jnp.mean(values, axis=-1, keepdims=True)
    centred = values - average
    variance = jnp.mean(centred * centred, axis=-1, keepdims=True)
    inverse = lax.rsqrt(variance + EPSILON)
    return centred * inverse, inverse


def norm_back(unit, inverse, gain, grad):
    scaled = grad * gain
    first = jnp.mean(scaled, axis=-1, keepdims=True)
    second = jnp.mean(scaled * unit, axis=-1, keepdims=True)
    return inverse * (scaled - first - unit * second)


class Sizes:
    def __init__(self, mesh_shape, tokens, w_qkv, w_up, lengths):
        self.n_dp = mesh_shape["dp"]
        self.n_sp = mesh_shape["sp"]
        self.n_tp = mesh_shape["tp"]
        self.S = tokens[0]
        self.R = tokens[1]
        self.D = tokens[2]
        self.LW = w_qkv[2]
        self.F = w_up[1]
        self.E = lengths[1]
        self.T = self.S * self.n_tp
        self.SEQ = self.T * self.n_sp
        self.H = self.LW // DH
        self.pairs = self.n_dp == 2 and self.n_sp == 4


def wgrad_kinds(z):
    def part(n):
        return max(128, (n * 5 // 8) // 128 * 128)

    out, offset = {}, 0
    for name, n in (("down", z.F), ("up", z.F), ("out", z.LW), ("qkv", 3 * z.LW)):
        out[name] = (n, offset, part(n))
        offset += n
    return out, offset


def make_kernel(z):
    S, R, D, LW, F, T, SEQ, H = z.S, z.R, z.D, z.LW, z.F, z.T, z.SEQ, z.H
    RT = R * T
    kinds, w_lanes = wgrad_kinds(z)
    scale = DH ** (-0.5)
    PD = D // 8

    def kernel(
        tok, og, lens, flags, eweight, g1, b1, g2, b2, wqkv_hbm, wout_hbm, wup_hbm, wdn_hbm,
        y_out, gin, norms, ro, rx, ry, sw, tx, ty, ph, g1h, extra_g2, extra_gy, extra_gm, extra_act, extra_gpre,
        extra_gproj, extra_att,
        arena, wqkv, wout, ga, g2b, gyb, q, kv, act, gpre, gproj, att, part, part2, slots, slots2,
        mid, bias, ds, raw, stage, nr, total,
        ag_s, ag_r, rs_s, rs_r, kv_s, kv_r, dk_s, dk_r, x_s, x_r, w_s, w_r, n_s, n_r, loc, raw_sem, stg_sem,
        rt_sem, free_x, free_c, free_y,
    ):
        dp = lax.axis_index("dp")
        sp = lax.axis_index("sp")
        tp = lax.axis_index("tp")
        par = lax.rem(sp, 2)
        yy = lax.div(sp, 2)
        mate = sp + 1 - 2 * par
        far = lax.rem(sp + 2, 4)
        odp = 1 - dp
        kv_row = sp * T
        own = tp * S

        def remote(src, dst, ssem, rsem, device):
            return pltpu.make_async_remote_copy(
                src_ref=src, dst_ref=dst, send_sem=ssem, recv_sem=rsem, device_id=device, device_id_type=MESH
            )

        class Gather:
            def __init__(self, buf, i, r):
                self.buf, self.i, self.r = buf, i, r

            def copy(self, shard, way, hop):
                sl = self.buf.at[rows_at(self.r * T + shard * S, S), :]
                to = tp + 1 if way == 0 else tp - 1
                return remote(
                    sl, sl, ag_s.at[self.i, self.r, way * 3 + hop], ag_r.at[self.i, self.r, shard], (dp, sp, to)
                )

            def start(self):
                @pl.when(tp < 3)
                def _():
                    self.copy(tp, 0, 0).start()

                @pl.when(tp > 0)
                def _():
                    self.copy(tp, 1, 0).start()

            def step(self, hop):
                @pl.when(tp >= hop)
                def _():
                    self.copy(tp - hop, 0, 0).wait_recv()

                if hop < 3:

                    @pl.when((tp >= hop) & (tp < 3))
                    def _():
                        self.copy(tp - hop, 0, hop).start()

                @pl.when(tp <= 3 - hop)
                def _():
                    self.copy(tp + hop, 1, 0).wait_recv()

                if hop < 3:

                    @pl.when((tp <= 3 - hop) & (tp > 0))
                    def _():
                        self.copy(tp + hop, 1, hop).start()

            def drain(self):
                for hop in range(3):

                    @pl.when((tp >= hop) & (tp < 3))
                    def _(hop=hop):
                        self.copy(tp - hop, 0, hop).wait_send()

                    @pl.when((tp <= 3 - hop) & (tp > 0))
                    def _(hop=hop):
                        self.copy(tp + hop, 1, hop).wait_send()

        class Scatter:
            def __init__(self, buf, box, i, r):
                self.buf, self.box, self.i, self.r = buf, box, i, r

            def copy(self, way, k):
                o = 3 - k if way == 0 else k
                to = tp + 1 if way == 0 else tp - 1
                n = way * 3 + k
                return remote(
                    self.buf.at[pl.ds(self.r * T + o * S, S), :],
                    self.box.at[self.r, n],
                    rs_s.at[self.i, self.r, n],
                    rs_r.at[self.i, self.r, n],
                    (dp, sp, to),
                )

            def start(self):
                for k in range(3):

                    @pl.when(tp == 0)
                    def _(k=k):
                        self.copy(0, k).start()

                    @pl.when(tp == 3)
                    def _(k=k):
                        self.copy(1, k).start()

            def relay(self, way, k):
                o = 3 - k if way == 0 else k
                sl = pl.ds(self.r * T + o * S, S)
                self.copy(way, k).wait_recv()
                self.buf[sl, :] = (
                    self.buf[sl, :].astype(f32) + self.box[self.r, way * 3 + k].astype(f32)
                ).astype(bf16)
                self.copy(way, k).start()

            def step(self, k):
                if 3 - k > 1:

                    @pl.when((tp > 0) & (tp < 3 - k))
                    def _():
                        self.relay(0, k)

                if k < 2:

                    @pl.when((tp < 3) & (tp > k))
                    def _():
                        self.relay(1, k)

            def finish(self):
                total[...] = self.buf[rows_at(self.r * T + own, S), :].astype(f32)
                for o in range(1, 4):

                    @pl.when(tp == o)
                    def _(o=o):
                        self.copy(0, 3 - o).wait_recv()
                        total[...] += self.box[self.r, 3 - o].astype(f32)

                for o in range(0, 3):

                    @pl.when(tp == o)
                    def _(o=o):
                        self.copy(1, o).wait_recv()
                        total[...] += self.box[self.r, 3 + o].astype(f32)

            def drain(self):
                for k in range(3):

                    @pl.when(tp < 3 - k)
                    def _(k=k):
                        self.copy(0, k).wait_send()

                    @pl.when(tp > k)
                    def _(k=k):
                        self.copy(1, k).wait_send()

        class Keys:
            def __init__(self, r):
                self.r = r

            def copy(self, block, to, n):
                sl = kv.at[self.r, rows_at(block * T, T), :]
                return remote(sl, sl, kv_s.at[self.r, n], kv_r.at[self.r, block], (dp, to, tp))

            def start(self):
                @pl.when(sp < 2)
                def _():
                    self.copy(sp, sp + 2, 0).start()

                @pl.when(par == 0)
                def _():
                    self.copy(sp, sp + 1, 1).start()

            def step(self):
                for me, block, to in ((2, 0, 3), (3, 1, 2)):

                    @pl.when(sp == me)
                    def _(block=block, to=to):
                        self.copy(block, to, 0).wait_recv()
                        self.copy(block, to, 2).start()

            def finish(self):
                for me, block in ((1, 0), (2, 1), (3, 0), (3, 2)):

                    @pl.when(sp == me)
                    def _(block=block):
                        self.copy(block, 0, 0).wait_recv()

            def drain(self):
                @pl.when(sp < 2)
                def _():
                    self.copy(sp, sp + 2, 0).wait_send()

                @pl.when(par == 0)
                def _():
                    self.copy(sp, sp + 1, 1).wait_send()

                for me, block, to in ((2, 0, 3), (3, 1, 2)):

                    @pl.when(sp == me)
                    def _(block=block, to=to):
                        self.copy(block, to, 2).wait_send()

        KW = 2 * LW
        DK0 = 5 * RT
        DR0 = RT

        class KeyGrads:
            def __init__(self, r):
                self.r = r

            def src(self, block):
                return arena.at[pl.ds(DK0 + block * T, T), pl.ds(self.r * KW, KW)]

            def dst(self, box):
                return arena.at[pl.ds(DR0 + box * T, T), pl.ds(self.r * KW, KW)]

            def copy(self, block, to, box, n):
                return remote(
                    self.src(block), self.dst(box), dk_s.at[self.r, n], dk_r.at[self.r, box], (dp, to, tp)
                )

            def start(self):
                for me, block, to, box, n in ((3, 0, 2, 0, 0), (3, 2, 2, 1, 1), (2, 1, 3, 0, 0), (1, 0, 0, 1, 0)):

                    @pl.when(sp == me)
                    def _(block=block, to=to, box=box, n=n):
                        self.copy(block, to, box, n).start()

            def step(self):
                for me, block, to in ((2, 0, 0), (3, 1, 1)):

                    @pl.when(sp == me)
                    def _(block=block, to=to):
                        self.copy(block, to, 0, 2).wait_recv()
                        mine = pl.ds(DK0 + block * T, T)
                        col = pl.ds(self.r * KW, KW)
                        arena[mine, col] = (
                            arena[mine, col].astype(f32) + arena[pl.ds(DR0, T), col].astype(f32)
                        ).astype(bf16)
                        self.copy(block, to, 2, 2).start()

            def finish(self):
                col = pl.ds(self.r * KW, KW)
                there = pl.ds(self.r * T, T)
                to = pl.ds(LW, KW)
                for me, boxes in ((0, (1, 2)), (1, (2,)), (2, (1,)), (3, ())):

                    @pl.when(sp == me)
                    def _(me=me, boxes=boxes):
                        value = arena[pl.ds(DK0 + me * T, T), col].astype(f32)
                        for box in boxes:
                            self.copy(0, 0, box, 0).wait_recv()
                            value += arena[pl.ds(DR0 + box * T, T), col].astype(f32)
                        gproj[there, to] = value.astype(bf16)

            def drain(self):
                for me, block, to, box, n in (
                    (3, 0, 2, 0, 0), (3, 2, 2, 1, 1), (2, 1, 3, 0, 0), (1, 0, 0, 1, 0), (2, 0, 0, 2, 2), (3, 1, 1, 2, 2),
                ):

                    @pl.when(sp == me)
                    def _(block=block, to=to, box=box, n=n):
                        self.copy(block, to, box, n).wait_send()

        ends = []
        for r in range(R):
            run, row = 0, []
            for e in range(z.E):
                run = run + lens[r, e]
                row.append(run)
            ends.append(row)

        def first_norm(r):
            unit, _ = norm_parts(tok[:, r, :].astype(f32))
            ga[rows_at(r * T + own, S), :] = (unit * g1[...] + b1[...]).astype(bf16)

        def weighted_grad(r):
            place = sp * T + own + lax.broadcasted_iota(jnp.int32, (S, 1), 0)
            factor = jnp.full((S, 1), eweight[r, 0] * (1.0 + flags[r, 0].astype(f32)), f32)
            for e in range(1, z.E):
                factor = jnp.where(
                    place >= ends[r][e - 1], eweight[r, e] * (1.0 + flags[r, e].astype(f32)), factor
                )
            return og[:, r, :].astype(f32) * factor

        def raw_copy(i):
            n = raw.shape[1]
            slot = lax.rem(i, 2)
            return pltpu.make_async_copy(
                wqkv_hbm.at[rows_at(i * n, n), :, :], raw.at[slot], raw_sem.at[slot]
            )

        raw_steps = D // raw.shape[1]

        def relay_weights(low, high):
            n = raw.shape[1]

            def one(i, carry):
                @pl.when(i + 1 < raw_steps)
                def _():
                    raw_copy(i + 1).start()

                raw_copy(i).wait()
                slot = lax.rem(i, 2)
                for j in range(3):
                    wqkv[rows_at(i * n, n), j * LW : (j + 1) * LW] = raw[slot, :, j, :]
                return carry

            lax.fori_loop(low, high, one, 0)

        def project(r, j):
            value = dot(ga[r * T : (r + 1) * T, :], wqkv[:, j * LW : (j + 1) * LW], 1, 0).astype(bf16)
            if j == 0:
                q[r * T : (r + 1) * T, :] = value
            else:
                kv[r, rows_at(kv_row, T), (j - 1) * LW : j * LW] = value

        def mask(r):
            here = kv_row + lax.broadcasted_iota(jnp.int32, (T, 1), 0)
            begin = jnp.zeros((T, 1), jnp.int32)
            for e in range(z.E):
                begin = jnp.where(here >= ends[r][e], jnp.maximum(begin, ends[r][e]), begin)
            there = lax.broadcasted_iota(jnp.int32, (T, SEQ), 1)
            bias[...] = jnp.where((there <= here) & (there >= begin), 0.0, NEG)

        half = T // 2
        ppl = D // SEQ
        keep = [act, gpre]

        def attend(r):
            def one(i, carry):
                rs = rows_at(i * half, half)
                qs = rows_at(r * T + i * half, half)
                for h in range(H):
                    hs = slice(h * DH, (h + 1) * DH)
                    s = dot(q[qs, hs], kv[r, :, hs], 1, 1) * scale + bias[rs, :]
                    peak = jnp.max(s, axis=1, keepdims=True)
                    e = jnp.exp(s - peak)
                    p = (e * (1.0 / jnp.sum(e, axis=1, keepdims=True))).astype(bf16)
                    keep[r][rows_at((h // ppl) * T + i * half, half), (h % ppl) * SEQ : (h % ppl + 1) * SEQ] = p
                    att[qs, hs] = dot(p, kv[r, :, LW + h * DH : LW + (h + 1) * DH], 1, 0).astype(bf16)
                return carry

            lax.fori_loop(0, 2, one, 0)

        def times(lhs, r, weight, out, transposed):
            width = 512
            n = out.shape[1] // width

            def one(j, carry):
                cs = lanes(j * width, width)
                w = weight(j, width)
                out[r * T : (r + 1) * T, cs] = dot(lhs, w, 1, 1 if transposed else 0).astype(bf16)
                return carry

            lax.fori_loop(0, n, one, 0)

        def project_out(r):
            def one(j, carry):
                cs = lanes(j * 512, 512)
                part[r * T : (r + 1) * T, cs] = dot(att[r * T : (r + 1) * T, :], wout[:, cs], 1, 0).astype(bf16)
                return carry

            lax.fori_loop(0, D // 512, one, 0)

        def ffn(r, low, high):
            rs = slice(r * T, (r + 1) * T)

            def one(j, carry):
                cs = lanes(j * 256, 256)
                pre = dot(g2b[rs, :], arena[0:D, cs], 1, 0)
                e = 0.5 * (1.0 + lax.erf(pre * 0.7071067811865476))
                act[rs, cs] = (pre * e).astype(bf16)
                slope = e + pre * (jnp.exp(-0.5 * pre * pre) * 0.3989422804014327)
                back = dot(gyb[rs, :], arena[rows_at(D + j * 256, 256), :], 1, 1)
                gpre[rs, cs] = (back * slope).astype(bf16)
                return carry

            lax.fori_loop(low, high, one, 0)

        def ffn_back(r):
            rs = slice(r * T, (r + 1) * T)

            def one(j, carry):
                part[rs, lanes(j * 512, 512)] = dot(gpre[rs, :], arena[rows_at(j * 512, 512), :], 1, 1).astype(bf16)
                return carry

            lax.fori_loop(0, D // 512, one, 0)

        def ffn_out(r):
            rs = slice(r * T, (r + 1) * T)

            def one(j, carry):
                cs = lanes(j * 512, 512)
                part2[rs, cs] = dot(act[rs, :], arena[D : D + F, cs], 1, 0).astype(bf16)
                return carry

            lax.fori_loop(0, D // 512, one, 0)

        def second_norm(r):
            value = tok[:, r, :].astype(f32) + total[...]
            mid[r] = value
            unit, _ = norm_parts(value)
            g2b[rows_at(r * T + own, S), :] = (unit * g2[...] + b2[...]).astype(bf16)

        def second_norm_back(r):
            unit, inverse = norm_parts(mid[r])
            grad = total[...]
            nr[0, pl.ds(tp, 1), 2:3, :] += jnp.sum(grad * unit, axis=0, keepdims=True)[None]
            nr[0, pl.ds(tp, 1), 3:4, :] += jnp.sum(grad, axis=0, keepdims=True)[None]
            value = weighted_grad(r) + norm_back(unit, inverse, g2[...], grad)
            gin[r] = value
            ga[rows_at(r * T + own, S), :] = value.astype(bf16)

        def first_norm_back(r):
            unit, inverse = norm_parts(tok[:, r, :].astype(f32))
            grad = total[...]
            nr[0, pl.ds(tp, 1), 0:1, :] += jnp.sum(grad * unit, axis=0, keepdims=True)[None]
            nr[0, pl.ds(tp, 1), 1:2, :] += jnp.sum(grad, axis=0, keepdims=True)[None]
            gin[r] = gin[r] + norm_back(unit, inverse, g1[...], grad)

        def attend_back(r):
            rows = slice(r * T, (r + 1) * T)
            for h in range(H):
                hs = slice(h * DH, (h + 1) * DH)
                vs = slice(LW + h * DH, LW + (h + 1) * DH)
                go = gproj[rows, hs]
                pc = slice((h % ppl) * SEQ, (h % ppl + 1) * SEQ)
                for t in range(2):
                    ts = slice(t * half, (t + 1) * half)
                    gp = dot(gproj[r * T + t * half : r * T + (t + 1) * half, hs], kv[r, :, vs], 1, 1)
                    p = keep[r][(h // ppl) * T + t * half : (h // ppl) * T + (t + 1) * half, pc].astype(f32)
                    x = p * gp
                    delta = jnp.sum(x, axis=1, keepdims=True)
                    ds[ts, :] = ((x - p * delta) * scale).astype(bf16)
                k0 = r * KW + h * DH
                arena[DK0 : DK0 + SEQ, k0 : k0 + DH] = dot(ds[...], q[rows, hs], 0, 0).astype(bf16)
                v0 = r * KW + LW + h * DH
                arena[DK0 : DK0 + SEQ, v0 : v0 + DH] = dot(
                    keep[r][(h // ppl) * T : (h // ppl + 1) * T, pc], go, 0, 0
                ).astype(bf16)
                gproj[rows, hs] = dot(ds[...], kv[r, :, hs], 1, 0).astype(bf16)

        def grad_attended(r):
            rows = slice(r * T, (r + 1) * T)
            gproj[rows, 0:LW] = dot(ga[rows, :], wout[...], 1, 1).astype(bf16)

        def qkv_back(r):
            rs = slice(r * T, (r + 1) * T)

            def one(j, carry):
                part[rs, lanes(j * 512, 512)] = dot(gproj[rs, :], wqkv[rows_at(j * 512, 512), :], 1, 1).astype(bf16)
                return carry

            lax.fori_loop(0, D // 512, one, 0)

        load_out = pltpu.make_async_copy(wout_hbm, wout, loc.at[0])
        load_up = pltpu.make_async_copy(wup_hbm, arena.at[pl.ds(0, D), :], loc.at[1])
        load_down = pltpu.make_async_copy(wdn_hbm, arena.at[pl.ds(D, F), :], loc.at[2])
        save_p = [pltpu.make_async_copy(keep[r], ph.at[r], loc.at[3 + r]) for r in range(R)]
        load_p = [pltpu.make_async_copy(ph.at[r], keep[r], loc.at[3 + r]) for r in range(R)]
        save_g1 = pltpu.make_async_copy(ga, g1h, loc.at[5])
        load_g1 = pltpu.make_async_copy(g1h, arena.at[pl.ds(7 * RT, RT), :], loc.at[5])

        XA, XP, XG, XH, XJ = 0, RT, 2 * RT, 3 * RT, 4 * RT
        there = (dp, mate, tp)
        oth = 1 - par

        def halves(buf, buf_row, to_row, to_lane, n):
            return [
                remote(
                    buf.at[pl.ds(buf_row, RT), lanes(b * 2 * PD + oth * PD, PD)],
                    arena.at[pl.ds(to_row, RT), pl.ds(to_lane + b * PD, PD)],
                    x_s.at[n + b],
                    x_r.at[n + b],
                    there,
                )
                for b in range(4)
            ]

        def whole(buf, to_row, to_lane, n):
            w = buf.shape[1]
            return [remote(buf, arena.at[pl.ds(to_row, RT), pl.ds(to_lane, w)], x_s.at[n], x_r.at[n], there)]

        trade_down = whole(act, XA, 0, 0) + halves(gyb, 0, XG, 0, 2)
        trade_up = whole(gpre, XP, 0, 1) + halves(g2b, 0, XG, D // 2, 6)
        trade_g1 = halves(arena, 7 * RT, XH, 0, 10)
        trade_out = whole(att, XJ, 3 * LW, 18) + halves(ga, 0, XH, D // 2, 14)
        trade_qkv = whole(gproj, XJ, 0, 19)

        names = ["down", "up", "out", "qkv"]
        operands = {
            "down": (gyb, 0, act, (XG, 0), (XA, 0)),
            "up": (g2b, 0, gpre, (XG, D // 2), (XP, 0)),
            "out": (ga, 0, att, (XH, D // 2), (XJ, 3 * LW)),
            "qkv": (arena, 7 * RT, gproj, (XH, 0), (XJ, 0)),
        }

        def w_copy(name, which):
            t = names.index(name)
            n, off, a = kinds[name]
            ca, cb = pl.ds(off, a), pl.ds(off + a, n - a)
            x_to, y_to = (odp, sp, tp), (dp, far, tp)
            rt = arena.at[pl.ds(0, PD), :]
            src, dst, to = {
                "S2": (sw.at[0, :, ca], tx.at[:, ca], x_to),
                "S4": (sw.at[0, :, cb], ty.at[:, cb], y_to),
                "S1": (sw.at[1, :, ca], rx.at[:, ca], x_to),
                "S3": (sw.at[2, :, cb], ry.at[:, cb], y_to),
                "R1": (arena.at[pl.ds(0, PD), pl.ds(0, a)], ry.at[:, ca], y_to),
                "R2": (arena.at[pl.ds(0, PD), pl.ds(D - (n - a), n - a)], rx.at[:, cb], x_to),
            }[which]
            k = ("S1", "S2", "S3", "S4", "R1", "R2").index(which)
            return remote(src, dst, w_s.at[t, k], w_r.at[t, k], to)

        first_sends = [("S2", "S4"), ("S1",), ("S3",), ()]

        def stage_copy(name, i):
            n, off, _ = kinds[name]
            dst = ro.at[:, pl.ds(off, n)] if i == 3 else sw.at[i, :, pl.ds(off, n)]
            return pltpu.make_async_copy(stage.at[i % 2, :, pl.ds(0, n)], dst, stg_sem.at[i % 2])

        def weight_grad(name, services=()):
            own_d, own_row, own_r, (xd_row, xd_lane), (xr_row, xr_lane) = operands[name]
            n, off, _ = kinds[name]
            width = min(n, 1024) if n % 1024 == 0 else 512
            services = list(services)
            for i, (dx, dy) in enumerate(((1, 1), (1, 0), (0, 1), (0, 0))):
                to_dp = odp if dx else dp
                to_y = 1 - yy if dy else yy
                b4 = to_dp * 2 + to_y
                if i >= 2:
                    stage_copy(name, i - 2).wait()
                    for which in first_sends[i - 2]:
                        w_copy(name, which).start()

                def one(j, carry, b4=b4, i=i):
                    cs = lanes(j * width, width)
                    xs = lanes(xr_lane + j * width, width)
                    value = dot(
                        own_d[own_row : own_row + RT, lanes(b4 * 2 * PD + par * PD, PD)], own_r[:, cs], 0, 0
                    )
                    value += dot(
                        arena[xd_row : xd_row + RT, lanes(xd_lane + b4 * PD, PD)],
                        arena[xr_row : xr_row + RT, xs],
                        0,
                        0,
                    )
                    stage[i % 2, :, cs] = value.astype(bf16)
                    return carry

                lax.fori_loop(0, n // width, one, 0)
                stage_copy(name, i).start()
                if services:
                    services.pop(0)()
            for i in (2, 3):
                stage_copy(name, i).wait()
                for which in first_sends[i]:
                    w_copy(name, which).start()
            for s in services:
                s()

        def relay_sums(name, before):
            n, off, a = kinds[name]
            ca, cb = pl.ds(off, a), pl.ds(off + a, n - a)
            if before is not None:
                w_copy(before, "R1").wait_send()
                w_copy(before, "R2").wait_send()
            la, lb = pl.ds(0, a), pl.ds(D - (n - a), n - a)
            r0, r1 = pl.ds(0, PD), pl.ds(PD, PD)
            own_a = pltpu.make_async_copy(sw.at[2, :, ca], arena.at[r0, la], rt_sem.at[0])
            own_b = pltpu.make_async_copy(sw.at[1, :, cb], arena.at[r0, lb], rt_sem.at[1])
            got_a = pltpu.make_async_copy(tx.at[:, ca], arena.at[r1, la], rt_sem.at[2])
            got_b = pltpu.make_async_copy(ty.at[:, cb], arena.at[r1, lb], rt_sem.at[3])
            own_a.start()
            own_b.start()
            for own_c, got_c, need, send, ls in ((own_a, got_a, "S2", "R1", la), (own_b, got_b, "S4", "R2", lb)):
                w_copy(name, need).wait_recv()
                got_c.start()
                own_c.wait()
                got_c.wait()
                arena[r0, ls] = (arena[r0, ls].astype(f32) + arena[r1, ls].astype(f32)).astype(bf16)
                w_copy(name, send).start()

        def finish_sums(name, last):
            for which in ("S1", "S3", "R1", "R2"):
                w_copy(name, which).wait_recv()
            for which in ("S1", "S2", "S3", "S4"):
                w_copy(name, which).wait_send()
            if last:
                w_copy(name, "R1").wait_send()
                w_copy(name, "R2").wait_send()

        def norm_sums():
            for stage_i, (axis_n, index) in enumerate(((4, tp), (4, sp), (z.n_dp, dp))):
                copies = []
                for d in range(1, axis_n):
                    to = lax.rem(index + d, axis_n)
                    device = ((dp, sp, to), (dp, to, tp), (to, sp, tp))[stage_i]
                    slot = nr.at[stage_i, pl.ds(index, 1)]
                    copies.append((remote(slot, slot, n_s.at[stage_i, d - 1], n_r.at[stage_i, d - 1], device), d))
                for c, _ in copies:
                    c.start()
                for c, d in copies:
                    c.wait_send()
                    c.wait_recv()
                value = nr[stage_i, 0]
                for k in range(1, axis_n):
                    value = value + nr[stage_i, k]
                if stage_i < 2:
                    nxt = (tp, sp, dp)[stage_i + 1]
                    nr[stage_i + 1, pl.ds(nxt, 1)] = value[None]
                else:
                    norms[...] = value

        load_out.start()
        raw_copy(0).start()
        barrier = pltpu.get_barrier_semaphore()
        greet = [(dp, sp, lax.rem(tp + d, 4)) for d in (1, 2, 3)]
        greet += [(dp, lax.rem(sp + d, 4), tp) for d in (1, 2, 3)]
        if z.pairs:
            greet += [(odp, sp, tp)]
        for device in greet:
            pl.semaphore_signal(barrier, inc=1, device_id=device, device_id_type=MESH)
        first_norm(0)
        pl.semaphore_wait(barrier, len(greet))

        ag1 = [Gather(ga, 0, r) for r in range(R)]
        ag2 = [Gather(g2b, 1, r) for r in range(R)]
        ag3 = [Gather(gyb, 2, r) for r in range(R)]
        ag4 = [Gather(ga, 3, r) for r in range(R)]
        rs1 = [Scatter(part, slots, 0, r) for r in range(R)]
        rs3 = [Scatter(part, slots, 1, r) for r in range(R)]
        rs4 = [Scatter(part, slots, 2, r) for r in range(R)]
        rs2 = [Scatter(part2, slots2, 3, r) for r in range(R)]
        keys = [Keys(r) for r in range(R)]
        kgrads = [KeyGrads(r) for r in range(R)]

        ag1[0].start()
        first_norm(1)
        for r in range(R):
            gyb[rows_at(r * T + own, S), :] = weighted_grad(r).astype(bf16)
        load_up.start()
        load_down.start()
        nr[0, pl.ds(tp, 1)] = jnp.zeros((1,) + nr.shape[2:], f32)
        for b in range(1, 4):

            @pl.when(b > sp)
            def _(b=b):
                kv[:, b * T : (b + 1) * T, :] = jnp.zeros((R, T, KW), bf16)

        relay_weights(0, raw_steps // 4)
        ag1[0].step(1)
        relay_weights(raw_steps // 4, raw_steps // 2)
        ag1[0].step(2)
        ag1[1].start()
        relay_weights(raw_steps // 2, raw_steps)
        mask(0)
        ag1[0].step(3)
        project(0, 1)
        project(0, 2)
        keys[0].start()
        project(0, 0)
        ag1[1].step(1)
        ag1[1].step(2)
        ag3[0].start()
        keys[0].step()
        ag1[1].step(3)
        project(1, 1)
        project(1, 2)
        keys[1].start()
        save_g1.start()
        load_out.wait()
        ag3[0].step(1)
        keys[0].finish()
        attend(0)
        save_p[0].start()
        project_out(0)
        rs1[0].start()
        project(1, 0)
        mask(1)
        ag3[0].step(2)
        rs1[0].step(0)
        ag3[0].step(3)
        rs1[0].step(1)
        keys[1].step()
        keys[1].finish()
        attend(1)
        save_p[1].start()
        project_out(1)
        rs1[0].step(2)
        rs1[0].finish()
        second_norm(0)
        ag2[0].start()
        rs1[1].start()
        rs1[1].step(0)
        ag2[0].step(1)
        rs1[1].step(1)
        ag2[0].step(2)
        ag3[1].start()
        rs1[1].step(2)
        rs1[1].finish()
        second_norm(1)
        ag2[1].start()
        load_up.wait()
        load_down.wait()
        save_p[0].wait()
        save_p[1].wait()
        for g in ag1 + [ag3[0]]:
            g.drain()
        save_g1.wait()
        for g in keys:
            g.drain()
        rs1[0].drain()
        ag3[1].step(1)
        ag2[0].step(3)
        ffn(0, 0, F // 512)
        ag2[1].step(1)
        ag3[1].step(2)
        ffn(0, F // 512, F // 256)
        ffn_back(0)
        rs3[0].start()
        ag2[1].step(2)
        ag3[1].step(3)
        ffn_out(0)
        rs3[0].step(0)
        ag2[1].step(3)
        ffn(1, 0, F // 512)
        rs3[0].step(1)
        ffn(1, F // 512, F // 256)
        rs1[1].drain()
        ffn_back(1)
        rs3[1].start()
        rs3[0].step(2)
        rs3[0].finish()
        second_norm_back(0)
        ag4[0].start()
        ffn_out(1)
        ag2[0].drain()
        ag2[1].drain()
        ag3[1].drain()
        if z.pairs:
            pl.semaphore_signal(free_x, inc=1, device_id=there, device_id_type=MESH)
        load_g1.start()
        if z.pairs:
            pl.semaphore_wait(free_x, 1)
            for c in trade_down + trade_up:
                c.start()
        rs3[1].step(0)
        ag4[0].step(1)
        load_g1.wait()
        if z.pairs:
            for c in trade_g1:
                c.start()
            for c in trade_down:
                c.wait_recv()
            weight_grad("down", [lambda: rs3[1].step(1), lambda: ag4[0].step(2)])
            for c in trade_up:
                c.wait_recv()
        else:
            rs3[1].step(1)
            ag4[0].step(2)
        rs3[1].step(2)
        rs3[1].finish()
        second_norm_back(1)
        ag4[1].start()
        rs2[0].start()
        if z.pairs:
            weight_grad("up", [])
            for c in trade_down + trade_up:
                c.wait_send()
        else:
            dumps = [
                pltpu.make_async_copy(act, extra_act, stg_sem.at[0]),
                pltpu.make_async_copy(gpre, extra_gpre, stg_sem.at[1]),
                pltpu.make_async_copy(g2b, extra_g2, rt_sem.at[0]),
                pltpu.make_async_copy(gyb, extra_gy, rt_sem.at[1]),
            ]
            for c in dumps:
                c.start()
            for c in dumps:
                c.wait()
        pl.semaphore_signal(free_c, inc=1, device_id=there, device_id_type=MESH)
        pl.semaphore_signal(free_y, inc=1, device_id=(dp, far, tp), device_id_type=MESH)
        for r in range(R):
            load_p[r].start()
        ag4[0].step(3)
        grad_attended(0)
        for r in range(R):
            load_p[r].wait()
        attend_back(0)
        pl.semaphore_wait(free_c, 1)
        kgrads[0].start()
        ag4[1].step(1)
        rs2[0].step(0)
        pl.semaphore_wait(free_y, 1)
        kgrads[0].step()
        ag4[1].step(2)
        rs2[0].step(1)
        if z.pairs:
            relay_sums("down", None)
        rs2[0].step(2)
        ag4[1].step(3)
        if z.pairs:
            for c in trade_out:
                c.start()
        grad_attended(1)
        attend_back(1)
        kgrads[1].start()
        rs3[0].drain()
        rs3[1].drain()
        kgrads[1].step()
        kgrads[0].finish()
        qkv_back(0)
        rs4[0].start()
        rs2[0].finish()
        y_out[0] = (mid[0] + total[...]).astype(bf16)
        rs2[1].start()
        if z.pairs:
            for c in trade_out + trade_g1:
                c.wait_recv()
            weight_grad("out", [])
            relay_sums("up", "down")
        rs4[0].step(0)
        rs2[1].step(0)
        kgrads[1].finish()
        if z.pairs:
            for c in trade_qkv:
                c.start()
        qkv_back(1)
        rs4[1].start()
        rs4[0].step(1)
        if z.pairs:
            for c in trade_qkv:
                c.wait_recv()
            weight_grad("qkv", [lambda: rs4[0].step(2)])
        else:
            rs4[0].step(2)
        rs4[1].step(0)
        rs4[0].finish()
        first_norm_back(0)
        rs2[1].step(1)
        rs4[1].step(1)
        if z.pairs:
            relay_sums("out", "up")
        rs2[1].step(2)
        rs4[1].step(2)
        rs4[1].finish()
        first_norm_back(1)
        rs2[1].finish()
        y_out[1] = (mid[1] + total[...]).astype(bf16)
        if z.pairs:
            norm_sums()
            relay_sums("qkv", "out")
            for name in names:
                finish_sums(name, name == "qkv")
            for c in trade_g1 + trade_out + trade_qkv:
                c.wait_send()
        else:
            norms[...] = nr[0, pl.ds(tp, 1)][0]
            dumps = [
                pltpu.make_async_copy(ga, extra_gm, stg_sem.at[0]),
                pltpu.make_async_copy(gproj, extra_gproj, stg_sem.at[1]),
                pltpu.make_async_copy(att, extra_att, rt_sem.at[0]),
            ]
            for c in dumps:
                c.start()
            for c in dumps:
                c.wait()
        for g in rs2 + rs4 + ag4 + kgrads:
            g.drain()

    return kernel, w_lanes


def layer(z, tokens, out_grad, lengths, self_flags, episode_weight, g1, b1, g2, b2, w_qkv, w_out, w_up, w_down):
    S, R, D, LW, F, T, SEQ, H = z.S, z.R, z.D, z.LW, z.F, z.T, z.SEQ, z.H
    RT, PD = R * T, D // 8
    kernel, w_lanes = make_kernel(z)
    sds = jax.ShapeDtypeStruct
    any_, vmem, smem = (pl.BlockSpec(memory_space=m) for m in (pl.ANY, pltpu.VMEM, pltpu.SMEM))
    extra = (lambda *s: sds(s, bf16)) if not z.pairs else (lambda *s: sds((16, 128), bf16))
    pairs = (lambda *s: sds(s, bf16)) if z.pairs else (lambda *s: sds((16, 128), bf16))
    out_shape = [
        sds((R, S, D), bf16),
        sds((R, S, D), f32),
        sds((8, D), f32),
        pairs(PD, w_lanes),
        pairs(PD, w_lanes),
        pairs(PD, w_lanes),
        pairs(3, PD, w_lanes),
        pairs(PD, w_lanes),
        pairs(PD, w_lanes),
        sds((R, RT, D), bf16),
        sds((RT, D), bf16),
        extra(RT, D),
        extra(RT, D),
        extra(RT, D),
        extra(RT, F),
        extra(RT, F),
        extra(RT, 3 * LW),
        extra(RT, LW),
    ]
    dma = pltpu.SemaphoreType.DMA
    reg = pltpu.SemaphoreType.REGULAR
    v = lambda *s: pltpu.VMEM(s, bf16)
    vf = lambda *s: pltpu.VMEM(s, f32)
    scratch = [
        v(D + F, D), v(D, 3 * LW), v(LW, D), v(RT, D), v(RT, D), v(RT, D),
        v(RT, LW), v(R, SEQ, 2 * LW), v(RT, F), v(RT, F), v(RT, 3 * LW), v(RT, LW),
        v(RT, D), v(RT, D), v(R, 6, S, D), v(R, 6, S, D),
        vf(R, S, D), vf(T, SEQ), v(T, SEQ), v(2, 128, 3, LW), v(2, PD, max(F, D)), vf(3, 4, 8, D), vf(S, D),
        dma((4, R, 6)), dma((4, R, 4)), dma((4, R, 6)), dma((4, R, 6)),
        dma((R, 3)), dma((R, 4)), dma((R, 3)), dma((R, 3)),
        dma((20,)), dma((20,)), dma((4, 6)), dma((4, 6)), dma((3, 3)), dma((3, 3)),
        dma((6,)), dma((2,)), dma((2,)), dma((4,)), reg, reg, reg,
    ]
    return pl.pallas_call(
        kernel,
        out_shape=out_shape,
        in_specs=[vmem] * 2 + [smem] * 3 + [vmem] * 4 + [any_] * 4,
        out_specs=[vmem] * 3 + [any_] * 15,
        scratch_shapes=scratch,
        compiler_params=pltpu.CompilerParams(
            collective_id=0, has_side_effects=True, vmem_limit_bytes=64 * 2**20 - 2**16
        ),
        cost_estimate=pl.CostEstimate(flops=42 * 10**9, bytes_accessed=10**8, transcendentals=10**7),
    )(tokens, out_grad, lengths, self_flags, episode_weight, g1, b1, g2, b2, w_qkv, w_out, w_up, w_down)


def solution(mesh):
    shape = dict(mesh.shape)

    def on_device(
        tokens, lengths, self_flags, episode_weight, ln1_gain, ln1_bias, w_qkv, w_out, ln2_gain, ln2_bias, w_up,
        w_down, out_grad,
    ):
        z = Sizes(shape, tokens.shape, w_qkv.shape, w_up.shape, lengths.shape)
        row = lambda a: a.reshape(1, -1)
        results = layer(
            z, tokens, out_grad, lengths, self_flags, episode_weight, row(ln1_gain), row(ln1_bias), row(ln2_gain),
            row(ln2_bias), w_qkv, w_out, w_up, w_down,
        )
        y, gin, norms, ro, rx, ry = results[:6]
        output = jnp.transpose(y, (1, 0, 2))
        grad_input = jnp.transpose(gin, (1, 0, 2))
        kinds, _ = wgrad_kinds(z)
        if z.pairs:

            def summed(name):
                n, off, _ = kinds[name]
                sl = slice(off, off + n)
                return ro[:, sl].astype(f32) + rx[:, sl].astype(f32) + ry[:, sl].astype(f32)

            grad_down = summed("down").T
            grad_up = summed("up")
            grad_out = summed("out").T
            grad_qkv = summed("qkv").reshape(-1, 3, z.LW)
            both = norms
        else:
            g1_all, g2_all, gy_all, gm_all, act, gpre, gproj, att = results[10:]

            def over_tokens(a, b, dim):
                value = jnp.einsum("ta,tb->ab", a, b, preferred_element_type=f32).astype(bf16)
                return lax.psum_scatter(value, ("dp", "sp"), scatter_dimension=dim, tiled=True).astype(f32)

            grad_down = over_tokens(act, gy_all, 1)
            grad_up = over_tokens(g2_all, gpre, 0)
            grad_out = over_tokens(att, gm_all, 1)
            grad_qkv = over_tokens(g1_all, gproj, 0).reshape(-1, 3, z.LW)
            both = lax.psum(norms, ("dp", "sp", "tp"))
        return output, grad_input, grad_qkv, grad_out, grad_up, grad_down, both[0:2], both[2:4]

    return jax.shard_map(
        on_device,
        mesh=mesh,
        in_specs=(
            P(("sp", "tp"), "dp", None), P("dp", None), P("dp", None), P("dp", None), P(), P(), P(None, None, "tp"),
            P("tp", None), P(), P(), P(None, "tp"), P("tp", None), P(("sp", "tp"), "dp", None),
        ),
        out_specs=(
            P(("sp", "tp"), "dp", None), P(("sp", "tp"), "dp", None), P(("dp", "sp"), None, "tp"),
            P("tp", ("dp", "sp")), P(("dp", "sp"), "tp"), P("tp", ("dp", "sp")), P(), P(),
        ),
        check_vma=False,
    )
```

```python
import jax
import jax.numpy as jnp
from jax import lax
from jax.experimental import pallas as pl
from jax.experimental.pallas import tpu as pltpu
from jax.sharding import PartitionSpec as P

DH = 128
EPSILON = 1e-05
NEG = -1e30
f32 = jnp.float32
bf16 = jnp.bfloat16
MESH = pl.DeviceIdType.MESH


def dot(a, b, ca, cb):
    return lax.dot_general(a, b, (((ca,), (cb,)), ((), ())), preferred_element_type=f32)


def lanes(start, size):
    if isinstance(start, int):
        return pl.ds(start, size)
    return pl.ds(pl.multiple_of(start, 128), size)


def rows_at(start, size):
    if isinstance(start, int):
        return pl.ds(start, size)
    return pl.ds(pl.multiple_of(start, 64), size)


def norm_parts(values):
    average = jnp.mean(values, axis=-1, keepdims=True)
    centred = values - average
    variance = jnp.mean(centred * centred, axis=-1, keepdims=True)
    inverse = lax.rsqrt(variance + EPSILON)
    return centred * inverse, inverse


def norm_back(unit, inverse, gain, grad):
    scaled = grad * gain
    first = jnp.mean(scaled, axis=-1, keepdims=True)
    second = jnp.mean(scaled * unit, axis=-1, keepdims=True)
    return inverse * (scaled - first - unit * second)


class Sizes:
    def __init__(self, mesh_shape, tokens, w_qkv, w_up, lengths):
        self.n_dp = mesh_shape["dp"]
        self.n_sp = mesh_shape["sp"]
        self.n_tp = mesh_shape["tp"]
        self.S = tokens[0]
        self.R = tokens[1]
        self.D = tokens[2]
        self.LW = w_qkv[2]
        self.F = w_up[1]
        self.E = lengths[1]
        self.T = self.S * self.n_tp
        self.SEQ = self.T * self.n_sp
        self.H = self.LW // DH
        self.pairs = self.n_dp == 2 and self.n_sp == 4


def wgrad_kinds(z):
    def part(n):
        return max(128, (n * 5 // 8) // 128 * 128)

    out, offset = {}, 0
    for name, n in (("down", z.F), ("up", z.F), ("out", z.LW), ("qkv", 3 * z.LW)):
        out[name] = (n, offset, part(n))
        offset += n
    return out, offset


def make_kernel(z):
    S, R, D, LW, F, T, SEQ, H = z.S, z.R, z.D, z.LW, z.F, z.T, z.SEQ, z.H
    RT = R * T
    kinds, w_lanes = wgrad_kinds(z)
    scale = DH ** (-0.5)
    PD = D // 8

    def kernel(
        tok, og, lens, flags, eweight, g1, b1, g2, b2, wqkv_hbm, wout_hbm, wup_hbm, wdn_hbm,
        y_out, gin, norms, ro, rx, ry, sw, tx, ty, ph, g1h, extra_g2, extra_gy, extra_gm, extra_act, extra_gpre,
        extra_gproj, extra_att,
        arena, wqkv, wout, ga, g2b, gyb, q, kv, act, gpre, gproj, att, part, part2, slots, slots2,
        mid, bias, ds, stage, nr, total,
        ag_s, ag_r, rs_s, rs_r, kv_s, kv_r, dk_s, dk_r, x_s, x_r, w_s, w_r, n_s, n_r, loc, raw_sem, stg_sem,
        rt_sem, free_x, free_c, free_y,
    ):
        dp = lax.axis_index("dp")
        sp = lax.axis_index("sp")
        tp = lax.axis_index("tp")
        par = lax.rem(sp, 2)
        yy = lax.div(sp, 2)
        mate = sp + 1 - 2 * par
        far = lax.rem(sp + 2, 4)
        odp = 1 - dp
        kv_row = sp * T
        own = tp * S

        def remote(src, dst, ssem, rsem, device):
            return pltpu.make_async_remote_copy(
                src_ref=src, dst_ref=dst, send_sem=ssem, recv_sem=rsem, device_id=device, device_id_type=MESH
            )

        class Gather:
            def __init__(self, buf, i, r):
                self.buf, self.i, self.r = buf, i, r

            def copy(self, shard, way, hop):
                sl = self.buf.at[rows_at(self.r * T + shard * S, S), :]
                to = tp + 1 if way == 0 else tp - 1
                return remote(
                    sl, sl, ag_s.at[self.i, self.r, way * 3 + hop], ag_r.at[self.i, self.r, shard], (dp, sp, to)
                )

            def start(self):
                @pl.when(tp < 3)
                def _():
                    self.copy(tp, 0, 0).start()

                @pl.when(tp > 0)
                def _():
                    self.copy(tp, 1, 0).start()

            def step(self, hop):
                @pl.when(tp >= hop)
                def _():
                    self.copy(tp - hop, 0, 0).wait_recv()

                if hop < 3:

                    @pl.when((tp >= hop) & (tp < 3))
                    def _():
                        self.copy(tp - hop, 0, hop).start()

                @pl.when(tp <= 3 - hop)
                def _():
                    self.copy(tp + hop, 1, 0).wait_recv()

                if hop < 3:

                    @pl.when((tp <= 3 - hop) & (tp > 0))
                    def _():
                        self.copy(tp + hop, 1, hop).start()

            def drain(self):
                for hop in range(3):

                    @pl.when((tp >= hop) & (tp < 3))
                    def _(hop=hop):
                        self.copy(tp - hop, 0, hop).wait_send()

                    @pl.when((tp <= 3 - hop) & (tp > 0))
                    def _(hop=hop):
                        self.copy(tp + hop, 1, hop).wait_send()

        class Scatter:
            def __init__(self, buf, box, i, r):
                self.buf, self.box, self.i, self.r = buf, box, i, r

            def copy(self, way, k):
                o = 3 - k if way == 0 else k
                to = tp + 1 if way == 0 else tp - 1
                n = way * 3 + k
                return remote(
                    self.buf.at[pl.ds(self.r * T + o * S, S), :],
                    self.box.at[self.r, n],
                    rs_s.at[self.i, self.r, n],
                    rs_r.at[self.i, self.r, n],
                    (dp, sp, to),
                )

            def start(self):
                for k in range(3):

                    @pl.when(tp == 0)
                    def _(k=k):
                        self.copy(0, k).start()

                    @pl.when(tp == 3)
                    def _(k=k):
                        self.copy(1, k).start()

            def relay(self, way, k):
                o = 3 - k if way == 0 else k
                sl = pl.ds(self.r * T + o * S, S)
                self.copy(way, k).wait_recv()
                self.buf[sl, :] = (
                    self.buf[sl, :].astype(f32) + self.box[self.r, way * 3 + k].astype(f32)
                ).astype(bf16)
                self.copy(way, k).start()

            def step(self, k):
                @pl.when(tp == 1)
                def _():
                    self.relay(0, k)

                @pl.when(tp == 2)
                def _():
                    self.relay(1, k)

                if k == 1:

                    @pl.when(tp == 1)
                    def _():
                        self.relay(1, 0)

                    @pl.when(tp == 2)
                    def _():
                        self.relay(0, 0)

            def finish(self):
                total[...] = self.buf[rows_at(self.r * T + own, S), :].astype(f32)
                for o in range(1, 4):

                    @pl.when(tp == o)
                    def _(o=o):
                        self.copy(0, 3 - o).wait_recv()
                        total[...] += self.box[self.r, 3 - o].astype(f32)

                for o in range(0, 3):

                    @pl.when(tp == o)
                    def _(o=o):
                        self.copy(1, o).wait_recv()
                        total[...] += self.box[self.r, 3 + o].astype(f32)

            def drain(self):
                for k in range(3):

                    @pl.when(tp < 3 - k)
                    def _(k=k):
                        self.copy(0, k).wait_send()

                    @pl.when(tp > k)
                    def _(k=k):
                        self.copy(1, k).wait_send()

        class Keys:
            def __init__(self, r):
                self.r = r

            def copy(self, block, to, n):
                sl = kv.at[self.r, rows_at(block * T, T), :]
                return remote(sl, sl, kv_s.at[self.r, n], kv_r.at[self.r, block], (dp, to, tp))

            def start(self):
                @pl.when(sp < 2)
                def _():
                    self.copy(sp, sp + 2, 0).start()

                @pl.when(par == 0)
                def _():
                    self.copy(sp, sp + 1, 1).start()

            def step(self):
                for me, block, to in ((2, 0, 3), (3, 1, 2)):

                    @pl.when(sp == me)
                    def _(block=block, to=to):
                        self.copy(block, to, 0).wait_recv()
                        self.copy(block, to, 2).start()

            def finish(self):
                for me, block in ((1, 0), (2, 1), (3, 0), (3, 2)):

                    @pl.when(sp == me)
                    def _(block=block):
                        self.copy(block, 0, 0).wait_recv()

            def drain(self):
                @pl.when(sp < 2)
                def _():
                    self.copy(sp, sp + 2, 0).wait_send()

                @pl.when(par == 0)
                def _():
                    self.copy(sp, sp + 1, 1).wait_send()

                for me, block, to in ((2, 0, 3), (3, 1, 2)):

                    @pl.when(sp == me)
                    def _(block=block, to=to):
                        self.copy(block, to, 2).wait_send()

        KW = 2 * LW
        DK0 = 5 * RT
        DR0 = RT

        class KeyGrads:
            def __init__(self, r):
                self.r = r

            def src(self, block):
                return arena.at[pl.ds(DK0 + block * T, T), pl.ds(self.r * KW, KW)]

            def dst(self, box):
                return arena.at[pl.ds(DR0 + box * T, T), pl.ds(self.r * KW, KW)]

            def copy(self, block, to, box, n):
                return remote(
                    self.src(block), self.dst(box), dk_s.at[self.r, n], dk_r.at[self.r, box], (dp, to, tp)
                )

            def start(self):
                for me, block, to, box, n in ((3, 0, 2, 0, 0), (3, 2, 2, 1, 1), (2, 1, 3, 0, 0), (1, 0, 0, 1, 0)):

                    @pl.when(sp == me)
                    def _(block=block, to=to, box=box, n=n):
                        self.copy(block, to, box, n).start()

            def step(self):
                for me, block, to in ((2, 0, 0), (3, 1, 1)):

                    @pl.when(sp == me)
                    def _(block=block, to=to):
                        self.copy(block, to, 0, 2).wait_recv()
                        mine = pl.ds(DK0 + block * T, T)
                        col = pl.ds(self.r * KW, KW)
                        arena[mine, col] = (
                            arena[mine, col].astype(f32) + arena[pl.ds(DR0, T), col].astype(f32)
                        ).astype(bf16)
                        self.copy(block, to, 2, 2).start()

            def finish(self):
                col = pl.ds(self.r * KW, KW)
                there = pl.ds(self.r * T, T)
                to = pl.ds(LW, KW)
                for me, boxes in ((0, (1, 2)), (1, (2,)), (2, (1,)), (3, ())):

                    @pl.when(sp == me)
                    def _(me=me, boxes=boxes):
                        value = arena[pl.ds(DK0 + me * T, T), col].astype(f32)
                        for box in boxes:
                            self.copy(0, 0, box, 0).wait_recv()
                            value += arena[pl.ds(DR0 + box * T, T), col].astype(f32)
                        gproj[there, to] = value.astype(bf16)

            def drain(self):
                for me, block, to, box, n in (
                    (3, 0, 2, 0, 0), (3, 2, 2, 1, 1), (2, 1, 3, 0, 0), (1, 0, 0, 1, 0), (2, 0, 0, 2, 2), (3, 1, 1, 2, 2),
                ):

                    @pl.when(sp == me)
                    def _(block=block, to=to, box=box, n=n):
                        self.copy(block, to, box, n).wait_send()

        ends = []
        for r in range(R):
            run, row = 0, []
            for e in range(z.E):
                run = run + lens[r, e]
                row.append(run)
            ends.append(row)

        def first_norm(r):
            unit, _ = norm_parts(tok[:, r, :].astype(f32))
            ga[rows_at(r * T + own, S), :] = (unit * g1[...] + b1[...]).astype(bf16)

        def weighted_grad(r):
            place = sp * T + own + lax.broadcasted_iota(jnp.int32, (S, 1), 0)
            factor = jnp.full((S, 1), eweight[r, 0] * (1.0 + flags[r, 0].astype(f32)), f32)
            for e in range(1, z.E):
                factor = jnp.where(
                    place >= ends[r][e - 1], eweight[r, e] * (1.0 + flags[r, e].astype(f32)), factor
                )
            return og[:, r, :].astype(f32) * factor

        def project(r, j):
            value = dot(ga[r * T : (r + 1) * T, :], wqkv[:, j * LW : (j + 1) * LW], 1, 0).astype(bf16)
            if j == 0:
                q[r * T : (r + 1) * T, :] = value
            else:
                kv[r, rows_at(kv_row, T), (j - 1) * LW : j * LW] = value

        def mask(r):
            here = kv_row + lax.broadcasted_iota(jnp.int32, (T, 1), 0)
            begin = jnp.zeros((T, 1), jnp.int32)
            for e in range(z.E):
                begin = jnp.where(here >= ends[r][e], jnp.maximum(begin, ends[r][e]), begin)
            there = lax.broadcasted_iota(jnp.int32, (T, SEQ), 1)
            bias[...] = jnp.where((there <= here) & (there >= begin), 0.0, NEG)

        half = T // 2
        ppl = D // SEQ
        keep = [act, gpre]

        def attend(r):
            def one(i, carry):
                rs = rows_at(i * half, half)
                qs = rows_at(r * T + i * half, half)
                for h in range(H):
                    hs = slice(h * DH, (h + 1) * DH)
                    s = dot(q[qs, hs], kv[r, :, hs], 1, 1) * scale + bias[rs, :]
                    peak = jnp.max(s, axis=1, keepdims=True)
                    e = jnp.exp(s - peak)
                    p = (e * (1.0 / jnp.sum(e, axis=1, keepdims=True))).astype(bf16)
                    keep[r][rows_at((h // ppl) * T + i * half, half), (h % ppl) * SEQ : (h % ppl + 1) * SEQ] = p
                    att[qs, hs] = dot(p, kv[r, :, LW + h * DH : LW + (h + 1) * DH], 1, 0).astype(bf16)
                return carry

            lax.fori_loop(0, 2, one, 0)

        def times(lhs, r, weight, out, transposed):
            width = 512
            n = out.shape[1] // width

            def one(j, carry):
                cs = lanes(j * width, width)
                w = weight(j, width)
                out[r * T : (r + 1) * T, cs] = dot(lhs, w, 1, 1 if transposed else 0).astype(bf16)
                return carry

            lax.fori_loop(0, n, one, 0)

        def project_out(r):
            def one(j, carry):
                cs = lanes(j * 512, 512)
                part[r * T : (r + 1) * T, cs] = dot(att[r * T : (r + 1) * T, :], wout[:, cs], 1, 0).astype(bf16)
                return carry

            lax.fori_loop(0, D // 512, one, 0)

        def ffn(r, low, high):
            rs = slice(r * T, (r + 1) * T)

            def one(j, carry):
                cs = lanes(j * 256, 256)
                pre = dot(g2b[rs, :], arena[0:D, cs], 1, 0)
                e = 0.5 * (1.0 + lax.erf(pre * 0.7071067811865476))
                act[rs, cs] = (pre * e).astype(bf16)
                slope = e + pre * (jnp.exp(-0.5 * pre * pre) * 0.3989422804014327)
                back = dot(gyb[rs, :], arena[rows_at(D + j * 256, 256), :], 1, 1)
                gpre[rs, cs] = (back * slope).astype(bf16)
                return carry

            lax.fori_loop(low, high, one, 0)

        def ffn_back(r):
            rs = slice(r * T, (r + 1) * T)

            def one(j, carry):
                part[rs, lanes(j * 512, 512)] = dot(gpre[rs, :], arena[rows_at(j * 512, 512), :], 1, 1).astype(bf16)
                return carry

            lax.fori_loop(0, D // 512, one, 0)

        def ffn_out(r):
            rs = slice(r * T, (r + 1) * T)

            def one(j, carry):
                cs = lanes(j * 512, 512)
                part2[rs, cs] = dot(act[rs, :], arena[D : D + F, cs], 1, 0).astype(bf16)
                return carry

            lax.fori_loop(0, D // 512, one, 0)

        def second_norm(r):
            value = tok[:, r, :].astype(f32) + total[...]
            mid[r] = value
            unit, _ = norm_parts(value)
            g2b[rows_at(r * T + own, S), :] = (unit * g2[...] + b2[...]).astype(bf16)

        def second_norm_back(r):
            unit, inverse = norm_parts(mid[r])
            grad = total[...]
            nr[0, pl.ds(tp, 1), 2:3, :] += jnp.sum(grad * unit, axis=0, keepdims=True)[None]
            nr[0, pl.ds(tp, 1), 3:4, :] += jnp.sum(grad, axis=0, keepdims=True)[None]
            value = weighted_grad(r) + norm_back(unit, inverse, g2[...], grad)
            gin[r] = value
            ga[rows_at(r * T + own, S), :] = value.astype(bf16)

        def first_norm_back(r):
            unit, inverse = norm_parts(tok[:, r, :].astype(f32))
            grad = total[...]
            nr[0, pl.ds(tp, 1), 0:1, :] += jnp.sum(grad * unit, axis=0, keepdims=True)[None]
            nr[0, pl.ds(tp, 1), 1:2, :] += jnp.sum(grad, axis=0, keepdims=True)[None]
            gin[r] = gin[r] + norm_back(unit, inverse, g1[...], grad)

        def attend_back(r):
            rows = slice(r * T, (r + 1) * T)
            for h in range(H):
                hs = slice(h * DH, (h + 1) * DH)
                vs = slice(LW + h * DH, LW + (h + 1) * DH)
                go = gproj[rows, hs]
                pc = slice((h % ppl) * SEQ, (h % ppl + 1) * SEQ)
                for t in range(2):
                    ts = slice(t * half, (t + 1) * half)
                    gp = dot(gproj[r * T + t * half : r * T + (t + 1) * half, hs], kv[r, :, vs], 1, 1)
                    p = keep[r][(h // ppl) * T + t * half : (h // ppl) * T + (t + 1) * half, pc].astype(f32)
                    x = p * gp
                    delta = jnp.sum(x, axis=1, keepdims=True)
                    ds[ts, :] = ((x - p * delta) * scale).astype(bf16)
                k0 = r * KW + h * DH
                arena[DK0 : DK0 + SEQ, k0 : k0 + DH] = dot(ds[...], q[rows, hs], 0, 0).astype(bf16)
                v0 = r * KW + LW + h * DH
                arena[DK0 : DK0 + SEQ, v0 : v0 + DH] = dot(
                    keep[r][(h // ppl) * T : (h // ppl + 1) * T, pc], go, 0, 0
                ).astype(bf16)
                gproj[rows, hs] = dot(ds[...], kv[r, :, hs], 1, 0).astype(bf16)

        def grad_attended(r):
            rows = slice(r * T, (r + 1) * T)
            gproj[rows, 0:LW] = dot(ga[rows, :], wout[...], 1, 1).astype(bf16)

        def qkv_back(r):
            rs = slice(r * T, (r + 1) * T)

            def one(j, carry):
                part[rs, lanes(j * 512, 512)] = dot(gproj[rs, :], wqkv[rows_at(j * 512, 512), :], 1, 1).astype(bf16)
                return carry

            lax.fori_loop(0, D // 512, one, 0)

        load_out = pltpu.make_async_copy(wout_hbm, wout, loc.at[0])
        load_qkv = [
            pltpu.make_async_copy(wqkv_hbm.at[j], wqkv.at[:, pl.ds(j * LW, LW)], raw_sem.at[j]) for j in range(3)
        ]
        load_up = pltpu.make_async_copy(wup_hbm, arena.at[pl.ds(0, D), :], loc.at[1])
        load_down = pltpu.make_async_copy(wdn_hbm, arena.at[pl.ds(D, F), :], loc.at[2])
        save_p = [pltpu.make_async_copy(keep[r], ph.at[r], loc.at[3 + r]) for r in range(R)]
        load_p = [pltpu.make_async_copy(ph.at[r], keep[r], loc.at[3 + r]) for r in range(R)]
        save_g1 = pltpu.make_async_copy(ga, g1h, loc.at[5])
        load_g1 = pltpu.make_async_copy(g1h, arena.at[pl.ds(7 * RT, RT), :], loc.at[5])

        XA, XP, XG, XH, XJ = 0, RT, 2 * RT, 3 * RT, 4 * RT
        there = (dp, mate, tp)
        oth = 1 - par

        def halves(buf, buf_row, to_row, to_lane, n):
            return [
                remote(
                    buf.at[pl.ds(buf_row, RT), lanes(b * 2 * PD + oth * PD, PD)],
                    arena.at[pl.ds(to_row, RT), pl.ds(to_lane + b * PD, PD)],
                    x_s.at[n + b],
                    x_r.at[n + b],
                    there,
                )
                for b in range(4)
            ]

        def whole(buf, to_row, to_lane, n):
            w = buf.shape[1]
            return [remote(buf, arena.at[pl.ds(to_row, RT), pl.ds(to_lane, w)], x_s.at[n], x_r.at[n], there)]

        trade_down = whole(act, XA, 0, 0) + halves(gyb, 0, XG, 0, 2)
        trade_up = whole(gpre, XP, 0, 1) + halves(g2b, 0, XG, D // 2, 6)
        trade_g1 = halves(arena, 7 * RT, XH, 0, 10)
        trade_out = whole(att, XJ, 3 * LW, 18) + halves(ga, 0, XH, D // 2, 14)
        trade_qkv = whole(gproj, XJ, 0, 19)

        names = ["down", "up", "out", "qkv"]
        operands = {
            "down": (gyb, 0, act, (XG, 0), (XA, 0)),
            "up": (g2b, 0, gpre, (XG, D // 2), (XP, 0)),
            "out": (ga, 0, att, (XH, D // 2), (XJ, 3 * LW)),
            "qkv": (arena, 7 * RT, gproj, (XH, 0), (XJ, 0)),
        }

        def w_copy(name, which):
            t = names.index(name)
            n, off, a = kinds[name]
            ca, cb = pl.ds(off, a), pl.ds(off + a, n - a)
            x_to, y_to = (odp, sp, tp), (dp, far, tp)
            rt = arena.at[pl.ds(0, PD), :]
            src, dst, to = {
                "S2": (sw.at[0, :, ca], tx.at[:, ca], x_to),
                "S4": (sw.at[0, :, cb], ty.at[:, cb], y_to),
                "S1": (sw.at[1, :, ca], rx.at[:, ca], x_to),
                "S3": (sw.at[2, :, cb], ry.at[:, cb], y_to),
                "R1": (arena.at[pl.ds(0, PD), pl.ds(0, a)], ry.at[:, ca], y_to),
                "R2": (arena.at[pl.ds(0, PD), pl.ds(D - (n - a), n - a)], rx.at[:, cb], x_to),
            }[which]
            k = ("S1", "S2", "S3", "S4", "R1", "R2").index(which)
            return remote(src, dst, w_s.at[t, k], w_r.at[t, k], to)

        first_sends = [("S2", "S4"), ("S1",), ("S3",), ()]

        def stage_copy(name, i):
            n, off, _ = kinds[name]
            dst = ro.at[:, pl.ds(off, n)] if i == 3 else sw.at[i, :, pl.ds(off, n)]
            return pltpu.make_async_copy(stage.at[i % 2, :, pl.ds(0, n)], dst, stg_sem.at[i % 2])

        def weight_grad(name, services=()):
            own_d, own_row, own_r, (xd_row, xd_lane), (xr_row, xr_lane) = operands[name]
            n, off, _ = kinds[name]
            width = min(n, 1024) if n % 1024 == 0 else 512
            services = list(services)
            for i, (dx, dy) in enumerate(((1, 1), (1, 0), (0, 1), (0, 0))):
                to_dp = odp if dx else dp
                to_y = 1 - yy if dy else yy
                b4 = to_dp * 2 + to_y
                if i >= 2:
                    stage_copy(name, i - 2).wait()
                    for which in first_sends[i - 2]:
                        w_copy(name, which).start()

                def one(j, carry, b4=b4, i=i):
                    cs = lanes(j * width, width)
                    xs = lanes(xr_lane + j * width, width)
                    value = dot(
                        own_d[own_row : own_row + RT, lanes(b4 * 2 * PD + par * PD, PD)], own_r[:, cs], 0, 0
                    )
                    value += dot(
                        arena[xd_row : xd_row + RT, lanes(xd_lane + b4 * PD, PD)],
                        arena[xr_row : xr_row + RT, xs],
                        0,
                        0,
                    )
                    stage[i % 2, :, cs] = value.astype(bf16)
                    return carry

                lax.fori_loop(0, n // width, one, 0)
                stage_copy(name, i).start()
                if services:
                    services.pop(0)()
            for i in (2, 3):
                stage_copy(name, i).wait()
                for which in first_sends[i]:
                    w_copy(name, which).start()
            for s in services:
                s()

        def relay_sums(name, before):
            n, off, a = kinds[name]
            ca, cb = pl.ds(off, a), pl.ds(off + a, n - a)
            if before is not None:
                w_copy(before, "R1").wait_send()
                w_copy(before, "R2").wait_send()
            la, lb = pl.ds(0, a), pl.ds(D - (n - a), n - a)
            r0, r1 = pl.ds(0, PD), pl.ds(PD, PD)
            own_a = pltpu.make_async_copy(sw.at[2, :, ca], arena.at[r0, la], rt_sem.at[0])
            own_b = pltpu.make_async_copy(sw.at[1, :, cb], arena.at[r0, lb], rt_sem.at[1])
            got_a = pltpu.make_async_copy(tx.at[:, ca], arena.at[r1, la], rt_sem.at[2])
            got_b = pltpu.make_async_copy(ty.at[:, cb], arena.at[r1, lb], rt_sem.at[3])
            own_a.start()
            own_b.start()
            for own_c, got_c, need, send, ls in ((own_a, got_a, "S2", "R1", la), (own_b, got_b, "S4", "R2", lb)):
                w_copy(name, need).wait_recv()
                got_c.start()
                own_c.wait()
                got_c.wait()
                arena[r0, ls] = (arena[r0, ls].astype(f32) + arena[r1, ls].astype(f32)).astype(bf16)
                w_copy(name, send).start()

        def finish_sums(name, last):
            for which in ("S1", "S3", "R1", "R2"):
                w_copy(name, which).wait_recv()
            for which in ("S1", "S2", "S3", "S4"):
                w_copy(name, which).wait_send()
            if last:
                w_copy(name, "R1").wait_send()
                w_copy(name, "R2").wait_send()

        def norm_sums():
            for stage_i, (axis_n, index) in enumerate(((4, tp), (4, sp), (z.n_dp, dp))):
                copies = []
                for d in range(1, axis_n):
                    to = lax.rem(index + d, axis_n)
                    device = ((dp, sp, to), (dp, to, tp), (to, sp, tp))[stage_i]
                    slot = nr.at[stage_i, pl.ds(index, 1)]
                    copies.append((remote(slot, slot, n_s.at[stage_i, d - 1], n_r.at[stage_i, d - 1], device), d))
                for c, _ in copies:
                    c.start()
                for c, d in copies:
                    c.wait_send()
                    c.wait_recv()
                value = nr[stage_i, 0]
                for k in range(1, axis_n):
                    value = value + nr[stage_i, k]
                if stage_i < 2:
                    nxt = (tp, sp, dp)[stage_i + 1]
                    nr[stage_i + 1, pl.ds(nxt, 1)] = value[None]
                else:
                    norms[...] = value

        load_out.start()
        for c in load_qkv:
            c.start()
        barrier = pltpu.get_barrier_semaphore()
        greet = [(dp, sp, lax.rem(tp + d, 4)) for d in (1, 2, 3)]
        greet += [(dp, lax.rem(sp + d, 4), tp) for d in (1, 2, 3)]
        if z.pairs:
            greet += [(odp, sp, tp)]
        for device in greet:
            pl.semaphore_signal(barrier, inc=1, device_id=device, device_id_type=MESH)
        first_norm(0)
        pl.semaphore_wait(barrier, len(greet))

        ag1 = [Gather(ga, 0, r) for r in range(R)]
        ag2 = [Gather(g2b, 1, r) for r in range(R)]
        ag3 = [Gather(gyb, 2, r) for r in range(R)]
        ag4 = [Gather(ga, 3, r) for r in range(R)]
        rs1 = [Scatter(part, slots, 0, r) for r in range(R)]
        rs3 = [Scatter(part, slots, 1, r) for r in range(R)]
        rs4 = [Scatter(part, slots, 2, r) for r in range(R)]
        rs2 = [Scatter(part2, slots2, 3, r) for r in range(R)]
        keys = [Keys(r) for r in range(R)]
        kgrads = [KeyGrads(r) for r in range(R)]

        def grad_rows(r):
            gyb[rows_at(r * T + own, S), :] = weighted_grad(r).astype(bf16)

        def clear():
            nr[0, pl.ds(tp, 1)] = jnp.zeros((1,) + nr.shape[2:], f32)
            for b in range(1, 4):

                @pl.when(b > sp)
                def _(b=b):
                    kv[:, b * T : (b + 1) * T, :] = jnp.zeros((R, T, KW), bf16)

        def keys_out(r):
            if r == 0:
                for c in load_qkv:
                    c.wait()
            project(r, 1)
            project(r, 2)
            keys[r].start()

        def queries(r):
            project(r, 0)

        def attention(r):
            attend(r)
            save_p[r].start()
            if r == 0:
                load_out.wait()
            project_out(r)
            rs1[r].start()

        def sum_one(r):
            rs1[r].finish()
            second_norm(r)
            ag2[r].start()

        def before_ffn():
            load_up.wait()
            load_down.wait()
            save_g1.wait()
            for c in save_p:
                c.wait()
            for g in ag1:
                g.drain()

        def ffn_a(r):
            ffn(r, 0, F // 512)

        def ffn_b(r):
            ffn(r, F // 512, F // 256)

        def ffn_c(r):
            rs1[r].drain()
            ffn_back(r)
            rs3[r].start()

        def sum_three(r):
            rs3[r].finish()
            second_norm_back(r)
            ag4[r].start()

        def sum_two(r):
            rs2[r].finish()
            y_out[r] = (mid[r] + total[...]).astype(bf16)

        def sum_four(r):
            rs4[r].finish()
            first_norm_back(r)

        def offer():
            if z.pairs:
                pl.semaphore_signal(free_x, inc=1, device_id=there, device_id_type=MESH)

        def trade_one():
            if z.pairs:
                pl.semaphore_wait(free_x, 1)
                for c in trade_down + trade_up:
                    c.start()

        def grads_down():
            if z.pairs:
                for c in trade_down:
                    c.wait_recv()
                weight_grad("down")

        def grads_up():
            if z.pairs:
                for c in trade_up:
                    c.wait_recv()
                weight_grad("up")

        def offer_two():
            if z.pairs:
                for c in trade_down + trade_up:
                    c.wait_send()
            else:
                dumps = [
                    pltpu.make_async_copy(act, extra_act, stg_sem.at[0]),
                    pltpu.make_async_copy(gpre, extra_gpre, stg_sem.at[1]),
                    pltpu.make_async_copy(g2b, extra_g2, rt_sem.at[0]),
                    pltpu.make_async_copy(gyb, extra_gy, rt_sem.at[1]),
                ]
                for c in dumps:
                    c.start()
                for c in dumps:
                    c.wait()
            pl.semaphore_signal(free_c, inc=1, device_id=there, device_id_type=MESH)
            pl.semaphore_signal(free_y, inc=1, device_id=(dp, far, tp), device_id_type=MESH)
            for c in load_p:
                c.start()

        def trade_two():
            load_g1.wait()
            if z.pairs:
                for c in trade_g1:
                    c.start()

        def attention_back(r):
            load_p[r].wait()
            attend_back(r)
            if r == 0:
                pl.semaphore_wait(free_c, 1)
            kgrads[r].start()

        def keys_back(r):
            if r == 0:
                pl.semaphore_wait(free_y, 1)
            kgrads[r].step()

        def keys_sum(r):
            kgrads[r].finish()

        def trade_three():
            if z.pairs:
                for c in trade_out:
                    c.start()

        def grads_out():
            if z.pairs:
                for c in trade_out:
                    c.wait_recv()
                weight_grad("out")

        def trade_four():
            if z.pairs:
                for c in trade_qkv:
                    c.start()

        def grads_qkv():
            if z.pairs:
                for c in trade_g1 + trade_qkv:
                    c.wait_recv()
                weight_grad("qkv")

        def pass_on(i):
            if z.pairs:
                relay_sums(names[i], names[i - 1] if i else None)

        def back_c(r):
            rs3[r].drain()
            qkv_back(r)
            rs4[r].start()

        def norms_end():
            if z.pairs:
                norm_sums()
            else:
                norms[...] = nr[0, pl.ds(tp, 1)][0]

        def the_end():
            if z.pairs:
                for name in names:
                    finish_sums(name, name == "qkv")
                for c in trade_g1 + trade_out + trade_qkv:
                    c.wait_send()
            else:
                dumps = [
                    pltpu.make_async_copy(ga, extra_gm, stg_sem.at[0]),
                    pltpu.make_async_copy(gproj, extra_gproj, stg_sem.at[1]),
                    pltpu.make_async_copy(att, extra_att, rt_sem.at[0]),
                ]
                for c in dumps:
                    c.start()
                for c in dumps:
                    c.wait()
            for g in keys + ag2 + ag3 + ag4 + rs2 + rs4 + kgrads:
                g.drain()

        ag1[0].start()
        clear()
        grad_rows(1)
        first_norm(1)
        ag1[0].step(1)
        ag1[1].start()
        load_down.start()
        ag1[0].step(2)
        grad_rows(0)
        ag1[0].step(3)
        ag1[1].step(1)
        keys_out(0)
        ag1[1].step(2)
        ag3[1].start()
        keys[0].step()
        ag3[0].start()
        mask(0)
        queries(0)
        ag1[1].step(3)
        save_g1.start()
        keys[0].finish()
        attention(0)
        keys_out(1)
        ag3[1].step(1)
        queries(1)
        ag3[0].step(1)
        keys[1].step()
        load_up.start()
        mask(1)
        ag3[1].step(2)
        keys[1].finish()
        rs1[0].step(0)
        attention(1)
        rs1[0].step(1)
        before_ffn()
        sum_one(0)
        rs1[1].step(0)
        ag3[0].step(2)
        rs1[1].step(1)
        ag2[0].step(1)
        sum_one(1)
        ag3[0].step(3)
        ag3[1].step(3)
        ag2[0].step(2)
        ag2[0].step(3)
        ffn_a(0)
        ffn_b(0)
        ffn_c(0)
        ag2[1].step(1)
        ag2[1].step(2)
        ag2[1].step(3)
        ffn_a(1)
        ffn_b(1)
        ffn_c(1)
        offer()
        trade_one()
        rs3[0].step(0)
        ffn_out(1)
        ffn_out(0)
        rs3[0].step(1)
        grads_down()
        load_g1.start()
        rs3[1].step(0)
        sum_three(0)
        grads_up()
        trade_two()
        offer_two()
        rs3[1].step(1)
        pass_on(0)
        ag4[0].step(1)
        sum_three(1)
        rs2[0].start()
        ag4[0].step(2)
        ag4[1].step(1)
        ag4[0].step(3)
        grad_attended(0)
        attention_back(0)
        ag4[1].step(2)
        rs2[1].start()
        rs2[0].step(0)
        ag4[1].step(3)
        trade_three()
        keys_back(0)
        rs2[0].step(1)
        grad_attended(1)
        attention_back(1)
        keys_back(1)
        rs2[1].step(0)
        grads_out()
        sum_two(0)
        rs2[1].step(1)
        keys_sum(0)
        back_c(0)
        pass_on(1)
        keys_sum(1)
        trade_four()
        sum_two(1)
        rs4[0].step(0)
        rs4[0].step(1)
        back_c(1)
        grads_qkv()
        rs4[1].step(0)
        sum_four(0)
        rs4[1].step(1)
        pass_on(2)
        pass_on(3)
        sum_four(1)
        norms_end()
        the_end()

    return kernel, w_lanes


def layer(z, tokens, out_grad, lengths, self_flags, episode_weight, g1, b1, g2, b2, w_qkv, w_out, w_up, w_down):
    S, R, D, LW, F, T, SEQ, H = z.S, z.R, z.D, z.LW, z.F, z.T, z.SEQ, z.H
    RT, PD = R * T, D // 8
    kernel, w_lanes = make_kernel(z)
    sds = jax.ShapeDtypeStruct
    any_, vmem, smem = (pl.BlockSpec(memory_space=m) for m in (pl.ANY, pltpu.VMEM, pltpu.SMEM))
    extra = (lambda *s: sds(s, bf16)) if not z.pairs else (lambda *s: sds((16, 128), bf16))
    pairs = (lambda *s: sds(s, bf16)) if z.pairs else (lambda *s: sds((16, 128), bf16))
    out_shape = [
        sds((R, S, D), bf16),
        sds((R, S, D), f32),
        sds((8, D), f32),
        pairs(PD, w_lanes),
        pairs(PD, w_lanes),
        pairs(PD, w_lanes),
        pairs(3, PD, w_lanes),
        pairs(PD, w_lanes),
        pairs(PD, w_lanes),
        sds((R, RT, D), bf16),
        sds((RT, D), bf16),
        extra(RT, D),
        extra(RT, D),
        extra(RT, D),
        extra(RT, F),
        extra(RT, F),
        extra(RT, 3 * LW),
        extra(RT, LW),
    ]
    dma = pltpu.SemaphoreType.DMA
    reg = pltpu.SemaphoreType.REGULAR
    v = lambda *s: pltpu.VMEM(s, bf16)
    vf = lambda *s: pltpu.VMEM(s, f32)
    scratch = [
        v(D + F, D), v(D, 3 * LW), v(LW, D), v(RT, D), v(RT, D), v(RT, D),
        v(RT, LW), v(R, SEQ, 2 * LW), v(RT, F), v(RT, F), v(RT, 3 * LW), v(RT, LW),
        v(RT, D), v(RT, D), v(R, 6, S, D), v(R, 6, S, D),
        vf(R, S, D), vf(T, SEQ), v(T, SEQ), v(2, PD, max(F, D)), vf(3, 4, 8, D), vf(S, D),
        dma((4, R, 6)), dma((4, R, 4)), dma((4, R, 6)), dma((4, R, 6)),
        dma((R, 3)), dma((R, 4)), dma((R, 3)), dma((R, 3)),
        dma((20,)), dma((20,)), dma((4, 6)), dma((4, 6)), dma((3, 3)), dma((3, 3)),
        dma((6,)), dma((3,)), dma((2,)), dma((4,)), reg, reg, reg,
    ]
    return pl.pallas_call(
        kernel,
        out_shape=out_shape,
        in_specs=[vmem] * 2 + [smem] * 3 + [vmem] * 4 + [any_] * 4,
        out_specs=[vmem] * 3 + [any_] * 15,
        scratch_shapes=scratch,
        compiler_params=pltpu.CompilerParams(
            collective_id=0, has_side_effects=True, vmem_limit_bytes=64 * 2**20 - 2**16
        ),
        cost_estimate=pl.CostEstimate(flops=42 * 10**9, bytes_accessed=10**8, transcendentals=10**7),
    )(tokens, out_grad, lengths, self_flags, episode_weight, g1, b1, g2, b2, w_qkv, w_out, w_up, w_down)


def solution(mesh):
    shape = dict(mesh.shape)

    def on_device(
        tokens, lengths, self_flags, episode_weight, ln1_gain, ln1_bias, w_qkv, w_out, ln2_gain, ln2_bias, w_up,
        w_down, out_grad,
    ):
        z = Sizes(shape, tokens.shape, w_qkv.shape, w_up.shape, lengths.shape)
        row = lambda a: a.reshape(1, -1)
        results = layer(
            z, tokens, out_grad, lengths, self_flags, episode_weight, row(ln1_gain), row(ln1_bias), row(ln2_gain),
            row(ln2_bias), jnp.transpose(w_qkv, (1, 0, 2)), w_out, w_up, w_down,
        )
        y, gin, norms, ro, rx, ry = results[:6]
        output = jnp.transpose(y, (1, 0, 2))
        grad_input = jnp.transpose(gin, (1, 0, 2))
        kinds, _ = wgrad_kinds(z)
        if z.pairs:

            def summed(name):
                n, off, _ = kinds[name]
                sl = slice(off, off + n)
                return ro[:, sl].astype(f32) + rx[:, sl].astype(f32) + ry[:, sl].astype(f32)

            grad_down = summed("down").T
            grad_up = summed("up")
            grad_out = summed("out").T
            grad_qkv = summed("qkv").reshape(-1, 3, z.LW)
            both = norms
        else:
            g1_all, g2_all, gy_all, gm_all, act, gpre, gproj, att = results[10:]

            def over_tokens(a, b, dim):
                value = jnp.einsum("ta,tb->ab", a, b, preferred_element_type=f32).astype(bf16)
                return lax.psum_scatter(value, ("dp", "sp"), scatter_dimension=dim, tiled=True).astype(f32)

            grad_down = over_tokens(act, gy_all, 1)
            grad_up = over_tokens(g2_all, gpre, 0)
            grad_out = over_tokens(att, gm_all, 1)
            grad_qkv = over_tokens(g1_all, gproj, 0).reshape(-1, 3, z.LW)
            both = lax.psum(norms, ("dp", "sp", "tp"))
        return output, grad_input, grad_qkv, grad_out, grad_up, grad_down, both[0:2], both[2:4]

    return jax.shard_map(
        on_device,
        mesh=mesh,
        in_specs=(
            P(("sp", "tp"), "dp", None), P("dp", None), P("dp", None), P("dp", None), P(), P(), P(None, None, "tp"),
            P("tp", None), P(), P(), P(None, "tp"), P("tp", None), P(("sp", "tp"), "dp", None),
        ),
        out_specs=(
            P(("sp", "tp"), "dp", None), P(("sp", "tp"), "dp", None), P(("dp", "sp"), None, "tp"),
            P("tp", ("dp", "sp")), P(("dp", "sp"), "tp"), P("tp", ("dp", "sp")), P(), P(),
        ),
        check_vma=False,
    )
```

```python
import jax
import jax.numpy as jnp
from jax import lax
from jax.experimental import pallas as pl
from jax.experimental.pallas import tpu as pltpu
from jax.sharding import PartitionSpec as P

DH = 128
EPSILON = 1e-05
NEG = -1e30
f32 = jnp.float32
bf16 = jnp.bfloat16
MESH = pl.DeviceIdType.MESH


def dot(a, b, ca, cb):
    return lax.dot_general(a, b, (((ca,), (cb,)), ((), ())), preferred_element_type=f32)


def lanes(start, size):
    if isinstance(start, int):
        return pl.ds(start, size)
    return pl.ds(pl.multiple_of(start, 128), size)


def rows_at(start, size):
    if isinstance(start, int):
        return pl.ds(start, size)
    return pl.ds(pl.multiple_of(start, 64), size)


def norm_parts(values):
    average = jnp.mean(values, axis=-1, keepdims=True)
    centred = values - average
    variance = jnp.mean(centred * centred, axis=-1, keepdims=True)
    inverse = lax.rsqrt(variance + EPSILON)
    return centred * inverse, inverse


def norm_back(unit, inverse, gain, grad):
    scaled = grad * gain
    first = jnp.mean(scaled, axis=-1, keepdims=True)
    second = jnp.mean(scaled * unit, axis=-1, keepdims=True)
    return inverse * (scaled - first - unit * second)


class Sizes:
    def __init__(self, mesh_shape, tokens, w_qkv, w_up, lengths):
        self.n_dp = mesh_shape["dp"]
        self.n_sp = mesh_shape["sp"]
        self.n_tp = mesh_shape["tp"]
        self.S = tokens[0]
        self.R = tokens[1]
        self.D = tokens[2]
        self.LW = w_qkv[2]
        self.F = w_up[1]
        self.E = lengths[1]
        self.T = self.S * self.n_tp
        self.SEQ = self.T * self.n_sp
        self.H = self.LW // DH
        self.pairs = self.n_dp == 2 and self.n_sp == 4


def wgrad_kinds(z):
    half = z.F // 2
    out, offset = {}, 0
    for name, n, along in (
        ("d0", half, 5), ("d1", half, 5), ("u0", half, 6), ("u1", half, 6), ("out", z.LW, 6), ("q", z.LW, 4),
        ("kv", 2 * z.LW, 5),
    ):
        out[name] = (n, offset, n * along // 8)
        offset += n
    return out, offset


def make_kernel(z):
    S, R, D, LW, F, T, SEQ, H = z.S, z.R, z.D, z.LW, z.F, z.T, z.SEQ, z.H
    RT = R * T
    kinds, w_lanes = wgrad_kinds(z)
    scale = DH ** (-0.5)
    PD = D // 8

    def kernel(
        tok, og, lens, flags, eweight, g1, b1, g2, b2, wqkv_hbm, wout_hbm, wup_hbm, wdn_hbm,
        y_out, gin, norms, ro, rx, ry, sw, tx, ty, ph, g1h, extra_g2, extra_gy, extra_gm, extra_act, extra_gpre,
        extra_gproj, extra_att,
        arena, xact, xgy, wqkv, wout, ga, g2b, gyb, q, kv, act, gpre, gproj, att, part, part2, slots, slots2,
        mid, ds, stage, nr, total,
        ag_s, ag_r, rs_s, rs_r, kv_s, kv_r, dk_s, dk_r, x_s, x_r, w_s, w_r, n_s, n_r, loc, raw_sem, stg_sem,
        rt_sem, free_x, free_c, free_y,
    ):
        dp = lax.axis_index("dp")
        sp = lax.axis_index("sp")
        tp = lax.axis_index("tp")
        par = lax.rem(sp, 2)
        yy = lax.div(sp, 2)
        mate = sp + 1 - 2 * par
        far = lax.rem(sp + 2, 4)
        odp = 1 - dp
        kv_row = sp * T
        own = tp * S

        def remote(src, dst, ssem, rsem, device):
            return pltpu.make_async_remote_copy(
                src_ref=src, dst_ref=dst, send_sem=ssem, recv_sem=rsem, device_id=device, device_id_type=MESH
            )

        class Gather:
            def __init__(self, buf, i, r):
                self.buf, self.i, self.r = buf, i, r

            def copy(self, shard, way, hop):
                sl = self.buf.at[rows_at(self.r * T + shard * S, S), :]
                to = tp + 1 if way == 0 else tp - 1
                return remote(
                    sl, sl, ag_s.at[self.i, self.r, way * 3 + hop], ag_r.at[self.i, self.r, shard], (dp, sp, to)
                )

            def start(self):
                @pl.when(tp < 3)
                def _():
                    self.copy(tp, 0, 0).start()

                @pl.when(tp > 0)
                def _():
                    self.copy(tp, 1, 0).start()

            def step(self, hop):
                @pl.when(tp >= hop)
                def _():
                    self.copy(tp - hop, 0, 0).wait_recv()

                if hop < 3:

                    @pl.when((tp >= hop) & (tp < 3))
                    def _():
                        self.copy(tp - hop, 0, hop).start()

                @pl.when(tp <= 3 - hop)
                def _():
                    self.copy(tp + hop, 1, 0).wait_recv()

                if hop < 3:

                    @pl.when((tp <= 3 - hop) & (tp > 0))
                    def _():
                        self.copy(tp + hop, 1, hop).start()

            def drain(self):
                for hop in range(3):

                    @pl.when((tp >= hop) & (tp < 3))
                    def _(hop=hop):
                        self.copy(tp - hop, 0, hop).wait_send()

                    @pl.when((tp <= 3 - hop) & (tp > 0))
                    def _(hop=hop):
                        self.copy(tp + hop, 1, hop).wait_send()

        class Scatter:
            def __init__(self, buf, box, i, r):
                self.buf, self.box, self.i, self.r = buf, box, i, r

            def copy(self, way, k):
                o = 3 - k if way == 0 else k
                to = tp + 1 if way == 0 else tp - 1
                n = way * 3 + k
                return remote(
                    self.buf.at[pl.ds(self.r * T + o * S, S), :],
                    self.box.at[self.r, k if way == 0 else 4 - k],
                    rs_s.at[self.i, self.r, n],
                    rs_r.at[self.i, self.r, n],
                    (dp, sp, to),
                )

            def start(self):
                for k in range(3):

                    @pl.when(tp == 0)
                    def _(k=k):
                        self.copy(0, k).start()

                    @pl.when(tp == 3)
                    def _(k=k):
                        self.copy(1, k).start()

            def relay(self, way, k):
                o = 3 - k if way == 0 else k
                sl = pl.ds(self.r * T + o * S, S)
                self.copy(way, k).wait_recv()
                self.buf[sl, :] = (
                    self.buf[sl, :].astype(f32) + self.box[self.r, k if way == 0 else 4 - k].astype(f32)
                ).astype(bf16)
                self.copy(way, k).start()

            def step(self, k):
                first, second, n = (0, 1, k) if k < 2 else (1, 0, 0)

                @pl.when(tp == 1)
                def _():
                    self.relay(first, n)

                @pl.when(tp == 2)
                def _():
                    self.relay(second, n)

            def finish(self):
                total[...] = self.buf[rows_at(self.r * T + own, S), :].astype(f32)
                for o in range(1, 4):

                    @pl.when(tp == o)
                    def _(o=o):
                        self.copy(0, 3 - o).wait_recv()
                        total[...] += self.box[self.r, 3 - o].astype(f32)

                for o in range(0, 3):

                    @pl.when(tp == o)
                    def _(o=o):
                        self.copy(1, o).wait_recv()
                        total[...] += self.box[self.r, 4 - o].astype(f32)

            def drain(self):
                for k in range(3):

                    @pl.when(tp < 3 - k)
                    def _(k=k):
                        self.copy(0, k).wait_send()

                    @pl.when(tp > k)
                    def _(k=k):
                        self.copy(1, k).wait_send()

        class Keys:
            def __init__(self, r):
                self.r = r

            def copy(self, block, to, n):
                sl = kv.at[self.r, rows_at(block * T, T), :]
                return remote(sl, sl, kv_s.at[self.r, n], kv_r.at[self.r, block], (dp, to, tp))

            def start(self):
                @pl.when(sp < 2)
                def _():
                    self.copy(sp, sp + 2, 0).start()

                @pl.when(par == 0)
                def _():
                    self.copy(sp, sp + 1, 1).start()

            def step(self):
                for me, block, to in ((2, 0, 3), (3, 1, 2)):

                    @pl.when(sp == me)
                    def _(block=block, to=to):
                        self.copy(block, to, 0).wait_recv()
                        self.copy(block, to, 2).start()

            def finish(self):
                for me, block in ((1, 0), (2, 1), (3, 0), (3, 2)):

                    @pl.when(sp == me)
                    def _(block=block):
                        self.copy(block, 0, 0).wait_recv()

            def drain(self):
                @pl.when(sp < 2)
                def _():
                    self.copy(sp, sp + 2, 0).wait_send()

                @pl.when(par == 0)
                def _():
                    self.copy(sp, sp + 1, 1).wait_send()

                for me, block, to in ((2, 0, 3), (3, 1, 2)):

                    @pl.when(sp == me)
                    def _(block=block, to=to):
                        self.copy(block, to, 2).wait_send()

        KW = 2 * LW
        DK0 = 5 * RT
        DR0 = RT

        class KeyGrads:
            def __init__(self, r):
                self.r = r

            def src(self, block):
                return arena.at[pl.ds(DK0 + block * T, T), pl.ds(self.r * KW, KW)]

            def dst(self, box):
                return arena.at[pl.ds(DR0 + box * T, T), pl.ds(self.r * KW, KW)]

            def copy(self, block, to, box, n):
                return remote(
                    self.src(block), self.dst(box), dk_s.at[self.r, n], dk_r.at[self.r, box], (dp, to, tp)
                )

            def start(self):
                for me, block, to, box, n in ((3, 0, 2, 0, 0), (3, 2, 2, 1, 1), (2, 1, 3, 0, 0), (1, 0, 0, 1, 0)):

                    @pl.when(sp == me)
                    def _(block=block, to=to, box=box, n=n):
                        self.copy(block, to, box, n).start()

            def step(self):
                for me, block, to in ((2, 0, 0), (3, 1, 1)):

                    @pl.when(sp == me)
                    def _(block=block, to=to):
                        self.copy(block, to, 0, 2).wait_recv()
                        mine = pl.ds(DK0 + block * T, T)
                        col = pl.ds(self.r * KW, KW)
                        arena[mine, col] = (
                            arena[mine, col].astype(f32) + arena[pl.ds(DR0, T), col].astype(f32)
                        ).astype(bf16)
                        self.copy(block, to, 2, 2).start()

            def finish(self):
                col = pl.ds(self.r * KW, KW)
                there = pl.ds(self.r * T, T)
                to = pl.ds(LW, KW)
                for me, boxes in ((0, (1, 2)), (1, (2,)), (2, (1,)), (3, ())):

                    @pl.when(sp == me)
                    def _(me=me, boxes=boxes):
                        value = arena[pl.ds(DK0 + me * T, T), col].astype(f32)
                        for box in boxes:
                            self.copy(0, 0, box, 0).wait_recv()
                            value += arena[pl.ds(DR0 + box * T, T), col].astype(f32)
                        gproj[there, to] = value.astype(bf16)

            def drain(self):
                for me, block, to, box, n in (
                    (3, 0, 2, 0, 0), (3, 2, 2, 1, 1), (2, 1, 3, 0, 0), (1, 0, 0, 1, 0), (2, 0, 0, 2, 2), (3, 1, 1, 2, 2),
                ):

                    @pl.when(sp == me)
                    def _(block=block, to=to, box=box, n=n):
                        self.copy(block, to, box, n).wait_send()

        ends = []
        for r in range(R):
            run, row = 0, []
            for e in range(z.E):
                run = run + lens[r, e]
                row.append(run)
            ends.append(row)

        def first_norm(r):
            unit, _ = norm_parts(tok[:, r, :].astype(f32))
            ga[rows_at(r * T + own, S), :] = (unit * g1[...] + b1[...]).astype(bf16)

        def weighted_grad(r):
            place = sp * T + own + lax.broadcasted_iota(jnp.int32, (S, 1), 0)
            factor = jnp.full((S, 1), eweight[r, 0] * (1.0 + flags[r, 0].astype(f32)), f32)
            for e in range(1, z.E):
                factor = jnp.where(
                    place >= ends[r][e - 1], eweight[r, e] * (1.0 + flags[r, e].astype(f32)), factor
                )
            return og[:, r, :].astype(f32) * factor

        def project(r, j):
            value = dot(ga[r * T : (r + 1) * T, :], wqkv[:, j * LW : (j + 1) * LW], 1, 0).astype(bf16)
            if j == 0:
                q[r * T : (r + 1) * T, :] = value
            else:
                kv[r, rows_at(kv_row, T), (j - 1) * LW : j * LW] = value

        def mask(r):
            here = kv_row + lax.broadcasted_iota(jnp.int32, (T, 1), 0)
            begin = jnp.zeros((T, 1), jnp.int32)
            for e in range(z.E):
                begin = jnp.where(here >= ends[r][e], jnp.maximum(begin, ends[r][e]), begin)
            there = lax.broadcasted_iota(jnp.int32, (T, SEQ), 1)
            ds[...] = jnp.where((there <= here) & (there >= begin), 0.0, NEG).astype(bf16)

        half = T // 2
        ppl = D // SEQ
        keep = [act, gpre]

        def attend(r):
            def one(i, carry):
                rs = rows_at(i * half, half)
                qs = rows_at(r * T + i * half, half)
                for h in range(H):
                    hs = slice(h * DH, (h + 1) * DH)
                    s = dot(q[qs, hs], kv[r, :, hs], 1, 1) * scale + ds[rs, :].astype(f32)
                    peak = jnp.max(s, axis=1, keepdims=True)
                    e = jnp.exp(s - peak)
                    p = (e * (1.0 / jnp.sum(e, axis=1, keepdims=True))).astype(bf16)
                    keep[r][rows_at((h // ppl) * T + i * half, half), (h % ppl) * SEQ : (h % ppl + 1) * SEQ] = p
                    att[qs, hs] = dot(p, kv[r, :, LW + h * DH : LW + (h + 1) * DH], 1, 0).astype(bf16)
                return carry

            lax.fori_loop(0, 2, one, 0)

        def times(lhs, r, weight, out, transposed):
            width = 512
            n = out.shape[1] // width

            def one(j, carry):
                cs = lanes(j * width, width)
                w = weight(j, width)
                out[r * T : (r + 1) * T, cs] = dot(lhs, w, 1, 1 if transposed else 0).astype(bf16)
                return carry

            lax.fori_loop(0, n, one, 0)

        def project_out(r):
            def one(j, carry):
                cs = lanes(j * 512, 512)
                part[r * T : (r + 1) * T, cs] = dot(att[r * T : (r + 1) * T, :], wout[:, cs], 1, 0).astype(bf16)
                return carry

            lax.fori_loop(0, D // 512, one, 0)

        def ffn(r, low, high):
            rs = slice(r * T, (r + 1) * T)

            def one(j, carry):
                cs = lanes(j * 256, 256)
                pre = dot(g2b[rs, :], arena[0:D, cs], 1, 0)
                e = 0.5 * (1.0 + lax.erf(pre * 0.7071067811865476))
                act[rs, cs] = (pre * e).astype(bf16)
                slope = e + pre * (jnp.exp(-0.5 * pre * pre) * 0.3989422804014327)
                back = dot(gyb[rs, :], arena[rows_at(D + j * 256, 256), :], 1, 1)
                gpre[rs, cs] = (back * slope).astype(bf16)
                return carry

            lax.fori_loop(low, high, one, 0)

        def ffn_back(r):
            rs = slice(r * T, (r + 1) * T)

            def one(j, carry):
                part[rs, lanes(j * 512, 512)] = dot(gpre[rs, :], arena[rows_at(j * 512, 512), :], 1, 1).astype(bf16)
                return carry

            lax.fori_loop(0, D // 512, one, 0)

        def ffn_out(r):
            rs = slice(r * T, (r + 1) * T)

            def one(j, carry):
                cs = lanes(j * 512, 512)
                part2[rs, cs] = dot(act[rs, :], arena[D : D + F, cs], 1, 0).astype(bf16)
                return carry

            lax.fori_loop(0, D // 512, one, 0)

        def second_norm(r):
            value = tok[:, r, :].astype(f32) + total[...]
            mid[r] = value
            unit, _ = norm_parts(value)
            g2b[rows_at(r * T + own, S), :] = (unit * g2[...] + b2[...]).astype(bf16)

        def add_norms(grad, unit):
            sums = (jnp.sum(grad * unit, axis=0, keepdims=True), jnp.sum(grad, axis=0, keepdims=True))
            for i in range(8):
                piece = sums[i // 4][:, (i % 4) * (D // 4) : (i % 4 + 1) * (D // 4)]
                nr[0, pl.ds(tp, 1), 8 + i : 9 + i, :] += piece[None]

        def second_norm_back(r):
            unit, inverse = norm_parts(mid[r])
            grad = total[...]
            add_norms(grad, unit)
            value = weighted_grad(r) + norm_back(unit, inverse, g2[...], grad)
            gin[r] = value
            ga[rows_at(r * T + own, S), :] = value.astype(bf16)

        def first_norm_back(r):
            unit, inverse = norm_parts(tok[:, r, :].astype(f32))
            grad = total[...]
            gin[r] = gin[r] + norm_back(unit, inverse, g1[...], grad)

        def attend_back(r):
            rows = slice(r * T, (r + 1) * T)
            for h in range(H):
                hs = slice(h * DH, (h + 1) * DH)
                vs = slice(LW + h * DH, LW + (h + 1) * DH)
                go = gproj[rows, hs]
                pc = slice((h % ppl) * SEQ, (h % ppl + 1) * SEQ)
                for t in range(2):
                    ts = slice(t * half, (t + 1) * half)
                    gp = dot(gproj[r * T + t * half : r * T + (t + 1) * half, hs], kv[r, :, vs], 1, 1)
                    p = keep[r][(h // ppl) * T + t * half : (h // ppl) * T + (t + 1) * half, pc].astype(f32)
                    x = p * gp
                    delta = jnp.sum(x, axis=1, keepdims=True)
                    ds[ts, :] = ((x - p * delta) * scale).astype(bf16)
                k0 = r * KW + h * DH
                arena[DK0 : DK0 + SEQ, k0 : k0 + DH] = dot(ds[...], q[rows, hs], 0, 0).astype(bf16)
                v0 = r * KW + LW + h * DH
                arena[DK0 : DK0 + SEQ, v0 : v0 + DH] = dot(
                    keep[r][(h // ppl) * T : (h // ppl + 1) * T, pc], go, 0, 0
                ).astype(bf16)
                gproj[rows, hs] = dot(ds[...], kv[r, :, hs], 1, 0).astype(bf16)

        def grad_attended(r):
            rows = slice(r * T, (r + 1) * T)
            gproj[rows, 0:LW] = dot(ga[rows, :], wout[...], 1, 1).astype(bf16)

        def qkv_back(r):
            rs = slice(r * T, (r + 1) * T)
            ns = slice(7 * RT + r * T, 7 * RT + (r + 1) * T)
            width = D // 4

            def one(j, carry):
                cs = lanes(j * width, width)
                value = dot(gproj[rs, :], wqkv[rows_at(j * width, width), :], 1, 1)
                part[rs, cs] = value.astype(bf16)
                normed = arena[ns, cs].astype(f32)
                nr[0, pl.ds(tp, 1), pl.ds(j, 1), :] += jnp.sum(value * normed, axis=0, keepdims=True)[None]
                nr[0, pl.ds(tp, 1), pl.ds(4 + j, 1), :] += jnp.sum(value, axis=0, keepdims=True)[None]
                return carry

            lax.fori_loop(0, 4, one, 0)

        load_out = pltpu.make_async_copy(wout_hbm, wout, loc.at[0])
        load_qkv = [
            pltpu.make_async_copy(wqkv_hbm.at[j], wqkv.at[:, pl.ds(j * LW, LW)], raw_sem.at[j]) for j in range(3)
        ]
        load_up = pltpu.make_async_copy(wup_hbm, arena.at[pl.ds(0, D), :], loc.at[1])
        load_down = pltpu.make_async_copy(wdn_hbm, arena.at[pl.ds(D, F), :], loc.at[2])
        save_p = [pltpu.make_async_copy(keep[r], ph.at[r], loc.at[3 + r]) for r in range(R)]
        load_p = [pltpu.make_async_copy(ph.at[r], keep[r], loc.at[3 + r]) for r in range(R)]
        save_g1 = pltpu.make_async_copy(ga, g1h, loc.at[5])
        load_g1 = pltpu.make_async_copy(g1h, arena.at[pl.ds(7 * RT, RT), :], loc.at[5])

        XP, XG, XH, XJ = RT, 2 * RT, 3 * RT, 4 * RT
        there = (dp, mate, tp)
        oth = 1 - par

        def halves(buf, buf_row, box, box_row, box_lane, n):
            return [
                remote(
                    buf.at[pl.ds(buf_row, RT), lanes(b * 2 * PD + oth * PD, PD)],
                    box.at[pl.ds(box_row, RT), pl.ds(box_lane + b * PD, PD)],
                    x_s.at[n + b],
                    x_r.at[n + b],
                    there,
                )
                for b in range(4)
            ]

        def piece(buf, row, size, lane, width, box, box_row, box_lane, n):
            return [
                remote(
                    buf.at[pl.ds(row, size), pl.ds(lane, width)],
                    box.at[pl.ds(box_row, size), pl.ds(box_lane, width)],
                    x_s.at[n],
                    x_r.at[n],
                    there,
                )
            ]

        trade_rows = [[piece(act, r * T, T, h * F // 2, F // 2, xact, r * T, h * F // 2, 2 * h + r) for r in range(R)] for h in range(2)]
        trade_gy = halves(gyb, 0, xgy, 0, 0, 22)
        trade_up = piece(gpre, 0, RT, 0, F, arena, XP, 0, 21) + halves(g2b, 0, arena, XG, 0, 6)
        trade_g1 = halves(arena, 7 * RT, arena, XH, 0, 10)
        trade_out = piece(att, 0, RT, 0, LW, arena, XJ, 3 * LW, 18) + halves(ga, 0, arena, XH, D // 2, 14)
        trade_q = piece(gproj, 0, RT, 0, LW, arena, XJ, 0, 19)
        trade_kv = piece(gproj, 0, RT, LW, 2 * LW, arena, XJ, LW, 20)

        names = list(kinds)
        operands = {
            "d0": ((gyb, 0), (act, 0), (xgy, 0, 0), (xact, 0, 0)),
            "d1": ((gyb, 0), (act, F // 2), (xgy, 0, 0), (xact, 0, F // 2)),
            "u0": ((g2b, 0), (gpre, 0), (arena, XG, 0), (arena, XP, 0)),
            "u1": ((g2b, 0), (gpre, F // 2), (arena, XG, 0), (arena, XP, F // 2)),
            "out": ((ga, 0), (att, 0), (arena, XH, D // 2), (arena, XJ, 3 * LW)),
            "q": ((arena, 7 * RT), (gproj, 0), (arena, XH, 0), (arena, XJ, 0)),
            "kv": ((arena, 7 * RT), (gproj, LW), (arena, XH, 0), (arena, XJ, LW)),
        }

        def tile(t, way, size):
            if way == 0:
                return arena.at[pl.ds(0, PD), pl.ds((t % 2) * (D // 2), size)]
            return arena.at[pl.ds(XG + PD, PD), pl.ds(D // 2 + (t % 2) * (D // 4), size)]

        def w_copy(name, which):
            t = names.index(name)
            n, off, a = kinds[name]
            ca, cb = pl.ds(off, a), pl.ds(off + a, n - a)
            x_to, y_to = (odp, sp, tp), (dp, far, tp)
            src, dst, to = {
                "S2": (sw.at[0, :, ca], tx.at[:, ca], x_to),
                "S4": (sw.at[0, :, cb], ty.at[:, cb], y_to),
                "S1": (sw.at[1, :, ca], rx.at[:, ca], x_to),
                "S3": (sw.at[2, :, cb], ry.at[:, cb], y_to),
                "R1": (tile(t, 0, a), ry.at[:, ca], y_to),
                "R2": (tile(t, 1, n - a), rx.at[:, cb], x_to),
            }[which]
            k = ("S1", "S2", "S3", "S4", "R1", "R2").index(which)
            return remote(src, dst, w_s.at[t, k], w_r.at[t, k], to)

        first_sends = [("S2",), ("S1",), (), ()]

        def stage_copy(name, i):
            n, off, _ = kinds[name]
            dst = ro.at[:, pl.ds(off, n)] if i == 3 else sw.at[i, :, pl.ds(off, n)]
            return pltpu.make_async_copy(stage.at[i % 2, :, pl.ds(0, n)], dst, stg_sem.at[i % 2])

        def weight_grad(name):
            (own_d, own_row), (own_r, own_lane), (mate_d, d_row, d_lane), (mate_r, r_row, r_lane) = operands[name]
            n, off, _ = kinds[name]
            width = n
            for i, (dx, dy) in enumerate(((1, 1), (1, 0), (0, 1), (0, 0))):
                to_dp = odp if dx else dp
                to_y = 1 - yy if dy else yy
                b4 = to_dp * 2 + to_y

                def one(j, carry, b4=b4, i=i):
                    value = dot(
                        own_d[own_row : own_row + RT, lanes(b4 * 2 * PD + par * PD, PD)],
                        own_r[:, lanes(own_lane + j * width, width)],
                        0,
                        0,
                    )
                    value += dot(
                        mate_d[d_row : d_row + RT, lanes(d_lane + b4 * PD, PD)],
                        mate_r[r_row : r_row + RT, lanes(r_lane + j * width, width)],
                        0,
                        0,
                    )
                    stage[i % 2, :, lanes(j * width, width)] = value.astype(bf16)
                    return carry

                lax.fori_loop(0, n // width, one, 0)
                stage_copy(name, i).start()
                if i:
                    stage_copy(name, i - 1).wait()
                    for which in first_sends[i - 1]:
                        w_copy(name, which).start()
            stage_copy(name, 3).wait()

        def relay_sum(name, way):
            t = names.index(name)
            n, off, a = kinds[name]
            first, size, box, block, need, send = (
                (0, a, tx, 2, "S2", "R1") if way == 0 else (a, n - a, ty, 1, "S4", "R2")
            )
            if t > 1:
                w_copy(names[t - 2], send).wait_send()
            there_l = pl.ds(off + first, size)
            mine, met = tile(t, way, size), arena.at[pl.ds(PD, PD), pl.ds(0, size)]
            own_c = pltpu.make_async_copy(sw.at[block, :, there_l], mine, rt_sem.at[way])
            got_c = pltpu.make_async_copy(box.at[:, there_l], met, rt_sem.at[2 + way])
            own_c.start()
            w_copy(name, need).wait_recv()
            got_c.start()
            own_c.wait()
            got_c.wait()
            mine[...] = (mine[...].astype(f32) + met[...].astype(f32)).astype(bf16)
            w_copy(name, send).start()

        def finish_sums(name):
            for which in ("S1", "S3", "R1", "R2"):
                w_copy(name, which).wait_recv()
            for which in ("S1", "S2", "S3", "S4"):
                w_copy(name, which).wait_send()
            if names.index(name) >= len(names) - 2:
                w_copy(name, "R1").wait_send()
                w_copy(name, "R2").wait_send()

        norm_axes = ((4, tp), (4, sp), (z.n_dp, dp))

        def norm_copies(i):
            axis_n, index = norm_axes[i]
            slot = nr.at[i, pl.ds(index, 1)]
            copies = []
            for d in range(1, axis_n):
                to = lax.rem(index + d, axis_n)
                device = ((dp, sp, to), (dp, to, tp), (to, sp, tp))[i]
                copies.append(remote(slot, slot, n_s.at[i, d - 1], n_r.at[i, d - 1], device))
            return copies

        def norm_result(value):
            norms[4:16, :] = value[4:16, :]
            for i in range(4):
                cs = slice(i * (D // 4), (i + 1) * (D // 4))
                norms[i : i + 1, :] = (value[i : i + 1, :] - b1[:, cs] * value[4 + i : 5 + i, :]) / g1[:, cs]

        def norm_add(i):
            for c in norm_copies(i):
                c.wait_send()
                c.wait_recv()
            value = nr[i, 0]
            for n in range(1, norm_axes[i][0]):
                value = value + nr[i, n]
            return value

        load_out.start()
        for c in load_qkv:
            c.start()
        barrier = pltpu.get_barrier_semaphore()
        greet = [(dp, sp, lax.rem(tp + d, 4)) for d in (1, 2, 3)]
        greet += [(dp, lax.rem(sp + d, 4), tp) for d in (1, 2, 3)]
        if z.pairs:
            greet += [(odp, sp, tp)]
        for device in greet:
            pl.semaphore_signal(barrier, inc=1, device_id=device, device_id_type=MESH)
        first_norm(0)
        pl.semaphore_wait(barrier, len(greet))

        ag1 = [Gather(ga, 0, r) for r in range(R)]
        ag2 = [Gather(g2b, 1, r) for r in range(R)]
        ag3 = [Gather(gyb, 2, r) for r in range(R)]
        ag4 = [Gather(ga, 3, r) for r in range(R)]
        rs1 = [Scatter(part, slots, 0, r) for r in range(R)]
        rs3 = [Scatter(part, slots, 1, r) for r in range(R)]
        rs4 = [Scatter(part, slots, 2, r) for r in range(R)]
        rs2 = [Scatter(part2, slots2, 3, r) for r in range(R)]
        keys = [Keys(r) for r in range(R)]
        kgrads = [KeyGrads(r) for r in range(R)]

        def grad_rows(r):
            gyb[rows_at(r * T + own, S), :] = weighted_grad(r).astype(bf16)

        def clear():
            nr[0, pl.ds(tp, 1)] = jnp.zeros((1,) + nr.shape[2:], f32)
            for b in range(1, 4):

                @pl.when(b > sp)
                def _(b=b):
                    kv[:, b * T : (b + 1) * T, :] = jnp.zeros((R, T, KW), bf16)

        def keys_out(r):
            if r == 0:
                for c in load_qkv:
                    c.wait()
            project(r, 1)
            project(r, 2)
            keys[r].start()

        def queries(r):
            project(r, 0)

        def attention(r):
            attend(r)
            save_p[r].start()
            if r == 0:
                load_out.wait()
            project_out(r)
            rs1[r].start()

        def sum_one(r):
            rs1[r].finish()
            second_norm(r)
            ag2[r].start()

        def before_ffn():
            load_up.wait()
            load_down.wait()
            save_g1.wait()
            for c in save_p:
                c.wait()
            for g in ag1:
                g.drain()

        def ffn_a(r):
            ffn(r, 0, F // 512)

        def ffn_b(r):
            ffn(r, F // 512, F // 256)

        def ffn_c(r):
            rs1[r].drain()
            ffn_back(r)
            rs3[r].start()

        def sum_three(r):
            rs3[r].finish()
            second_norm_back(r)
            ag4[r].start()

        def sum_two(r):
            rs2[r].finish()
            y_out[r] = (mid[r] + total[...]).astype(bf16)

        def sum_four(r):
            rs4[r].finish()
            first_norm_back(r)

        def offer():
            if z.pairs:
                pl.semaphore_signal(free_x, inc=1, device_id=there, device_id_type=MESH)

        def trade_act(h, r):
            if z.pairs:
                for c in trade_rows[h][r]:
                    c.start()

        def trade_grad():
            if z.pairs:
                for c in trade_gy:
                    c.start()

        def trade_one():
            if z.pairs:
                pl.semaphore_wait(free_x, 1)
                for c in trade_up:
                    c.start()

        def grads_down(h):
            if z.pairs:
                for c in trade_rows[h][0] + trade_rows[h][1] + (trade_gy if h == 0 else []):
                    c.wait_recv()
                weight_grad(names[h])

        def grads_up(h):
            if z.pairs:
                if h == 0:
                    for c in trade_up:
                        c.wait_recv()
                weight_grad(names[2 + h])

        def offer_two():
            if z.pairs:
                for c in trade_rows[0][0] + trade_rows[0][1] + trade_rows[1][0] + trade_rows[1][1] + trade_gy + trade_up:
                    c.wait_send()
            else:
                dumps = [
                    pltpu.make_async_copy(act, extra_act, stg_sem.at[0]),
                    pltpu.make_async_copy(gpre, extra_gpre, stg_sem.at[1]),
                    pltpu.make_async_copy(g2b, extra_g2, rt_sem.at[0]),
                    pltpu.make_async_copy(gyb, extra_gy, rt_sem.at[1]),
                ]
                for c in dumps:
                    c.start()
                for c in dumps:
                    c.wait()
            pl.semaphore_signal(free_c, inc=1, device_id=there, device_id_type=MESH)
            pl.semaphore_signal(free_y, inc=1, device_id=(dp, far, tp), device_id_type=MESH)
            for c in load_p:
                c.start()

        def trade_two():
            load_g1.wait()
            if z.pairs:
                for c in trade_g1:
                    c.start()

        def attention_back(r):
            load_p[r].wait()
            attend_back(r)
            if r == 0:
                pl.semaphore_wait(free_c, 1)
            kgrads[r].start()

        def keys_back(r):
            if r == 0:
                pl.semaphore_wait(free_y, 1)
            kgrads[r].step()

        def keys_sum(r):
            kgrads[r].finish()

        def trade_three():
            if z.pairs:
                for c in trade_out:
                    c.start()

        def grads_out():
            if z.pairs:
                for c in trade_out:
                    c.wait_recv()
                weight_grad("out")

        def trade_four():
            if z.pairs:
                for c in trade_q:
                    c.start()

        def trade_five():
            if z.pairs:
                for c in trade_kv:
                    c.start()

        def grads_q():
            if z.pairs:
                for c in trade_g1 + trade_q:
                    c.wait_recv()
                weight_grad("q")

        def grads_kv():
            if z.pairs:
                for c in trade_kv:
                    c.wait_recv()
                weight_grad("kv")

        def push(i):
            if z.pairs:
                w_copy(names[i], "S4").start()
                w_copy(names[i], "S3").start()

        def pass_y(i):
            if z.pairs:
                relay_sum(names[i], 0)

        def pass_x(i):
            if z.pairs:
                relay_sum(names[i], 1)

        def back_c(r):
            rs3[r].drain()
            qkv_back(r)
            rs4[r].start()

        def norms_at(i):
            if not z.pairs:
                if i == 3:
                    norm_result(nr[0, pl.ds(tp, 1)][0])
                return
            if i:
                value = norm_add(i - 1)
                if i == 3:
                    norm_result(value)
                    return
                nr[i, pl.ds((sp, dp)[i - 1], 1)] = value[None]
            for c in norm_copies(i):
                c.start()

        def the_end():
            if z.pairs:
                for name in names:
                    finish_sums(name)
                for c in trade_g1 + trade_out + trade_q + trade_kv:
                    c.wait_send()
            else:
                dumps = [
                    pltpu.make_async_copy(ga, extra_gm, stg_sem.at[0]),
                    pltpu.make_async_copy(gproj, extra_gproj, stg_sem.at[1]),
                    pltpu.make_async_copy(att, extra_att, rt_sem.at[0]),
                ]
                for c in dumps:
                    c.start()
                for c in dumps:
                    c.wait()
            for g in keys + ag2 + ag3 + ag4 + rs2 + rs4 + kgrads:
                g.drain()

        ag1[0].start()
        grad_rows(0)
        clear()
        first_norm(1)
        load_up.start()
        grad_rows(1)
        ag1[0].step(1)
        ag1[0].step(2)
        ag1[1].start()
        ag1[0].step(3)
        keys_out(0)
        mask(0)
        queries(0)
        ag1[1].step(1)
        ag1[1].step(2)
        ag3[1].start()
        keys[0].step()
        load_down.start()
        keys[0].finish()
        ag3[0].start()
        attention(0)
        ag1[1].step(3)
        save_g1.start()
        keys_out(1)
        ag3[0].step(1)
        keys[1].step()
        queries(1)
        rs1[0].step(0)
        ag3[1].step(1)
        mask(1)
        ag3[0].step(2)
        keys[1].finish()
        attention(1)
        before_ffn()
        rs1[0].step(1)
        rs1[0].step(2)
        ag3[1].step(2)
        rs1[1].step(0)
        sum_one(0)
        rs1[1].step(1)
        rs1[1].step(2)
        ag2[0].step(1)
        ag3[1].step(3)
        ag2[0].step(2)
        sum_one(1)
        ag3[0].step(3)
        trade_grad()
        ag2[0].step(3)
        ffn_a(0)
        ffn_b(0)
        trade_act(0, 0)
        ag2[1].step(1)
        trade_act(1, 0)
        ffn_c(0)
        ffn_out(0)
        ag2[1].step(2)
        ag2[1].step(3)
        ffn_a(1)
        ffn_b(1)
        rs3[0].step(0)
        trade_act(0, 1)
        ffn_c(1)
        grads_down(0)
        rs3[0].step(1)
        push(0)
        trade_act(1, 1)
        offer()
        rs3[0].step(2)
        trade_one()
        grads_down(1)
        pass_y(0)
        rs3[1].step(0)
        sum_three(0)
        grads_up(0)
        push(2)
        rs3[1].step(1)
        rs3[1].step(2)
        grads_up(1)
        push(1)
        pass_x(0)
        pass_y(1)
        ag4[0].step(1)
        ffn_out(1)
        sum_three(1)
        rs2[1].start()
        pass_x(1)
        offer_two()
        push(3)
        ag4[0].step(2)
        pass_y(2)
        ag4[0].step(3)
        grad_attended(0)
        load_g1.start()
        rs2[0].start()
        ag4[1].step(1)
        attention_back(0)
        rs2[1].step(0)
        ag4[1].step(2)
        keys_back(0)
        ag4[1].step(3)
        trade_three()
        grad_attended(1)
        attention_back(1)
        grads_out()
        trade_four()
        keys_back(1)
        rs2[1].step(1)
        trade_two()
        pass_y(3)
        keys_sum(0)
        rs2[1].step(2)
        rs2[0].step(0)
        back_c(0)
        rs2[0].step(1)
        rs2[0].step(2)
        pass_x(2)
        grads_q()
        push(5)
        rs4[0].step(0)
        pass_x(3)
        keys_sum(1)
        push(4)
        trade_five()
        rs4[0].step(1)
        back_c(1)
        grads_kv()
        push(6)
        sum_two(1)
        pass_x(4)
        rs4[1].step(0)
        norms_at(0)
        pass_y(4)
        rs4[0].step(2)
        pass_x(5)
        pass_x(6)
        rs4[1].step(1)
        pass_y(6)
        rs4[1].step(2)
        sum_two(0)
        sum_four(0)
        norms_at(1)
        pass_y(5)
        sum_four(1)
        norms_at(2)
        norms_at(3)
        the_end()

    return kernel, w_lanes


def layer(z, tokens, out_grad, lengths, self_flags, episode_weight, g1, b1, g2, b2, w_qkv, w_out, w_up, w_down):
    S, R, D, LW, F, T, SEQ, H = z.S, z.R, z.D, z.LW, z.F, z.T, z.SEQ, z.H
    RT, PD = R * T, D // 8
    kernel, w_lanes = make_kernel(z)
    sds = jax.ShapeDtypeStruct
    any_, vmem, smem = (pl.BlockSpec(memory_space=m) for m in (pl.ANY, pltpu.VMEM, pltpu.SMEM))
    extra = (lambda *s: sds(s, bf16)) if not z.pairs else (lambda *s: sds((16, 128), bf16))
    pairs = (lambda *s: sds(s, bf16)) if z.pairs else (lambda *s: sds((16, 128), bf16))
    out_shape = [
        sds((R, S, D), bf16),
        sds((R, S, D), f32),
        sds((16, D // 4), f32),
        pairs(PD, w_lanes),
        pairs(PD, w_lanes),
        pairs(PD, w_lanes),
        pairs(3, PD, w_lanes),
        pairs(PD, w_lanes),
        pairs(PD, w_lanes),
        sds((R, RT, D), bf16),
        sds((RT, D), bf16),
        extra(RT, D),
        extra(RT, D),
        extra(RT, D),
        extra(RT, F),
        extra(RT, F),
        extra(RT, 3 * LW),
        extra(RT, LW),
    ]
    dma = pltpu.SemaphoreType.DMA
    reg = pltpu.SemaphoreType.REGULAR
    v = lambda *s: pltpu.VMEM(s, bf16)
    vf = lambda *s: pltpu.VMEM(s, f32)
    scratch = [
        v(D + F, D), v(RT, F), v(RT, D // 2), v(D, 3 * LW), v(LW, D), v(RT, D), v(RT, D), v(RT, D),
        v(RT, LW), v(R, SEQ, 2 * LW), v(RT, F), v(RT, F), v(RT, 3 * LW), v(RT, LW),
        v(RT, D), v(RT, D), v(R, 5, S, D), v(R, 5, S, D),
        vf(R, S, D), v(T, SEQ), v(2, PD, max(F, D) // 2), vf(3, 4, 16, D // 4), vf(S, D),
        dma((4, R, 6)), dma((4, R, 4)), dma((4, R, 6)), dma((4, R, 6)),
        dma((R, 3)), dma((R, 4)), dma((R, 3)), dma((R, 3)),
        dma((26,)), dma((26,)), dma((7, 6)), dma((7, 6)), dma((3, 3)), dma((3, 3)),
        dma((6,)), dma((3,)), dma((2,)), dma((4,)), reg, reg, reg,
    ]
    return pl.pallas_call(
        kernel,
        out_shape=out_shape,
        in_specs=[vmem] * 2 + [smem] * 3 + [vmem] * 4 + [any_] * 4,
        out_specs=[vmem] * 3 + [any_] * 15,
        scratch_shapes=scratch,
        compiler_params=pltpu.CompilerParams(
            collective_id=0, has_side_effects=True, vmem_limit_bytes=64 * 2**20 - 2**16
        ),
        cost_estimate=pl.CostEstimate(flops=42 * 10**9, bytes_accessed=10**8, transcendentals=10**7),
    )(tokens, out_grad, lengths, self_flags, episode_weight, g1, b1, g2, b2, w_qkv, w_out, w_up, w_down)


def last_step(z, y, gin, norms, ro, rx, ry):
    S, R, D, LW, F, PD = z.S, z.R, z.D, z.LW, z.F, z.D // 8
    steps = 4
    wide, slim = F // steps, LW // steps
    offsets = [(wide, 0), (wide, steps)]
    base = 2 * F // slim
    offsets += [(slim, base + k * steps) for k in range(4)]

    def kernel(*refs):
        y_in, gin_in, norms_in = refs[:3]
        parts = refs[3:21]
        out, gout, qkv, proj, up, down, one, two = refs[21:]

        def total(k):
            return parts[k][...].astype(f32) + parts[6 + k][...].astype(f32) + parts[12 + k][...].astype(f32)

        down[...] = total(0).T
        up[...] = total(1)
        proj[...] = total(2).T
        for j in range(3):
            qkv[j] = total(3 + j)
        for r in range(R):
            gout[:, r, :] = gin_in[r]
        out[...] = jnp.stack([y_in[r].astype(f32) for r in range(R)], axis=1).astype(bf16)
        for k, ref in enumerate((one, two)):
            for i in range(8):
                ref[i // 4 : i // 4 + 1, (i % 4) * (D // 4) : (i % 4 + 1) * (D // 4)] = norms_in[k * 8 + i : k * 8 + i + 1, :]

    spec = pl.BlockSpec
    rows = spec((R, S // steps, D), lambda i: (0, i, 0))
    in_specs = [rows, rows, spec((16, D // 4), lambda i: (0, 0))]
    for _ in range(3):
        in_specs += [spec((PD, w), lambda i, o=o: (0, o + i)) for w, o in offsets]
    sds = jax.ShapeDtypeStruct
    return pl.pallas_call(
        kernel,
        grid=(steps,),
        out_shape=[
            sds((S, R, D), bf16), sds((S, R, D), f32), sds((3, PD, LW), f32), sds((LW, PD), f32), sds((PD, F), f32),
            sds((F, PD), f32), sds((2, D), f32), sds((2, D), f32),
        ],
        in_specs=in_specs,
        out_specs=[
            spec((S // steps, R, D), lambda i: (i, 0, 0)), spec((S // steps, R, D), lambda i: (i, 0, 0)),
            spec((3, PD, slim), lambda i: (0, 0, i)), spec((slim, PD), lambda i: (i, 0)),
            spec((PD, wide), lambda i: (0, i)), spec((wide, PD), lambda i: (i, 0)), spec((2, D), lambda i: (0, 0)),
            spec((2, D), lambda i: (0, 0)),
        ],
        compiler_params=pltpu.CompilerParams(vmem_limit_bytes=64 * 2**20 - 2**16),
    )(y, gin, norms, *([ro] * 6 + [rx] * 6 + [ry] * 6))


def solution(mesh):
    shape = dict(mesh.shape)

    def on_device(
        tokens, lengths, self_flags, episode_weight, ln1_gain, ln1_bias, w_qkv, w_out, ln2_gain, ln2_bias, w_up,
        w_down, out_grad,
    ):
        z = Sizes(shape, tokens.shape, w_qkv.shape, w_up.shape, lengths.shape)
        row = lambda a: a.reshape(1, -1)
        results = layer(
            z, tokens, out_grad, lengths, self_flags, episode_weight, row(ln1_gain), row(ln1_bias), row(ln2_gain),
            row(ln2_bias), jnp.transpose(w_qkv, (1, 0, 2)), w_out, w_up, w_down,
        )
        y, gin, norms, ro, rx, ry = results[:6]
        if z.pairs:
            output, grad_input, qkv, grad_out, grad_up, grad_down, one, two = last_step(z, y, gin, norms, ro, rx, ry)
            return output, grad_input, jnp.transpose(qkv, (1, 0, 2)), grad_out, grad_up, grad_down, one, two
        output = jnp.transpose(y, (1, 0, 2))
        grad_input = jnp.transpose(gin, (1, 0, 2))
        g1_all, g2_all, gy_all, gm_all, act, gpre, gproj, att = results[10:]

        def over_tokens(a, b, dim):
            value = jnp.einsum("ta,tb->ab", a, b, preferred_element_type=f32).astype(bf16)
            return lax.psum_scatter(value, ("dp", "sp"), scatter_dimension=dim, tiled=True).astype(f32)

        grad_down = over_tokens(act, gy_all, 1)
        grad_up = over_tokens(g2_all, gpre, 0)
        grad_out = over_tokens(att, gm_all, 1)
        grad_qkv = over_tokens(g1_all, gproj, 0).reshape(-1, 3, z.LW)
        both = lax.psum(norms, ("dp", "sp", "tp"))
        both = both.reshape(2, 2, -1)
        return output, grad_input, grad_qkv, grad_out, grad_up, grad_down, both[0], both[1]

    return jax.shard_map(
        on_device,
        mesh=mesh,
        in_specs=(
            P(("sp", "tp"), "dp", None), P("dp", None), P("dp", None), P("dp", None), P(), P(), P(None, None, "tp"),
            P("tp", None), P(), P(), P(None, "tp"), P("tp", None), P(("sp", "tp"), "dp", None),
        ),
        out_specs=(
            P(("sp", "tp"), "dp", None), P(("sp", "tp"), "dp", None), P(("dp", "sp"), None, "tp"),
            P("tp", ("dp", "sp")), P(("dp", "sp"), "tp"), P("tp", ("dp", "sp")), P(), P(),
        ),
        check_vma=False,
    )
```

```python
import jax
import jax.numpy as jnp
from jax import lax
from jax.experimental import pallas as pl
from jax.experimental.pallas import tpu as pltpu
from jax.sharding import PartitionSpec as P

DH = 128
EPSILON = 1e-05
NEG = -1e30
f32 = jnp.float32
bf16 = jnp.bfloat16
MESH = pl.DeviceIdType.MESH


def dot(a, b, ca, cb):
    return lax.dot_general(a, b, (((ca,), (cb,)), ((), ())), preferred_element_type=f32)


def lanes(start, size):
    if isinstance(start, int):
        return pl.ds(start, size)
    return pl.ds(pl.multiple_of(start, 128), size)


def rows_at(start, size):
    if isinstance(start, int):
        return pl.ds(start, size)
    return pl.ds(pl.multiple_of(start, 64), size)


def norm_parts(values):
    average = jnp.mean(values, axis=-1, keepdims=True)
    centred = values - average
    variance = jnp.mean(centred * centred, axis=-1, keepdims=True)
    inverse = lax.rsqrt(variance + EPSILON)
    return centred * inverse, inverse


def norm_back(unit, inverse, gain, grad):
    scaled = grad * gain
    first = jnp.mean(scaled, axis=-1, keepdims=True)
    second = jnp.mean(scaled * unit, axis=-1, keepdims=True)
    return inverse * (scaled - first - unit * second)


class Sizes:
    def __init__(self, mesh_shape, tokens, w_qkv, w_up, lengths):
        self.n_dp = mesh_shape["dp"]
        self.n_sp = mesh_shape["sp"]
        self.n_tp = mesh_shape["tp"]
        self.S = tokens[0]
        self.R = tokens[1]
        self.D = tokens[2]
        self.LW = w_qkv[2]
        self.F = w_up[1]
        self.E = lengths[1]
        self.T = self.S * self.n_tp
        self.SEQ = self.T * self.n_sp
        self.H = self.LW // DH
        self.pairs = self.n_dp == 2 and self.n_sp == 4


def wgrad_kinds(z):
    half = z.F // 2
    out, offset = {}, 0
    for name, n, along in (
        ("d0", half, 5), ("d1", half, 5), ("u0", half, 6), ("u1", half, 6), ("out", z.LW, 6), ("q", z.LW, 4),
        ("kv", 2 * z.LW, 5),
    ):
        out[name] = (n, offset, n * along // 8)
        offset += n
    return out, offset


def make_kernel(z):
    S, R, D, LW, F, T, SEQ, H = z.S, z.R, z.D, z.LW, z.F, z.T, z.SEQ, z.H
    RT = R * T
    kinds, w_lanes = wgrad_kinds(z)
    scale = DH ** (-0.5)
    PD = D // 8

    def kernel(
        tok, og, lens, flags, eweight, g1, b1, g2, b2, wqkv_hbm, wout_hbm, wup_hbm, wdn_hbm,
        y_out, gin, norms, ro, rx, ry, sw, tx, ty, ph, g1h, extra_g2, extra_gy, extra_gm, extra_act, extra_gpre,
        extra_gproj, extra_att,
        arena, xact, xgy, wqkv, wout, ga, g2b, gyb, q, kv, act, gpre, gproj, att, part, part2, slots, slots2,
        mid, ds, stage, nr, total,
        ag_s, ag_r, rs_s, rs_r, kv_s, kv_r, dk_s, dk_r, x_s, x_r, w_s, w_r, n_s, n_r, loc, raw_sem, stg_sem,
        rt_sem, free_x, free_c, free_y,
    ):
        dp = lax.axis_index("dp")
        sp = lax.axis_index("sp")
        tp = lax.axis_index("tp")
        par = lax.rem(sp, 2)
        yy = lax.div(sp, 2)
        mate = sp + 1 - 2 * par
        far = lax.rem(sp + 2, 4)
        odp = 1 - dp
        kv_row = sp * T
        own = tp * S

        def remote(src, dst, ssem, rsem, device):
            return pltpu.make_async_remote_copy(
                src_ref=src, dst_ref=dst, send_sem=ssem, recv_sem=rsem, device_id=device, device_id_type=MESH
            )

        HS = S // 2

        class Gather:
            def __init__(self, buf, i, r):
                self.buf, self.i, self.r = buf, i, r

            def copy(self, shard, way, hop, h):
                sl = self.buf.at[pl.ds(pl.multiple_of(self.r * T + shard * S + h * HS, HS), HS), :]
                to = tp + 1 if way == 0 else tp - 1
                return remote(
                    sl,
                    sl,
                    ag_s.at[self.i, self.r, way * 3 + hop, h],
                    ag_r.at[self.i, self.r, shard, h],
                    (dp, sp, to),
                )

            def start(self):
                for h in range(2):

                    @pl.when(tp < 3)
                    def _(h=h):
                        self.copy(tp, 0, 0, h).start()

                    @pl.when(tp > 0)
                    def _(h=h):
                        self.copy(tp, 1, 0, h).start()

            def step(self, hop):
                for h in range(2):

                    @pl.when(tp >= hop)
                    def _(h=h):
                        self.copy(tp - hop, 0, 0, h).wait_recv()

                    if hop < 3:

                        @pl.when((tp >= hop) & (tp < 3))
                        def _(h=h):
                            self.copy(tp - hop, 0, hop, h).start()

                    @pl.when(tp <= 3 - hop)
                    def _(h=h):
                        self.copy(tp + hop, 1, 0, h).wait_recv()

                    if hop < 3:

                        @pl.when((tp <= 3 - hop) & (tp > 0))
                        def _(h=h):
                            self.copy(tp + hop, 1, hop, h).start()

            def drain(self):
                for hop in range(3):

                    @pl.when((tp >= hop) & (tp < 3))
                    def _(hop=hop):
                        for h in range(2):
                            self.copy(tp - hop, 0, hop, h).wait_send()

                    @pl.when((tp <= 3 - hop) & (tp > 0))
                    def _(hop=hop):
                        for h in range(2):
                            self.copy(tp + hop, 1, hop, h).wait_send()

        class Scatter:
            def __init__(self, buf, box, i, r):
                self.buf, self.box, self.i, self.r = buf, box, i, r

            def place(self, way, k, h):
                o = 3 - k if way == 0 else k
                return pl.ds(self.r * T + o * S + h * HS, HS)

            def slot(self, way, k):
                return k if way == 0 else 4 - k

            def copy(self, way, k, h):
                to = tp + 1 if way == 0 else tp - 1
                n = way * 3 + k
                return remote(
                    self.buf.at[self.place(way, k, h), :],
                    self.box.at[self.r, self.slot(way, k), pl.ds(h * HS, HS), :],
                    rs_s.at[self.i, self.r, n, h],
                    rs_r.at[self.i, self.r, n, h],
                    (dp, sp, to),
                )

            def start(self):
                for k in range(3):

                    @pl.when(tp == 0)
                    def _(k=k):
                        for h in range(2):
                            self.copy(0, k, h).start()

                    @pl.when(tp == 3)
                    def _(k=k):
                        for h in range(2):
                            self.copy(1, k, h).start()

            def relay(self, way, k):
                for h in range(2):
                    sl = self.place(way, k, h)
                    self.copy(way, k, h).wait_recv()
                    self.buf[sl, :] = (
                        self.buf[sl, :].astype(f32)
                        + self.box[self.r, self.slot(way, k), h * HS : (h + 1) * HS].astype(f32)
                    ).astype(bf16)
                    self.copy(way, k, h).start()

            def step(self, k):
                first, second, n = (0, 1, k) if k < 2 else (1, 0, 0)

                @pl.when(tp == 1)
                def _():
                    self.relay(first, n)

                @pl.when(tp == 2)
                def _():
                    self.relay(second, n)

            def finish(self):
                total[...] = self.buf[rows_at(self.r * T + own, S), :].astype(f32)
                for way in range(2):
                    for k in range(3):

                        @pl.when(tp == (3 - k if way == 0 else k))
                        def _(way=way, k=k):
                            for h in range(2):
                                self.copy(way, k, h).wait_recv()
                            total[...] += self.box[self.r, self.slot(way, k)].astype(f32)

            def drain(self):
                for k in range(3):

                    @pl.when(tp < 3 - k)
                    def _(k=k):
                        for h in range(2):
                            self.copy(0, k, h).wait_send()

                    @pl.when(tp > k)
                    def _(k=k):
                        for h in range(2):
                            self.copy(1, k, h).wait_send()

        class Keys:
            def __init__(self, r):
                self.r = r

            def copy(self, block, to, n):
                sl = kv.at[self.r, rows_at(block * T, T), :]
                return remote(sl, sl, kv_s.at[self.r, n], kv_r.at[self.r, block], (dp, to, tp))

            def start(self):
                @pl.when(sp < 2)
                def _():
                    self.copy(sp, sp + 2, 0).start()

                @pl.when(par == 0)
                def _():
                    self.copy(sp, sp + 1, 1).start()

            def step(self):
                for me, block, to in ((2, 0, 3), (3, 1, 2)):

                    @pl.when(sp == me)
                    def _(block=block, to=to):
                        self.copy(block, to, 0).wait_recv()
                        self.copy(block, to, 2).start()

            def finish(self):
                for me, block in ((1, 0), (2, 1), (3, 0), (3, 2)):

                    @pl.when(sp == me)
                    def _(block=block):
                        self.copy(block, 0, 0).wait_recv()

            def drain(self):
                @pl.when(sp < 2)
                def _():
                    self.copy(sp, sp + 2, 0).wait_send()

                @pl.when(par == 0)
                def _():
                    self.copy(sp, sp + 1, 1).wait_send()

                for me, block, to in ((2, 0, 3), (3, 1, 2)):

                    @pl.when(sp == me)
                    def _(block=block, to=to):
                        self.copy(block, to, 2).wait_send()

        KW = 2 * LW
        DK0 = 5 * RT
        DR0 = RT

        class KeyGrads:
            def __init__(self, r):
                self.r = r

            def src(self, block):
                return arena.at[pl.ds(DK0 + block * T, T), pl.ds(self.r * KW, KW)]

            def dst(self, box):
                return arena.at[pl.ds(DR0 + box * T, T), pl.ds(self.r * KW, KW)]

            def copy(self, block, to, box, n):
                return remote(
                    self.src(block), self.dst(box), dk_s.at[self.r, n], dk_r.at[self.r, box], (dp, to, tp)
                )

            def start(self):
                for me, block, to, box, n in ((3, 0, 2, 0, 0), (3, 2, 2, 1, 1), (2, 1, 3, 0, 0), (1, 0, 0, 1, 0)):

                    @pl.when(sp == me)
                    def _(block=block, to=to, box=box, n=n):
                        self.copy(block, to, box, n).start()

            def step(self):
                for me, block, to in ((2, 0, 0), (3, 1, 1)):

                    @pl.when(sp == me)
                    def _(block=block, to=to):
                        self.copy(block, to, 0, 2).wait_recv()
                        mine = pl.ds(DK0 + block * T, T)
                        col = pl.ds(self.r * KW, KW)
                        arena[mine, col] = (
                            arena[mine, col].astype(f32) + arena[pl.ds(DR0, T), col].astype(f32)
                        ).astype(bf16)
                        self.copy(block, to, 2, 2).start()

            def finish(self):
                col = pl.ds(self.r * KW, KW)
                there = pl.ds(self.r * T, T)
                to = pl.ds(LW, KW)
                for me, boxes in ((0, (1, 2)), (1, (2,)), (2, (1,)), (3, ())):

                    @pl.when(sp == me)
                    def _(me=me, boxes=boxes):
                        value = arena[pl.ds(DK0 + me * T, T), col].astype(f32)
                        for box in boxes:
                            self.copy(0, 0, box, 0).wait_recv()
                            value += arena[pl.ds(DR0 + box * T, T), col].astype(f32)
                        gproj[there, to] = value.astype(bf16)

            def drain(self):
                for me, block, to, box, n in (
                    (3, 0, 2, 0, 0), (3, 2, 2, 1, 1), (2, 1, 3, 0, 0), (1, 0, 0, 1, 0), (2, 0, 0, 2, 2), (3, 1, 1, 2, 2),
                ):

                    @pl.when(sp == me)
                    def _(block=block, to=to, box=box, n=n):
                        self.copy(block, to, box, n).wait_send()

        ends = []
        for r in range(R):
            run, row = 0, []
            for e in range(z.E):
                run = run + lens[r, e]
                row.append(run)
            ends.append(row)

        def first_norm(r):
            unit, _ = norm_parts(tok[:, r, :].astype(f32))
            ga[rows_at(r * T + own, S), :] = (unit * g1[...] + b1[...]).astype(bf16)

        def weighted_grad(r):
            place = sp * T + own + lax.broadcasted_iota(jnp.int32, (S, 1), 0)
            factor = jnp.full((S, 1), eweight[r, 0] * (1.0 + flags[r, 0].astype(f32)), f32)
            for e in range(1, z.E):
                factor = jnp.where(
                    place >= ends[r][e - 1], eweight[r, e] * (1.0 + flags[r, e].astype(f32)), factor
                )
            return og[:, r, :].astype(f32) * factor

        def project(r, j):
            value = dot(ga[r * T : (r + 1) * T, :], wqkv[:, j * LW : (j + 1) * LW], 1, 0).astype(bf16)
            if j == 0:
                q[r * T : (r + 1) * T, :] = value
            else:
                kv[r, rows_at(kv_row, T), (j - 1) * LW : j * LW] = value

        def mask(r):
            here = kv_row + lax.broadcasted_iota(jnp.int32, (T, 1), 0)
            begin = jnp.zeros((T, 1), jnp.int32)
            for e in range(z.E):
                begin = jnp.where(here >= ends[r][e], jnp.maximum(begin, ends[r][e]), begin)
            there = lax.broadcasted_iota(jnp.int32, (T, SEQ), 1)
            ds[...] = jnp.where((there <= here) & (there >= begin), 0.0, NEG).astype(bf16)

        half = T // 2
        ppl = D // SEQ
        keep = [act, gpre]

        def attend(r):
            def one(i, carry):
                rs = rows_at(i * half, half)
                qs = rows_at(r * T + i * half, half)
                for h in range(H):
                    hs = slice(h * DH, (h + 1) * DH)
                    s = dot(q[qs, hs], kv[r, :, hs], 1, 1) * scale + ds[rs, :].astype(f32)
                    peak = jnp.max(s, axis=1, keepdims=True)
                    e = jnp.exp(s - peak)
                    p = (e * (1.0 / jnp.sum(e, axis=1, keepdims=True))).astype(bf16)
                    keep[r][rows_at((h // ppl) * T + i * half, half), (h % ppl) * SEQ : (h % ppl + 1) * SEQ] = p
                    att[qs, hs] = dot(p, kv[r, :, LW + h * DH : LW + (h + 1) * DH], 1, 0).astype(bf16)
                return carry

            lax.fori_loop(0, 2, one, 0)

        def times(lhs, r, weight, out, transposed):
            width = 512
            n = out.shape[1] // width

            def one(j, carry):
                cs = lanes(j * width, width)
                w = weight(j, width)
                out[r * T : (r + 1) * T, cs] = dot(lhs, w, 1, 1 if transposed else 0).astype(bf16)
                return carry

            lax.fori_loop(0, n, one, 0)

        def project_out(r):
            def one(j, carry):
                cs = lanes(j * 512, 512)
                part[r * T : (r + 1) * T, cs] = dot(att[r * T : (r + 1) * T, :], wout[:, cs], 1, 0).astype(bf16)
                return carry

            lax.fori_loop(0, D // 512, one, 0)

        def ffn_up(r, low, high):
            rs = slice(r * T, (r + 1) * T)

            def one(j, carry):
                cs = lanes(j * 256, 256)
                pre = dot(g2b[rs, :], arena[0:D, cs], 1, 0)
                e = 0.5 * (1.0 + lax.erf(pre * 0.7071067811865476))
                act[rs, cs] = (pre * e).astype(bf16)
                gpre[rs, cs] = (e + pre * (jnp.exp(-0.5 * pre * pre) * 0.3989422804014327)).astype(bf16)
                return carry

            lax.fori_loop(low, high, one, 0)

        def ffn_slope(r, low, high):
            rs = slice(r * T, (r + 1) * T)

            def one(j, carry):
                cs = lanes(j * 256, 256)
                back = dot(gyb[rs, :], arena[rows_at(D + j * 256, 256), :], 1, 1)
                gpre[rs, cs] = (back * gpre[rs, cs].astype(f32)).astype(bf16)
                return carry

            lax.fori_loop(low, high, one, 0)

        def ffn_back(r):
            rs = slice(r * T, (r + 1) * T)

            def one(j, carry):
                part[rs, lanes(j * 512, 512)] = dot(gpre[rs, :], arena[rows_at(j * 512, 512), :], 1, 1).astype(bf16)
                return carry

            lax.fori_loop(0, D // 512, one, 0)

        def ffn_out(r):
            rs = slice(r * T, (r + 1) * T)

            def one(j, carry):
                cs = lanes(j * 512, 512)
                part2[rs, cs] = dot(act[rs, :], arena[D : D + F, cs], 1, 0).astype(bf16)
                return carry

            lax.fori_loop(0, D // 512, one, 0)

        def second_norm(r):
            value = tok[:, r, :].astype(f32) + total[...]
            mid[r] = value
            unit, _ = norm_parts(value)
            g2b[rows_at(r * T + own, S), :] = (unit * g2[...] + b2[...]).astype(bf16)

        def add_norms(grad, unit):
            sums = (jnp.sum(grad * unit, axis=0, keepdims=True), jnp.sum(grad, axis=0, keepdims=True))
            for i in range(8):
                piece = sums[i // 4][:, (i % 4) * (D // 4) : (i % 4 + 1) * (D // 4)]
                nr[0, pl.ds(tp, 1), 8 + i : 9 + i, :] += piece[None]

        def second_norm_back(r):
            unit, inverse = norm_parts(mid[r])
            grad = total[...]
            add_norms(grad, unit)
            value = weighted_grad(r) + norm_back(unit, inverse, g2[...], grad)
            gin[r] = value
            ga[rows_at(r * T + own, S), :] = value.astype(bf16)

        def first_norm_back(r):
            unit, inverse = norm_parts(tok[:, r, :].astype(f32))
            grad = total[...]
            gin[r] = gin[r] + norm_back(unit, inverse, g1[...], grad)

        def attend_back(r):
            rows = slice(r * T, (r + 1) * T)

            def one(h, carry):
                hs, vs = lanes(h * DH, DH), lanes(LW + h * DH, DH)
                top = lax.div(h, ppl) * T
                pc = lanes(lax.rem(h, ppl) * SEQ, SEQ)
                for t in range(2):
                    gp = dot(gproj[r * T + t * half : r * T + (t + 1) * half, hs], kv[r, :, vs], 1, 1)
                    p = keep[r][rows_at(top + t * half, half), pc].astype(f32)
                    x = p * gp
                    delta = jnp.sum(x, axis=1, keepdims=True)
                    ds[t * half : (t + 1) * half, :] = ((x - p * delta) * scale).astype(bf16)
                arena[DK0 : DK0 + SEQ, lanes(r * KW + h * DH, DH)] = dot(ds[...], q[rows, hs], 0, 0).astype(bf16)
                arena[DK0 : DK0 + SEQ, lanes(r * KW + LW + h * DH, DH)] = dot(
                    keep[r][rows_at(top, T), pc], gproj[rows, hs], 0, 0
                ).astype(bf16)
                gproj[rows, hs] = dot(ds[...], kv[r, :, hs], 1, 0).astype(bf16)
                return carry

            lax.fori_loop(0, H, one, 0)

        def grad_attended(r):
            rows = slice(r * T, (r + 1) * T)
            gproj[rows, 0:LW] = dot(ga[rows, :], wout[...], 1, 1).astype(bf16)

        def qkv_back(r):
            rs = slice(r * T, (r + 1) * T)
            ns = slice(7 * RT + r * T, 7 * RT + (r + 1) * T)
            width = D // 4

            def one(j, carry):
                cs = lanes(j * width, width)
                value = dot(gproj[rs, :], wqkv[rows_at(j * width, width), :], 1, 1)
                part[rs, cs] = value.astype(bf16)
                normed = arena[ns, cs].astype(f32)
                nr[0, pl.ds(tp, 1), pl.ds(j, 1), :] += jnp.sum(value * normed, axis=0, keepdims=True)[None]
                nr[0, pl.ds(tp, 1), pl.ds(4 + j, 1), :] += jnp.sum(value, axis=0, keepdims=True)[None]
                return carry

            lax.fori_loop(0, 4, one, 0)

        load_out = pltpu.make_async_copy(wout_hbm, wout, loc.at[0])
        load_qkv = [
            pltpu.make_async_copy(wqkv_hbm.at[j], wqkv.at[:, pl.ds(j * LW, LW)], raw_sem.at[j]) for j in range(3)
        ]
        load_up = pltpu.make_async_copy(wup_hbm, arena.at[pl.ds(0, D), :], loc.at[1])
        load_down = pltpu.make_async_copy(wdn_hbm, arena.at[pl.ds(D, F), :], loc.at[2])
        save_p = [pltpu.make_async_copy(keep[r], ph.at[r], loc.at[3 + r]) for r in range(R)]
        load_p = [pltpu.make_async_copy(ph.at[r], keep[r], loc.at[3 + r]) for r in range(R)]
        save_g1 = pltpu.make_async_copy(ga, g1h, loc.at[5])
        load_g1 = pltpu.make_async_copy(g1h, arena.at[pl.ds(7 * RT, RT), :], loc.at[5])

        XP, XG, XH, XJ = RT, 2 * RT, 3 * RT, 4 * RT
        there = (dp, mate, tp)
        oth = 1 - par

        def halves(buf, buf_row, size, box, box_row, box_lane, n):
            return [
                remote(
                    buf.at[pl.ds(buf_row, size), lanes(b * 2 * PD + oth * PD, PD)],
                    box.at[pl.ds(box_row, size), pl.ds(box_lane + b * PD, PD)],
                    x_s.at[n + b],
                    x_r.at[n + b],
                    there,
                )
                for b in range(4)
            ]

        def piece(buf, row, size, lane, width, box, box_row, box_lane, n):
            return [
                remote(
                    buf.at[pl.ds(row, size), pl.ds(lane, width)],
                    box.at[pl.ds(box_row, size), pl.ds(box_lane, width)],
                    x_s.at[n],
                    x_r.at[n],
                    there,
                )
            ]

        trade_rows = [[piece(act, r * T, T, h * F // 2, F // 2, xact, r * T, h * F // 2, 2 * h + r) for r in range(R)] for h in range(2)]
        trade_gy = [halves(gyb, r * T, T, xgy, r * T, 0, 22 + 4 * r) for r in range(R)]
        trade_up = piece(gpre, 0, RT, 0, F, arena, XP, 0, 21) + halves(g2b, 0, RT, arena, XG, 0, 6)
        trade_g1 = halves(arena, 7 * RT, RT, arena, XH, 0, 10)
        trade_out = piece(att, 0, RT, 0, LW, arena, XJ, 3 * LW, 18) + halves(ga, 0, RT, arena, XH, D // 2, 14)
        trade_q = piece(gproj, 0, RT, 0, LW, arena, XJ, 0, 19)
        trade_kv = piece(gproj, 0, RT, LW, 2 * LW, arena, XJ, LW, 20)

        names = list(kinds)
        operands = {
            "d0": ((gyb, 0), (act, 0), (xgy, 0, 0), (xact, 0, 0)),
            "d1": ((gyb, 0), (act, F // 2), (xgy, 0, 0), (xact, 0, F // 2)),
            "u0": ((g2b, 0), (gpre, 0), (arena, XG, 0), (arena, XP, 0)),
            "u1": ((g2b, 0), (gpre, F // 2), (arena, XG, 0), (arena, XP, F // 2)),
            "out": ((ga, 0), (att, 0), (arena, XH, D // 2), (arena, XJ, 3 * LW)),
            "q": ((arena, 7 * RT), (gproj, 0), (arena, XH, 0), (arena, XJ, 0)),
            "kv": ((arena, 7 * RT), (gproj, LW), (arena, XH, 0), (arena, XJ, LW)),
        }

        def tile(t, way, size):
            if way == 0:
                return arena.at[pl.ds(0, PD), pl.ds((t % 2) * (D // 2), size)]
            return arena.at[pl.ds(XG + PD, PD), pl.ds(D // 2 + (t % 2) * (D // 4), size)]

        def w_copy(name, which):
            t = names.index(name)
            n, off, a = kinds[name]
            ca, cb = pl.ds(off, a), pl.ds(off + a, n - a)
            x_to, y_to = (odp, sp, tp), (dp, far, tp)
            src, dst, to = {
                "S2": (sw.at[0, :, ca], tx.at[:, ca], x_to),
                "S4": (sw.at[0, :, cb], ty.at[:, cb], y_to),
                "S1": (sw.at[1, :, ca], rx.at[:, ca], x_to),
                "S3": (sw.at[2, :, cb], ry.at[:, cb], y_to),
                "R1": (tile(t, 0, a), ry.at[:, ca], y_to),
                "R2": (tile(t, 1, n - a), rx.at[:, cb], x_to),
            }[which]
            k = ("S1", "S2", "S3", "S4", "R1", "R2").index(which)
            return remote(src, dst, w_s.at[t, k], w_r.at[t, k], to)

        def weight_grad(name):
            (own_d, own_row), (own_r, own_lane), (mate_d, d_row, d_lane), (mate_r, r_row, r_lane) = operands[name]
            n, off, _ = kinds[name]
            own_r = own_r.at[:, pl.ds(own_lane, n)]
            mate_r = mate_r.at[pl.ds(r_row, RT), pl.ds(r_lane, n)]

            def staged(i, dst):
                slot = lax.rem(i, 2)
                return pltpu.make_async_copy(
                    stage.at[slot, :, pl.ds(0, n)], dst.at[:, pl.ds(off, n)], stg_sem.at[slot]
                )

            def one(i, carry):
                b4 = jnp.where(i < 2, odp, dp) * 2 + jnp.where(lax.rem(i, 2) == 0, 1 - yy, yy)
                value = dot(own_d[own_row : own_row + RT, lanes(b4 * 2 * PD + par * PD, PD)], own_r[...], 0, 0)
                value += dot(mate_d[d_row : d_row + RT, lanes(d_lane + b4 * PD, PD)], mate_r[...], 0, 0)
                stage[lax.rem(i, 2), :, 0:n] = value.astype(bf16)

                @pl.when(i < 3)
                def _():
                    staged(i, sw.at[i]).start()

                @pl.when(i == 3)
                def _():
                    staged(i, ro).start()

                @pl.when(i > 0)
                def _():
                    staged(i - 1, sw.at[i - 1]).wait()

                for k, which in ((1, "S2"), (2, "S1")):

                    @pl.when(i == k)
                    def _(which=which):
                        w_copy(name, which).start()

                return carry

            lax.fori_loop(0, 4, one, 0)
            staged(3, ro).wait()

        def relay_sum(name, way):
            t = names.index(name)
            n, off, a = kinds[name]
            first, size, box, block, need, send = (
                (0, a, tx, 2, "S2", "R1") if way == 0 else (a, n - a, ty, 1, "S4", "R2")
            )
            if t > 1:
                w_copy(names[t - 2], send).wait_send()
            there_l = pl.ds(off + first, size)
            mine, met = tile(t, way, size), arena.at[pl.ds(PD, PD), pl.ds(0, size)]
            own_c = pltpu.make_async_copy(sw.at[block, :, there_l], mine, rt_sem.at[way])
            got_c = pltpu.make_async_copy(box.at[:, there_l], met, rt_sem.at[2 + way])
            own_c.start()
            w_copy(name, need).wait_recv()
            got_c.start()
            own_c.wait()
            got_c.wait()
            mine[...] = (mine[...].astype(f32) + met[...].astype(f32)).astype(bf16)
            w_copy(name, send).start()

        def finish_sums(name):
            for which in ("S1", "S3", "R1", "R2"):
                w_copy(name, which).wait_recv()
            for which in ("S1", "S2", "S3", "S4"):
                w_copy(name, which).wait_send()
            if names.index(name) >= len(names) - 2:
                w_copy(name, "R1").wait_send()
                w_copy(name, "R2").wait_send()

        norm_axes = ((4, tp), (4, sp), (z.n_dp, dp))

        def norm_copies(i):
            axis_n, index = norm_axes[i]
            slot = nr.at[i, pl.ds(index, 1)]
            copies = []
            for d in range(1, axis_n):
                to = lax.rem(index + d, axis_n)
                device = ((dp, sp, to), (dp, to, tp), (to, sp, tp))[i]
                copies.append(remote(slot, slot, n_s.at[i, d - 1], n_r.at[i, d - 1], device))
            return copies

        def norm_result(value):
            norms[4:16, :] = value[4:16, :]
            for i in range(4):
                cs = slice(i * (D // 4), (i + 1) * (D // 4))
                norms[i : i + 1, :] = (value[i : i + 1, :] - b1[:, cs] * value[4 + i : 5 + i, :]) / g1[:, cs]

        def norm_add(i):
            for c in norm_copies(i):
                c.wait_send()
                c.wait_recv()
            value = nr[i, 0]
            for n in range(1, norm_axes[i][0]):
                value = value + nr[i, n]
            return value

        load_out.start()
        for c in load_qkv:
            c.start()
        barrier = pltpu.get_barrier_semaphore()
        greet = [(dp, sp, lax.rem(tp + d, 4)) for d in (1, 2, 3)]
        greet += [(dp, lax.rem(sp + d, 4), tp) for d in (1, 2, 3)]
        if z.pairs:
            greet += [(odp, sp, tp)]
        for device in greet:
            pl.semaphore_signal(barrier, inc=1, device_id=device, device_id_type=MESH)
        first_norm(0)
        pl.semaphore_wait(barrier, len(greet))

        ag1 = [Gather(ga, 0, r) for r in range(R)]
        ag2 = [Gather(g2b, 1, r) for r in range(R)]
        ag3 = [Gather(gyb, 2, r) for r in range(R)]
        ag4 = [Gather(ga, 3, r) for r in range(R)]
        rs1 = [Scatter(part, slots, 0, r) for r in range(R)]
        rs3 = [Scatter(part, slots, 1, r) for r in range(R)]
        rs4 = [Scatter(part, slots, 2, r) for r in range(R)]
        rs2 = [Scatter(part2, slots2, 3, r) for r in range(R)]
        keys = [Keys(r) for r in range(R)]
        kgrads = [KeyGrads(r) for r in range(R)]

        def grad_rows(r):
            gyb[rows_at(r * T + own, S), :] = weighted_grad(r).astype(bf16)

        def clear():
            nr[0, pl.ds(tp, 1)] = jnp.zeros((1,) + nr.shape[2:], f32)
            for b in range(1, 4):

                @pl.when(b > sp)
                def _(b=b):
                    kv[:, b * T : (b + 1) * T, :] = jnp.zeros((R, T, KW), bf16)

        def keys_out(r):
            if r == 0:
                for c in load_qkv:
                    c.wait()
            project(r, 1)
            project(r, 2)
            keys[r].start()

        def queries(r):
            project(r, 0)

        def attention(r):
            attend(r)
            save_p[r].start()
            if r == 0:
                load_out.wait()
            project_out(r)
            rs1[r].start()

        def sum_one(r):
            rs1[r].finish()
            second_norm(r)
            ag2[r].start()

        def before_ffn():
            load_up.wait()
            load_down.wait()
            save_g1.wait()
            for c in save_p:
                c.wait()
            for g in ag1:
                g.drain()

        def up_a(r):
            ffn_up(r, 0, F // 512)

        def up_b(r):
            ffn_up(r, F // 512, F // 256)

        def back_a(r):
            ffn_slope(r, 0, F // 512)

        def back_b(r):
            ffn_slope(r, F // 512, F // 256)

        def ffn_c(r):
            rs1[r].drain()
            ffn_back(r)
            rs3[r].start()

        def sum_three(r):
            rs3[r].finish()
            second_norm_back(r)
            ag4[r].start()

        def sum_two(r):
            rs2[r].finish()
            y_out[r] = (mid[r] + total[...]).astype(bf16)

        def sum_four(r):
            rs4[r].finish()
            first_norm_back(r)

        def offer():
            if z.pairs:
                pl.semaphore_signal(free_x, inc=1, device_id=there, device_id_type=MESH)

        def trade_act(h, r):
            if z.pairs:
                for c in trade_rows[h][r]:
                    c.start()

        def trade_grad(r):
            if z.pairs:
                for c in trade_gy[r]:
                    c.start()

        def trade_one():
            if z.pairs:
                pl.semaphore_wait(free_x, 1)
                for c in trade_up:
                    c.start()

        def grads_down(h):
            if z.pairs:
                for c in trade_rows[h][0] + trade_rows[h][1] + (trade_gy[0] + trade_gy[1] if h == 0 else []):
                    c.wait_recv()
                weight_grad(names[h])

        def grads_up(h):
            if z.pairs:
                if h == 0:
                    for c in trade_up:
                        c.wait_recv()
                weight_grad(names[2 + h])

        def offer_two():
            if z.pairs:
                for c in trade_rows[0][0] + trade_rows[0][1] + trade_rows[1][0] + trade_rows[1][1] + trade_gy[0] + trade_gy[1] + trade_up:
                    c.wait_send()
            else:
                dumps = [
                    pltpu.make_async_copy(act, extra_act, stg_sem.at[0]),
                    pltpu.make_async_copy(gpre, extra_gpre, stg_sem.at[1]),
                    pltpu.make_async_copy(g2b, extra_g2, rt_sem.at[0]),
                    pltpu.make_async_copy(gyb, extra_gy, rt_sem.at[1]),
                ]
                for c in dumps:
                    c.start()
                for c in dumps:
                    c.wait()
            pl.semaphore_signal(free_c, inc=1, device_id=there, device_id_type=MESH)
            pl.semaphore_signal(free_y, inc=1, device_id=(dp, far, tp), device_id_type=MESH)
            for c in load_p:
                c.start()

        def trade_two():
            load_g1.wait()
            if z.pairs:
                for c in trade_g1:
                    c.start()

        def attention_back(r):
            load_p[r].wait()
            attend_back(r)
            if r == 0:
                pl.semaphore_wait(free_c, 1)
            kgrads[r].start()

        def keys_back(r):
            if r == 0:
                pl.semaphore_wait(free_y, 1)
            kgrads[r].step()

        def keys_sum(r):
            kgrads[r].finish()

        def trade_three():
            if z.pairs:
                for c in trade_out:
                    c.start()

        def grads_out():
            if z.pairs:
                for c in trade_out:
                    c.wait_recv()
                weight_grad("out")

        def trade_four():
            if z.pairs:
                for c in trade_q:
                    c.start()

        def trade_five():
            if z.pairs:
                for c in trade_kv:
                    c.start()

        def grads_q():
            if z.pairs:
                for c in trade_g1 + trade_q:
                    c.wait_recv()
                weight_grad("q")

        def grads_kv():
            if z.pairs:
                for c in trade_kv:
                    c.wait_recv()
                weight_grad("kv")

        def push(i):
            if z.pairs:
                w_copy(names[i], "S4").start()
                w_copy(names[i], "S3").start()

        def pass_y(i):
            if z.pairs:
                relay_sum(names[i], 0)

        def pass_x(i):
            if z.pairs:
                relay_sum(names[i], 1)

        def back_c(r):
            rs3[r].drain()
            qkv_back(r)
            rs4[r].start()

        def norms_at(i):
            if not z.pairs:
                if i == 3:
                    norm_result(nr[0, pl.ds(tp, 1)][0])
                return
            if i:
                value = norm_add(i - 1)
                if i == 3:
                    norm_result(value)
                    return
                nr[i, pl.ds((sp, dp)[i - 1], 1)] = value[None]
            for c in norm_copies(i):
                c.start()

        def the_end():
            if z.pairs:
                for name in names:
                    finish_sums(name)
                for c in trade_g1 + trade_out + trade_q + trade_kv:
                    c.wait_send()
            else:
                dumps = [
                    pltpu.make_async_copy(ga, extra_gm, stg_sem.at[0]),
                    pltpu.make_async_copy(gproj, extra_gproj, stg_sem.at[1]),
                    pltpu.make_async_copy(att, extra_att, rt_sem.at[0]),
                ]
                for c in dumps:
                    c.start()
                for c in dumps:
                    c.wait()
            for g in keys + ag2 + ag3 + ag4 + rs2 + rs4 + kgrads:
                g.drain()

        ag1[0].start()
        mask(0)
        first_norm(1)
        clear()
        grad_rows(0)
        load_up.start()
        ag1[0].step(1)
        load_down.start()
        ag1[0].step(2)
        ag1[1].start()
        ag1[0].step(3)
        keys_out(0)
        queries(0)
        grad_rows(1)
        ag1[1].step(1)
        ag1[1].step(2)
        ag3[1].start()
        ag3[0].start()
        keys[0].step()
        keys[0].finish()
        attention(0)
        ag1[1].step(3)
        keys_out(1)
        mask(1)
        queries(1)
        ag3[0].step(1)
        rs1[0].step(0)
        keys[1].step()
        ag3[0].step(2)
        keys[1].finish()
        rs1[0].step(1)
        rs1[0].step(2)
        ag3[1].step(1)
        attention(1)
        sum_one(0)
        rs1[1].step(0)
        rs1[1].step(1)
        ag3[0].step(3)
        rs1[1].step(2)
        ag2[0].step(1)
        ag2[0].step(2)
        save_g1.start()
        sum_one(1)
        before_ffn()
        ag2[0].step(3)
        up_a(0)
        up_b(0)
        trade_grad(0)
        back_a(0)
        trade_act(0, 0)
        ag2[1].step(1)
        back_b(0)
        ffn_c(0)
        ag2[1].step(2)
        trade_act(1, 0)
        ag2[1].step(3)
        ag3[1].step(2)
        up_a(1)
        trade_act(0, 1)
        up_b(1)
        ag3[1].step(3)
        back_a(1)
        back_b(1)
        rs3[0].step(0)
        trade_grad(1)
        ffn_c(1)
        grads_down(0)
        rs3[0].step(1)
        push(0)
        trade_act(1, 1)
        ffn_out(1)
        offer()
        trade_one()
        rs3[0].step(2)
        grads_down(1)
        push(1)
        rs3[1].step(0)
        sum_three(0)
        pass_x(0)
        rs2[1].start()
        pass_y(0)
        rs3[1].step(1)
        ffn_out(0)
        rs3[1].step(2)
        pass_x(1)
        grads_up(0)
        load_g1.start()
        trade_two()
        push(2)
        ag4[0].step(1)
        grads_up(1)
        offer_two()
        pass_y(1)
        ag4[0].step(2)
        sum_three(1)
        push(3)
        ag4[0].step(3)
        grad_attended(0)
        attention_back(0)
        keys_back(0)
        ag4[1].step(1)
        rs2[0].start()
        pass_x(3)
        pass_y(2)
        ag4[1].step(2)
        ag4[1].step(3)
        grad_attended(1)
        rs2[0].step(0)
        attention_back(1)
        trade_four()
        keys_sum(0)
        rs2[0].step(1)
        rs2[0].step(2)
        keys_back(1)
        back_c(0)
        trade_three()
        rs2[1].step(0)
        grads_q()
        pass_x(2)
        grads_out()
        push(4)
        rs2[1].step(1)
        pass_y(3)
        keys_sum(1)
        trade_five()
        rs2[1].step(2)
        back_c(1)
        push(5)
        norms_at(0)
        sum_two(1)
        pass_x(4)
        pass_y(4)
        rs4[0].step(0)
        grads_kv()
        sum_two(0)
        push(6)
        pass_x(5)
        rs4[1].step(0)
        rs4[1].step(1)
        rs4[1].step(2)
        rs4[0].step(1)
        pass_y(5)
        rs4[0].step(2)
        pass_x(6)
        norms_at(1)
        pass_y(6)
        sum_four(1)
        norms_at(2)
        sum_four(0)
        norms_at(3)
        the_end()

    return kernel, w_lanes


def layer(z, tokens, out_grad, lengths, self_flags, episode_weight, g1, b1, g2, b2, w_qkv, w_out, w_up, w_down):
    S, R, D, LW, F, T, SEQ, H = z.S, z.R, z.D, z.LW, z.F, z.T, z.SEQ, z.H
    RT, PD = R * T, D // 8
    kernel, w_lanes = make_kernel(z)
    sds = jax.ShapeDtypeStruct
    any_, vmem, smem = (pl.BlockSpec(memory_space=m) for m in (pl.ANY, pltpu.VMEM, pltpu.SMEM))
    extra = (lambda *s: sds(s, bf16)) if not z.pairs else (lambda *s: sds((16, 128), bf16))
    pairs = (lambda *s: sds(s, bf16)) if z.pairs else (lambda *s: sds((16, 128), bf16))
    out_shape = [
        sds((R, S, D), bf16),
        sds((R, S, D), f32),
        sds((16, D // 4), f32),
        pairs(PD, w_lanes),
        pairs(PD, w_lanes),
        pairs(PD, w_lanes),
        pairs(3, PD, w_lanes),
        pairs(PD, w_lanes),
        pairs(PD, w_lanes),
        sds((R, RT, D), bf16),
        sds((RT, D), bf16),
        extra(RT, D),
        extra(RT, D),
        extra(RT, D),
        extra(RT, F),
        extra(RT, F),
        extra(RT, 3 * LW),
        extra(RT, LW),
    ]
    dma = pltpu.SemaphoreType.DMA
    reg = pltpu.SemaphoreType.REGULAR
    v = lambda *s: pltpu.VMEM(s, bf16)
    vf = lambda *s: pltpu.VMEM(s, f32)
    scratch = [
        v(D + F, D), v(RT, F), v(RT, D // 2), v(D, 3 * LW), v(LW, D), v(RT, D), v(RT, D), v(RT, D),
        v(RT, LW), v(R, SEQ, 2 * LW), v(RT, F), v(RT, F), v(RT, 3 * LW), v(RT, LW),
        v(RT, D), v(RT, D), v(R, 5, S, D), v(R, 5, S, D),
        vf(R, S, D), v(T, SEQ), v(2, PD, max(F, D) // 2), vf(3, 4, 16, D // 4), vf(S, D),
        dma((4, R, 6, 2)), dma((4, R, 4, 2)), dma((4, R, 6, 2)), dma((4, R, 6, 2)),
        dma((R, 3)), dma((R, 4)), dma((R, 3)), dma((R, 3)),
        dma((30,)), dma((30,)), dma((7, 6)), dma((7, 6)), dma((3, 3)), dma((3, 3)),
        dma((6,)), dma((3,)), dma((2,)), dma((4,)), reg, reg, reg,
    ]
    return pl.pallas_call(
        kernel,
        out_shape=out_shape,
        in_specs=[vmem] * 2 + [smem] * 3 + [vmem] * 4 + [any_] * 4,
        out_specs=[vmem] * 3 + [any_] * 15,
        scratch_shapes=scratch,
        compiler_params=pltpu.CompilerParams(
            collective_id=0, has_side_effects=True, vmem_limit_bytes=64 * 2**20 - 2**16
        ),
        cost_estimate=pl.CostEstimate(flops=42 * 10**9, bytes_accessed=10**8, transcendentals=10**7),
    )(tokens, out_grad, lengths, self_flags, episode_weight, g1, b1, g2, b2, w_qkv, w_out, w_up, w_down)


def last_step(z, y, gin, norms, ro, rx, ry):
    S, R, D, LW, F, PD = z.S, z.R, z.D, z.LW, z.F, z.D // 8
    steps = 4
    wide, slim = F // steps, LW // steps
    offsets = [(wide, 0), (wide, steps)]
    base = 2 * F // slim
    offsets += [(slim, base + k * steps) for k in range(4)]

    def kernel(*refs):
        y_in, gin_in, norms_in = refs[:3]
        parts = refs[3:21]
        out, gout, qkv, proj, up, down, one, two = refs[21:]

        def total(k):
            return parts[k][...].astype(f32) + parts[6 + k][...].astype(f32) + parts[12 + k][...].astype(f32)

        down[...] = total(0).T
        up[...] = total(1)
        proj[...] = total(2).T
        for j in range(3):
            qkv[j] = total(3 + j)
        for r in range(R):
            gout[:, r, :] = gin_in[r]
        out[...] = jnp.stack([y_in[r].astype(f32) for r in range(R)], axis=1).astype(bf16)
        for k, ref in enumerate((one, two)):
            for i in range(8):
                ref[i // 4 : i // 4 + 1, (i % 4) * (D // 4) : (i % 4 + 1) * (D // 4)] = norms_in[k * 8 + i : k * 8 + i + 1, :]

    spec = pl.BlockSpec
    rows = spec((R, S // steps, D), lambda i: (0, i, 0))
    in_specs = [rows, rows, spec((16, D // 4), lambda i: (0, 0))]
    for _ in range(3):
        in_specs += [spec((PD, w), lambda i, o=o: (0, o + i)) for w, o in offsets]
    sds = jax.ShapeDtypeStruct
    return pl.pallas_call(
        kernel,
        grid=(steps,),
        out_shape=[
            sds((S, R, D), bf16), sds((S, R, D), f32), sds((3, PD, LW), f32), sds((LW, PD), f32), sds((PD, F), f32),
            sds((F, PD), f32), sds((2, D), f32), sds((2, D), f32),
        ],
        in_specs=in_specs,
        out_specs=[
            spec((S // steps, R, D), lambda i: (i, 0, 0)), spec((S // steps, R, D), lambda i: (i, 0, 0)),
            spec((3, PD, slim), lambda i: (0, 0, i)), spec((slim, PD), lambda i: (i, 0)),
            spec((PD, wide), lambda i: (0, i)), spec((wide, PD), lambda i: (i, 0)), spec((2, D), lambda i: (0, 0)),
            spec((2, D), lambda i: (0, 0)),
        ],
        compiler_params=pltpu.CompilerParams(vmem_limit_bytes=64 * 2**20 - 2**16),
    )(y, gin, norms, *([ro] * 6 + [rx] * 6 + [ry] * 6))


def solution(mesh):
    shape = dict(mesh.shape)

    def on_device(
        tokens, lengths, self_flags, episode_weight, ln1_gain, ln1_bias, w_qkv, w_out, ln2_gain, ln2_bias, w_up,
        w_down, out_grad,
    ):
        z = Sizes(shape, tokens.shape, w_qkv.shape, w_up.shape, lengths.shape)
        row = lambda a: a.reshape(1, -1)
        results = layer(
            z, tokens, out_grad, lengths, self_flags, episode_weight, row(ln1_gain), row(ln1_bias), row(ln2_gain),
            row(ln2_bias), jnp.transpose(w_qkv, (1, 0, 2)), w_out, w_up, w_down,
        )
        y, gin, norms, ro, rx, ry = results[:6]
        if z.pairs:
            output, grad_input, qkv, grad_out, grad_up, grad_down, one, two = last_step(z, y, gin, norms, ro, rx, ry)
            return output, grad_input, jnp.transpose(qkv, (1, 0, 2)), grad_out, grad_up, grad_down, one, two
        output = jnp.transpose(y, (1, 0, 2))
        grad_input = jnp.transpose(gin, (1, 0, 2))
        g1_all, g2_all, gy_all, gm_all, act, gpre, gproj, att = results[10:]

        def over_tokens(a, b, dim):
            value = jnp.einsum("ta,tb->ab", a, b, preferred_element_type=f32).astype(bf16)
            return lax.psum_scatter(value, ("dp", "sp"), scatter_dimension=dim, tiled=True).astype(f32)

        grad_down = over_tokens(act, gy_all, 1)
        grad_up = over_tokens(g2_all, gpre, 0)
        grad_out = over_tokens(att, gm_all, 1)
        grad_qkv = over_tokens(g1_all, gproj, 0).reshape(-1, 3, z.LW)
        both = lax.psum(norms, ("dp", "sp", "tp"))
        both = both.reshape(2, 2, -1)
        return output, grad_input, grad_qkv, grad_out, grad_up, grad_down, both[0], both[1]

    return jax.shard_map(
        on_device,
        mesh=mesh,
        in_specs=(
            P(("sp", "tp"), "dp", None), P("dp", None), P("dp", None), P("dp", None), P(), P(), P(None, None, "tp"),
            P("tp", None), P(), P(), P(None, "tp"), P("tp", None), P(("sp", "tp"), "dp", None),
        ),
        out_specs=(
            P(("sp", "tp"), "dp", None), P(("sp", "tp"), "dp", None), P(("dp", "sp"), None, "tp"),
            P("tp", ("dp", "sp")), P(("dp", "sp"), "tp"), P("tp", ("dp", "sp")), P(), P(),
        ),
        check_vma=False,
    )
```

```python
import jax
import jax.numpy as jnp
from jax import lax
from jax.experimental import pallas as pl
from jax.experimental.pallas import tpu as pltpu
from jax.sharding import PartitionSpec as P

DH = 128
EPSILON = 1e-05
NEG = -1e30
f32 = jnp.float32
bf16 = jnp.bfloat16
MESH = pl.DeviceIdType.MESH


def dot(a, b, ca, cb):
    return lax.dot_general(a, b, (((ca,), (cb,)), ((), ())), preferred_element_type=f32)


def lanes(start, size):
    if isinstance(start, int):
        return pl.ds(start, size)
    return pl.ds(pl.multiple_of(start, 128), size)


def rows_at(start, size):
    if isinstance(start, int):
        return pl.ds(start, size)
    return pl.ds(pl.multiple_of(start, 64), size)


def norm_parts(values):
    average = jnp.mean(values, axis=-1, keepdims=True)
    centred = values - average
    variance = jnp.mean(centred * centred, axis=-1, keepdims=True)
    inverse = lax.rsqrt(variance + EPSILON)
    return centred * inverse, inverse


def norm_back(unit, inverse, gain, grad):
    scaled = grad * gain
    first = jnp.mean(scaled, axis=-1, keepdims=True)
    second = jnp.mean(scaled * unit, axis=-1, keepdims=True)
    return inverse * (scaled - first - unit * second)


class Sizes:
    def __init__(self, mesh_shape, tokens, w_qkv, w_up, lengths):
        self.n_dp = mesh_shape["dp"]
        self.n_sp = mesh_shape["sp"]
        self.n_tp = mesh_shape["tp"]
        self.S = tokens[0]
        self.R = tokens[1]
        self.D = tokens[2]
        self.LW = w_qkv[2]
        self.F = w_up[1]
        self.E = lengths[1]
        self.T = self.S * self.n_tp
        self.SEQ = self.T * self.n_sp
        self.H = self.LW // DH
        self.pairs = self.n_dp == 2 and self.n_sp == 4


def wgrad_kinds(z):
    half = z.F // 2
    out, offset = {}, 0
    for name, n, along in (
        ("d0", half, 5), ("d1", half, 5), ("u0", half, 6), ("u1", half, 6), ("out", z.LW, 6), ("q", z.LW, 4),
        ("kv", 2 * z.LW, 6),
    ):
        out[name] = (n, offset, n * along // 8)
        offset += n
    return out, offset


def make_kernel(z):
    S, R, D, LW, F, T, SEQ, H = z.S, z.R, z.D, z.LW, z.F, z.T, z.SEQ, z.H
    RT = R * T
    kinds, w_lanes = wgrad_kinds(z)
    scale = DH ** (-0.5)
    PD = D // 8

    def kernel(
        tok, og, lens, flags, eweight, g1, b1, g2, b2, wqkv_hbm, wout_hbm, wup_hbm, wdn_hbm,
        y_out, gin, norms, ro, rx, ry, sw, tx, ty, ph, g1h, extra_g2, extra_gy, extra_gm, extra_act, extra_gpre,
        extra_gproj, extra_att,
        arena, xact, xgy, wqkv, wout, ga, g2b, gyb, q, kv, act, gpre, gproj, att, part, part2, slots, slots2,
        mid, ds, stage, nr, total,
        ag_s, ag_r, rs_s, rs_r, kv_s, kv_r, dk_s, dk_r, x_s, x_r, w_s, w_r, n_s, n_r, loc, raw_sem, stg_sem,
        rt_sem, free_x, free_c, free_y,
    ):
        dp = lax.axis_index("dp")
        sp = lax.axis_index("sp")
        tp = lax.axis_index("tp")
        par = lax.rem(sp, 2)
        yy = lax.div(sp, 2)
        mate = sp + 1 - 2 * par
        far = lax.rem(sp + 2, 4)
        odp = 1 - dp
        kv_row = sp * T
        own = tp * S

        def remote(src, dst, ssem, rsem, device):
            return pltpu.make_async_remote_copy(
                src_ref=src, dst_ref=dst, send_sem=ssem, recv_sem=rsem, device_id=device, device_id_type=MESH
            )

        HS = S // 2

        class Gather:
            def __init__(self, buf, i, r):
                self.buf, self.i, self.r = buf, i, r

            def copy(self, shard, way, hop, h):
                sl = self.buf.at[pl.ds(pl.multiple_of(self.r * T + shard * S + h * HS, HS), HS), :]
                to = tp + 1 if way == 0 else tp - 1
                return remote(
                    sl,
                    sl,
                    ag_s.at[self.i, self.r, way * 3 + hop, h],
                    ag_r.at[self.i, self.r, shard, h],
                    (dp, sp, to),
                )

            def start(self):
                for h in range(2):

                    @pl.when(tp < 3)
                    def _(h=h):
                        self.copy(tp, 0, 0, h).start()

                    @pl.when(tp > 0)
                    def _(h=h):
                        self.copy(tp, 1, 0, h).start()

            def step(self, hop):
                for h in range(2):

                    @pl.when(tp >= hop)
                    def _(h=h):
                        self.copy(tp - hop, 0, 0, h).wait_recv()

                    if hop < 3:

                        @pl.when((tp >= hop) & (tp < 3))
                        def _(h=h):
                            self.copy(tp - hop, 0, hop, h).start()

                    @pl.when(tp <= 3 - hop)
                    def _(h=h):
                        self.copy(tp + hop, 1, 0, h).wait_recv()

                    if hop < 3:

                        @pl.when((tp <= 3 - hop) & (tp > 0))
                        def _(h=h):
                            self.copy(tp + hop, 1, hop, h).start()

            def drain(self):
                for hop in range(3):

                    @pl.when((tp >= hop) & (tp < 3))
                    def _(hop=hop):
                        for h in range(2):
                            self.copy(tp - hop, 0, hop, h).wait_send()

                    @pl.when((tp <= 3 - hop) & (tp > 0))
                    def _(hop=hop):
                        for h in range(2):
                            self.copy(tp + hop, 1, hop, h).wait_send()

        class Scatter:
            def __init__(self, buf, box, i, r):
                self.buf, self.box, self.i, self.r = buf, box, i, r

            def place(self, way, k, h):
                o = 3 - k if way == 0 else k
                return pl.ds(self.r * T + o * S + h * HS, HS)

            def slot(self, way, k):
                return k if way == 0 else 4 - k

            def copy(self, way, k, h):
                to = tp + 1 if way == 0 else tp - 1
                n = way * 3 + k
                return remote(
                    self.buf.at[self.place(way, k, h), :],
                    self.box.at[self.r, self.slot(way, k), pl.ds(h * HS, HS), :],
                    rs_s.at[self.i, self.r, n, h],
                    rs_r.at[self.i, self.r, n, h],
                    (dp, sp, to),
                )

            def start(self):
                for k in range(3):

                    @pl.when(tp == 0)
                    def _(k=k):
                        for h in range(2):
                            self.copy(0, k, h).start()

                    @pl.when(tp == 3)
                    def _(k=k):
                        for h in range(2):
                            self.copy(1, k, h).start()

            def relay(self, way, k):
                for h in range(2):
                    sl = self.place(way, k, h)
                    self.copy(way, k, h).wait_recv()
                    self.buf[sl, :] = (
                        self.buf[sl, :].astype(f32)
                        + self.box[self.r, self.slot(way, k), h * HS : (h + 1) * HS].astype(f32)
                    ).astype(bf16)
                    self.copy(way, k, h).start()

            def step(self, k):
                first, second, n = (0, 1, k) if k < 2 else (1, 0, 0)

                @pl.when(tp == 1)
                def _():
                    self.relay(first, n)

                @pl.when(tp == 2)
                def _():
                    self.relay(second, n)

            def finish(self):
                total[...] = self.buf[rows_at(self.r * T + own, S), :].astype(f32)
                for way in range(2):
                    for k in range(3):

                        @pl.when(tp == (3 - k if way == 0 else k))
                        def _(way=way, k=k):
                            for h in range(2):
                                self.copy(way, k, h).wait_recv()
                            total[...] += self.box[self.r, self.slot(way, k)].astype(f32)

            def drain(self):
                for k in range(3):

                    @pl.when(tp < 3 - k)
                    def _(k=k):
                        for h in range(2):
                            self.copy(0, k, h).wait_send()

                    @pl.when(tp > k)
                    def _(k=k):
                        for h in range(2):
                            self.copy(1, k, h).wait_send()

        class Keys:
            def __init__(self, r):
                self.r = r

            def copy(self, block, to, n):
                sl = kv.at[self.r, rows_at(block * T, T), :]
                return remote(sl, sl, kv_s.at[self.r, n], kv_r.at[self.r, block], (dp, to, tp))

            def start(self):
                @pl.when(sp < 2)
                def _():
                    self.copy(sp, sp + 2, 0).start()

                @pl.when(par == 0)
                def _():
                    self.copy(sp, sp + 1, 1).start()

            def step(self):
                for me, block, to in ((2, 0, 3), (3, 1, 2)):

                    @pl.when(sp == me)
                    def _(block=block, to=to):
                        self.copy(block, to, 0).wait_recv()
                        self.copy(block, to, 2).start()

            def finish(self):
                for me, block in ((1, 0), (2, 1), (3, 0), (3, 2)):

                    @pl.when(sp == me)
                    def _(block=block):
                        self.copy(block, 0, 0).wait_recv()

            def drain(self):
                @pl.when(sp < 2)
                def _():
                    self.copy(sp, sp + 2, 0).wait_send()

                @pl.when(par == 0)
                def _():
                    self.copy(sp, sp + 1, 1).wait_send()

                for me, block, to in ((2, 0, 3), (3, 1, 2)):

                    @pl.when(sp == me)
                    def _(block=block, to=to):
                        self.copy(block, to, 2).wait_send()

        KW = 2 * LW
        DK0 = 5 * RT
        DR0 = RT

        class KeyGrads:
            def __init__(self, r):
                self.r = r

            def src(self, block):
                return arena.at[pl.ds(DK0 + block * T, T), pl.ds(self.r * KW, KW)]

            def dst(self, box):
                return arena.at[pl.ds(DR0 + box * T, T), pl.ds(self.r * KW, KW)]

            def copy(self, block, to, box, n):
                return remote(
                    self.src(block), self.dst(box), dk_s.at[self.r, n], dk_r.at[self.r, box], (dp, to, tp)
                )

            def start(self):
                for me, block, to, box, n in ((3, 0, 2, 0, 0), (3, 2, 2, 1, 1), (2, 1, 3, 0, 0), (1, 0, 0, 1, 0)):

                    @pl.when(sp == me)
                    def _(block=block, to=to, box=box, n=n):
                        self.copy(block, to, box, n).start()

            def step(self):
                for me, block, to in ((2, 0, 0), (3, 1, 1)):

                    @pl.when(sp == me)
                    def _(block=block, to=to):
                        self.copy(block, to, 0, 2).wait_recv()
                        mine = pl.ds(DK0 + block * T, T)
                        col = pl.ds(self.r * KW, KW)
                        arena[mine, col] = (
                            arena[mine, col].astype(f32) + arena[pl.ds(DR0, T), col].astype(f32)
                        ).astype(bf16)
                        self.copy(block, to, 2, 2).start()

            def finish(self):
                col = pl.ds(self.r * KW, KW)
                there = pl.ds(self.r * T, T)
                to = pl.ds(LW, KW)
                for me, boxes in ((0, (1, 2)), (1, (2,)), (2, (1,)), (3, ())):

                    @pl.when(sp == me)
                    def _(me=me, boxes=boxes):
                        value = arena[pl.ds(DK0 + me * T, T), col].astype(f32)
                        for box in boxes:
                            self.copy(0, 0, box, 0).wait_recv()
                            value += arena[pl.ds(DR0 + box * T, T), col].astype(f32)
                        gproj[there, to] = value.astype(bf16)

            def drain(self):
                for me, block, to, box, n in (
                    (3, 0, 2, 0, 0), (3, 2, 2, 1, 1), (2, 1, 3, 0, 0), (1, 0, 0, 1, 0), (2, 0, 0, 2, 2), (3, 1, 1, 2, 2),
                ):

                    @pl.when(sp == me)
                    def _(block=block, to=to, box=box, n=n):
                        self.copy(block, to, box, n).wait_send()

        ends = []
        for r in range(R):
            run, row = 0, []
            for e in range(z.E):
                run = run + lens[r, e]
                row.append(run)
            ends.append(row)

        def first_norm(r):
            unit, _ = norm_parts(tok[:, r, :].astype(f32))
            ga[rows_at(r * T + own, S), :] = (unit * g1[...] + b1[...]).astype(bf16)

        def weighted_grad(r):
            place = sp * T + own + lax.broadcasted_iota(jnp.int32, (S, 1), 0)
            factor = jnp.full((S, 1), eweight[r, 0] * (1.0 + flags[r, 0].astype(f32)), f32)
            for e in range(1, z.E):
                factor = jnp.where(
                    place >= ends[r][e - 1], eweight[r, e] * (1.0 + flags[r, e].astype(f32)), factor
                )
            return og[:, r, :].astype(f32) * factor

        def project(r, j):
            value = dot(ga[r * T : (r + 1) * T, :], wqkv[:, j * LW : (j + 1) * LW], 1, 0).astype(bf16)
            if j == 0:
                q[r * T : (r + 1) * T, :] = value
            else:
                kv[r, rows_at(kv_row, T), (j - 1) * LW : j * LW] = value

        def mask(r):
            here = kv_row + lax.broadcasted_iota(jnp.int32, (T, 1), 0)
            begin = jnp.zeros((T, 1), jnp.int32)
            for e in range(z.E):
                begin = jnp.where(here >= ends[r][e], jnp.maximum(begin, ends[r][e]), begin)
            there = lax.broadcasted_iota(jnp.int32, (T, SEQ), 1)
            ds[...] = jnp.where((there <= here) & (there >= begin), 0.0, NEG).astype(bf16)

        half = T // 2
        ppl = D // SEQ
        keep = [act, gpre]

        def attend(r):
            def one(i, carry):
                rs = rows_at(i * half, half)
                qs = rows_at(r * T + i * half, half)
                for h in range(H):
                    hs = slice(h * DH, (h + 1) * DH)
                    s = dot(q[qs, hs], kv[r, :, hs], 1, 1) * scale + ds[rs, :].astype(f32)
                    peak = jnp.max(s, axis=1, keepdims=True)
                    e = jnp.exp(s - peak)
                    p = (e * (1.0 / jnp.sum(e, axis=1, keepdims=True))).astype(bf16)
                    keep[r][rows_at((h // ppl) * T + i * half, half), (h % ppl) * SEQ : (h % ppl + 1) * SEQ] = p
                    att[qs, hs] = dot(p, kv[r, :, LW + h * DH : LW + (h + 1) * DH], 1, 0).astype(bf16)
                return carry

            lax.fori_loop(0, 2, one, 0)

        def times(lhs, r, weight, out, transposed):
            width = 512
            n = out.shape[1] // width

            def one(j, carry):
                cs = lanes(j * width, width)
                w = weight(j, width)
                out[r * T : (r + 1) * T, cs] = dot(lhs, w, 1, 1 if transposed else 0).astype(bf16)
                return carry

            lax.fori_loop(0, n, one, 0)

        def project_out(r):
            def one(j, carry):
                cs = lanes(j * 512, 512)
                part[r * T : (r + 1) * T, cs] = dot(att[r * T : (r + 1) * T, :], wout[:, cs], 1, 0).astype(bf16)
                return carry

            lax.fori_loop(0, D // 512, one, 0)

        def ffn_up(r, low, high):
            rs = slice(r * T, (r + 1) * T)

            def one(j, carry):
                cs = lanes(j * 256, 256)
                pre = dot(g2b[rs, :], arena[0:D, cs], 1, 0)
                e = 0.5 * (1.0 + lax.erf(pre * 0.7071067811865476))
                act[rs, cs] = (pre * e).astype(bf16)
                gpre[rs, cs] = (e + pre * (jnp.exp(-0.5 * pre * pre) * 0.3989422804014327)).astype(bf16)
                return carry

            lax.fori_loop(low, high, one, 0)

        def ffn_slope(r, low, high):
            rs = slice(r * T, (r + 1) * T)

            def one(j, carry):
                cs = lanes(j * 256, 256)
                back = dot(gyb[rs, :], arena[rows_at(D + j * 256, 256), :], 1, 1)
                gpre[rs, cs] = (back * gpre[rs, cs].astype(f32)).astype(bf16)
                return carry

            lax.fori_loop(low, high, one, 0)

        def ffn_back(r):
            rs = slice(r * T, (r + 1) * T)

            def one(j, carry):
                part[rs, lanes(j * 512, 512)] = dot(gpre[rs, :], arena[rows_at(j * 512, 512), :], 1, 1).astype(bf16)
                return carry

            lax.fori_loop(0, D // 512, one, 0)

        def ffn_out(r):
            rs = slice(r * T, (r + 1) * T)

            def one(j, carry):
                cs = lanes(j * 512, 512)
                part2[rs, cs] = dot(act[rs, :], arena[D : D + F, cs], 1, 0).astype(bf16)
                return carry

            lax.fori_loop(0, D // 512, one, 0)

        def second_norm(r):
            value = tok[:, r, :].astype(f32) + total[...]
            mid[r] = value
            unit, _ = norm_parts(value)
            g2b[rows_at(r * T + own, S), :] = (unit * g2[...] + b2[...]).astype(bf16)

        def add_norms(grad, unit):
            sums = (jnp.sum(grad * unit, axis=0, keepdims=True), jnp.sum(grad, axis=0, keepdims=True))
            for i in range(8):
                piece = sums[i // 4][:, (i % 4) * (D // 4) : (i % 4 + 1) * (D // 4)]
                nr[0, pl.ds(tp, 1), 8 + i : 9 + i, :] += piece[None]

        def second_norm_back(r):
            unit, inverse = norm_parts(mid[r])
            grad = total[...]
            add_norms(grad, unit)
            value = weighted_grad(r) + norm_back(unit, inverse, g2[...], grad)
            gin[r] = value
            ga[rows_at(r * T + own, S), :] = value.astype(bf16)

        def first_norm_back(r):
            unit, inverse = norm_parts(tok[:, r, :].astype(f32))
            grad = total[...]
            gin[r] = gin[r] + norm_back(unit, inverse, g1[...], grad)

        def attend_back(r):
            rows = slice(r * T, (r + 1) * T)

            def one(h, carry):
                hs, vs = lanes(h * DH, DH), lanes(LW + h * DH, DH)
                top = lax.div(h, ppl) * T
                pc = lanes(lax.rem(h, ppl) * SEQ, SEQ)
                for t in range(2):
                    gp = dot(gproj[r * T + t * half : r * T + (t + 1) * half, hs], kv[r, :, vs], 1, 1)
                    p = keep[r][rows_at(top + t * half, half), pc].astype(f32)
                    x = p * gp
                    delta = jnp.sum(x, axis=1, keepdims=True)
                    ds[t * half : (t + 1) * half, :] = ((x - p * delta) * scale).astype(bf16)
                arena[DK0 : DK0 + SEQ, lanes(r * KW + h * DH, DH)] = dot(ds[...], q[rows, hs], 0, 0).astype(bf16)
                arena[DK0 : DK0 + SEQ, lanes(r * KW + LW + h * DH, DH)] = dot(
                    keep[r][rows_at(top, T), pc], gproj[rows, hs], 0, 0
                ).astype(bf16)
                gproj[rows, hs] = dot(ds[...], kv[r, :, hs], 1, 0).astype(bf16)
                return carry

            lax.fori_loop(0, H, one, 0)

        def grad_attended(r):
            rows = slice(r * T, (r + 1) * T)
            gproj[rows, 0:LW] = dot(ga[rows, :], wout[...], 1, 1).astype(bf16)

        def qkv_back(r):
            rs = slice(r * T, (r + 1) * T)
            ns = slice(7 * RT + r * T, 7 * RT + (r + 1) * T)
            width = D // 4

            def one(j, carry):
                cs = lanes(j * width, width)
                value = dot(gproj[rs, :], wqkv[rows_at(j * width, width), :], 1, 1)
                part[rs, cs] = value.astype(bf16)
                normed = arena[ns, cs].astype(f32)
                nr[0, pl.ds(tp, 1), pl.ds(j, 1), :] += jnp.sum(value * normed, axis=0, keepdims=True)[None]
                nr[0, pl.ds(tp, 1), pl.ds(4 + j, 1), :] += jnp.sum(value, axis=0, keepdims=True)[None]
                return carry

            lax.fori_loop(0, 4, one, 0)

        load_out = pltpu.make_async_copy(wout_hbm, wout, loc.at[0])
        load_qkv = [
            pltpu.make_async_copy(wqkv_hbm.at[j], wqkv.at[:, pl.ds(j * LW, LW)], raw_sem.at[j]) for j in range(3)
        ]
        load_up = pltpu.make_async_copy(wup_hbm, arena.at[pl.ds(0, D), :], loc.at[1])
        load_down = pltpu.make_async_copy(wdn_hbm, arena.at[pl.ds(D, F), :], loc.at[2])
        save_p = [pltpu.make_async_copy(keep[r], ph.at[r], loc.at[3 + r]) for r in range(R)]
        load_p = [pltpu.make_async_copy(ph.at[r], keep[r], loc.at[3 + r]) for r in range(R)]
        save_g1 = pltpu.make_async_copy(ga, g1h, loc.at[5])
        load_g1 = pltpu.make_async_copy(g1h, arena.at[pl.ds(7 * RT, RT), :], loc.at[5])

        XP, XG, XH, XJ = RT, 2 * RT, 3 * RT, 4 * RT
        there = (dp, mate, tp)
        oth = 1 - par

        def halves(buf, buf_row, size, box, box_row, box_lane, n):
            return [
                remote(
                    buf.at[pl.ds(buf_row, size), lanes(b * 2 * PD + oth * PD, PD)],
                    box.at[pl.ds(box_row, size), pl.ds(box_lane + b * PD, PD)],
                    x_s.at[n + b],
                    x_r.at[n + b],
                    there,
                )
                for b in range(4)
            ]

        def piece(buf, row, size, lane, width, box, box_row, box_lane, n):
            return [
                remote(
                    buf.at[pl.ds(row, size), pl.ds(lane, width)],
                    box.at[pl.ds(box_row, size), pl.ds(box_lane, width)],
                    x_s.at[n],
                    x_r.at[n],
                    there,
                )
            ]

        trade_rows = [[piece(act, r * T, T, h * F // 2, F // 2, xact, r * T, h * F // 2, 2 * h + r) for r in range(R)] for h in range(2)]
        trade_gy = [halves(gyb, r * T, T, xgy, r * T, 0, 22 + 4 * r) for r in range(R)]
        trade_up = piece(gpre, 0, RT, 0, F, arena, XP, 0, 21) + halves(g2b, 0, RT, arena, XG, 0, 6)
        trade_g1 = halves(arena, 7 * RT, RT, arena, XH, 0, 10)
        trade_out = piece(att, 0, RT, 0, LW, arena, XJ, 3 * LW, 18) + halves(ga, 0, RT, arena, XH, D // 2, 14)
        trade_q = piece(gproj, 0, RT, 0, LW, arena, XJ, 0, 19)
        trade_kv = piece(gproj, 0, RT, LW, 2 * LW, arena, XJ, LW, 20)

        names = list(kinds)
        operands = {
            "d0": ((gyb, 0), (act, 0), (xgy, 0, 0), (xact, 0, 0)),
            "d1": ((gyb, 0), (act, F // 2), (xgy, 0, 0), (xact, 0, F // 2)),
            "u0": ((g2b, 0), (gpre, 0), (arena, XG, 0), (arena, XP, 0)),
            "u1": ((g2b, 0), (gpre, F // 2), (arena, XG, 0), (arena, XP, F // 2)),
            "out": ((ga, 0), (att, 0), (arena, XH, D // 2), (arena, XJ, 3 * LW)),
            "q": ((arena, 7 * RT), (gproj, 0), (arena, XH, 0), (arena, XJ, 0)),
            "kv": ((arena, 7 * RT), (gproj, LW), (arena, XH, 0), (arena, XJ, LW)),
        }

        def tile(t, way, size):
            if way == 0:
                return arena.at[pl.ds(0, PD), pl.ds((t % 2) * (D // 2), size)]
            return arena.at[pl.ds(XG + PD, PD), pl.ds(D // 2 + (t % 2) * (D // 4), size)]

        def w_copy(name, which):
            t = names.index(name)
            n, off, a = kinds[name]
            ca, cb = pl.ds(off, a), pl.ds(off + a, n - a)
            x_to, y_to = (odp, sp, tp), (dp, far, tp)
            src, dst, to = {
                "S2": (sw.at[0, :, ca], tx.at[:, ca], x_to),
                "S4": (sw.at[0, :, cb], ty.at[:, cb], y_to),
                "S1": (sw.at[1, :, ca], rx.at[:, ca], x_to),
                "S3": (sw.at[2, :, cb], ry.at[:, cb], y_to),
                "R1": (tile(t, 0, a), ry.at[:, ca], y_to),
                "R2": (tile(t, 1, n - a), rx.at[:, cb], x_to),
            }[which]
            k = ("S1", "S2", "S3", "S4", "R1", "R2").index(which)
            return remote(src, dst, w_s.at[t, k], w_r.at[t, k], to)

        def weight_grad(name):
            (own_d, own_row), (own_r, own_lane), (mate_d, d_row, d_lane), (mate_r, r_row, r_lane) = operands[name]
            n, off, _ = kinds[name]
            own_r = own_r.at[:, pl.ds(own_lane, n)]
            mate_r = mate_r.at[pl.ds(r_row, RT), pl.ds(r_lane, n)]

            def staged(i, dst):
                slot = lax.rem(i, 2)
                return pltpu.make_async_copy(
                    stage.at[slot, :, pl.ds(0, n)], dst.at[:, pl.ds(off, n)], stg_sem.at[slot]
                )

            def one(i, carry):
                b4 = jnp.where(i < 2, odp, dp) * 2 + jnp.where(lax.rem(i, 2) == 0, 1 - yy, yy)
                value = dot(own_d[own_row : own_row + RT, lanes(b4 * 2 * PD + par * PD, PD)], own_r[...], 0, 0)
                value += dot(mate_d[d_row : d_row + RT, lanes(d_lane + b4 * PD, PD)], mate_r[...], 0, 0)
                stage[lax.rem(i, 2), :, 0:n] = value.astype(bf16)

                @pl.when(i < 3)
                def _():
                    staged(i, sw.at[i]).start()

                @pl.when(i == 3)
                def _():
                    staged(i, ro).start()

                @pl.when(i > 0)
                def _():
                    staged(i - 1, sw.at[i - 1]).wait()

                for k, which in ((1, "S2"), (2, "S1")):

                    @pl.when(i == k)
                    def _(which=which):
                        w_copy(name, which).start()

                return carry

            lax.fori_loop(0, 4, one, 0)
            staged(3, ro).wait()

        def relay_sum(name, way):
            t = names.index(name)
            n, off, a = kinds[name]
            first, size, box, block, need, send = (
                (0, a, tx, 2, "S2", "R1") if way == 0 else (a, n - a, ty, 1, "S4", "R2")
            )
            if t > 1:
                w_copy(names[t - 2], send).wait_send()
            there_l = pl.ds(off + first, size)
            mine, met = tile(t, way, size), arena.at[pl.ds(PD, PD), pl.ds(0, size)]
            own_c = pltpu.make_async_copy(sw.at[block, :, there_l], mine, rt_sem.at[way])
            got_c = pltpu.make_async_copy(box.at[:, there_l], met, rt_sem.at[2 + way])
            own_c.start()
            w_copy(name, need).wait_recv()
            got_c.start()
            own_c.wait()
            got_c.wait()
            mine[...] = (mine[...].astype(f32) + met[...].astype(f32)).astype(bf16)
            w_copy(name, send).start()

        def finish_sums(name):
            for which in ("S1", "S3", "R1", "R2"):
                w_copy(name, which).wait_recv()
            for which in ("S1", "S2", "S3", "S4"):
                w_copy(name, which).wait_send()
            if names.index(name) >= len(names) - 2:
                w_copy(name, "R1").wait_send()
                w_copy(name, "R2").wait_send()

        norm_axes = ((4, tp), (4, sp), (z.n_dp, dp))

        def norm_copies(i):
            axis_n, index = norm_axes[i]
            slot = nr.at[i, pl.ds(index, 1)]
            copies = []
            for d in range(1, axis_n):
                to = lax.rem(index + d, axis_n)
                device = ((dp, sp, to), (dp, to, tp), (to, sp, tp))[i]
                copies.append(remote(slot, slot, n_s.at[i, d - 1], n_r.at[i, d - 1], device))
            return copies

        def norm_result(value):
            norms[4:16, :] = value[4:16, :]
            for i in range(4):
                cs = slice(i * (D // 4), (i + 1) * (D // 4))
                norms[i : i + 1, :] = (value[i : i + 1, :] - b1[:, cs] * value[4 + i : 5 + i, :]) / g1[:, cs]

        def norm_add(i):
            for c in norm_copies(i):
                c.wait_send()
                c.wait_recv()
            value = nr[i, 0]
            for n in range(1, norm_axes[i][0]):
                value = value + nr[i, n]
            return value

        load_out.start()
        for c in load_qkv:
            c.start()
        barrier = pltpu.get_barrier_semaphore()
        greet = [(dp, sp, lax.rem(tp + d, 4)) for d in (1, 2, 3)]
        greet += [(dp, lax.rem(sp + d, 4), tp) for d in (1, 2, 3)]
        if z.pairs:
            greet += [(odp, sp, tp)]
        for device in greet:
            pl.semaphore_signal(barrier, inc=1, device_id=device, device_id_type=MESH)
        first_norm(0)
        pl.semaphore_wait(barrier, len(greet))

        ag1 = [Gather(ga, 0, r) for r in range(R)]
        ag2 = [Gather(g2b, 1, r) for r in range(R)]
        ag3 = [Gather(gyb, 2, r) for r in range(R)]
        ag4 = [Gather(ga, 3, r) for r in range(R)]
        rs1 = [Scatter(part, slots, 0, r) for r in range(R)]
        rs3 = [Scatter(part, slots, 1, r) for r in range(R)]
        rs4 = [Scatter(part, slots, 2, r) for r in range(R)]
        rs2 = [Scatter(part2, slots2, 3, r) for r in range(R)]
        keys = [Keys(r) for r in range(R)]
        kgrads = [KeyGrads(r) for r in range(R)]

        def grad_rows(r):
            gyb[rows_at(r * T + own, S), :] = weighted_grad(r).astype(bf16)

        def clear():
            nr[0, pl.ds(tp, 1)] = jnp.zeros((1,) + nr.shape[2:], f32)
            for b in range(1, 4):

                @pl.when(b > sp)
                def _(b=b):
                    kv[:, b * T : (b + 1) * T, :] = jnp.zeros((R, T, KW), bf16)

        def keys_out(r):
            if r == 0:
                for c in load_qkv:
                    c.wait()
            project(r, 1)
            project(r, 2)
            keys[r].start()

        def queries(r):
            project(r, 0)

        def attention(r):
            attend(r)
            save_p[r].start()
            if r == 0:
                load_out.wait()
            project_out(r)
            rs1[r].start()

        def sum_one(r):
            rs1[r].finish()
            second_norm(r)
            ag2[r].start()

        def before_ffn():
            load_up.wait()
            load_down.wait()
            save_g1.wait()
            for c in save_p:
                c.wait()
            for g in ag1:
                g.drain()

        def up_a(r):
            ffn_up(r, 0, F // 512)

        def up_b(r):
            ffn_up(r, F // 512, F // 256)

        def back_a(r):
            ffn_slope(r, 0, F // 512)

        def back_b(r):
            ffn_slope(r, F // 512, F // 256)

        def ffn_c(r):
            rs1[r].drain()
            ffn_back(r)
            rs3[r].start()

        def sum_three(r):
            rs3[r].finish()
            second_norm_back(r)
            ag4[r].start()

        def sum_two(r):
            rs2[r].finish()
            y_out[r] = (mid[r] + total[...]).astype(bf16)

        def sum_four(r):
            rs4[r].finish()
            first_norm_back(r)

        def offer():
            if z.pairs:
                pl.semaphore_signal(free_x, inc=1, device_id=there, device_id_type=MESH)

        def trade_act(h, r):
            if z.pairs:
                for c in trade_rows[h][r]:
                    c.start()

        def trade_grad(r):
            if z.pairs:
                for c in trade_gy[r]:
                    c.start()

        def trade_one():
            if z.pairs:
                pl.semaphore_wait(free_x, 1)
                for c in trade_up:
                    c.start()

        def grads_down(h):
            if z.pairs:
                for c in trade_rows[h][0] + trade_rows[h][1] + (trade_gy[0] + trade_gy[1] if h == 0 else []):
                    c.wait_recv()
                weight_grad(names[h])

        def grads_up(h):
            if z.pairs:
                if h == 0:
                    for c in trade_up:
                        c.wait_recv()
                weight_grad(names[2 + h])

        def offer_two():
            if z.pairs:
                for c in trade_rows[0][0] + trade_rows[0][1] + trade_rows[1][0] + trade_rows[1][1] + trade_gy[0] + trade_gy[1] + trade_up:
                    c.wait_send()
            else:
                dumps = [
                    pltpu.make_async_copy(act, extra_act, stg_sem.at[0]),
                    pltpu.make_async_copy(gpre, extra_gpre, stg_sem.at[1]),
                    pltpu.make_async_copy(g2b, extra_g2, rt_sem.at[0]),
                    pltpu.make_async_copy(gyb, extra_gy, rt_sem.at[1]),
                ]
                for c in dumps:
                    c.start()
                for c in dumps:
                    c.wait()
            pl.semaphore_signal(free_c, inc=1, device_id=there, device_id_type=MESH)
            pl.semaphore_signal(free_y, inc=1, device_id=(dp, far, tp), device_id_type=MESH)
            for c in load_p:
                c.start()

        def trade_two():
            load_g1.wait()
            if z.pairs:
                for c in trade_g1:
                    c.start()

        def attention_back(r):
            load_p[r].wait()
            attend_back(r)
            if r == 0:
                pl.semaphore_wait(free_c, 1)
            kgrads[r].start()

        def keys_back(r):
            if r == 0:
                pl.semaphore_wait(free_y, 1)
            kgrads[r].step()

        def keys_sum(r):
            kgrads[r].finish()

        def trade_three():
            if z.pairs:
                for c in trade_out:
                    c.start()

        def grads_out():
            if z.pairs:
                for c in trade_out:
                    c.wait_recv()
                weight_grad("out")

        def trade_four():
            if z.pairs:
                for c in trade_q:
                    c.start()

        def trade_five():
            if z.pairs:
                for c in trade_kv:
                    c.start()

        def grads_q():
            if z.pairs:
                for c in trade_g1 + trade_q:
                    c.wait_recv()
                weight_grad("q")

        def grads_kv():
            if z.pairs:
                for c in trade_kv:
                    c.wait_recv()
                weight_grad("kv")

        def push(i):
            if z.pairs:
                w_copy(names[i], "S4").start()
                w_copy(names[i], "S3").start()

        def pass_y(i):
            if z.pairs:
                relay_sum(names[i], 0)

        def pass_x(i):
            if z.pairs:
                relay_sum(names[i], 1)

        def back_c(r):
            rs3[r].drain()
            qkv_back(r)
            rs4[r].start()

        def norms_at(i):
            if not z.pairs:
                if i == 3:
                    norm_result(nr[0, pl.ds(tp, 1)][0])
                return
            if i:
                value = norm_add(i - 1)
                if i == 3:
                    norm_result(value)
                    return
                nr[i, pl.ds((sp, dp)[i - 1], 1)] = value[None]
            for c in norm_copies(i):
                c.start()

        def the_end():
            if z.pairs:
                for name in names:
                    finish_sums(name)
                for c in trade_g1 + trade_out + trade_q + trade_kv:
                    c.wait_send()
            else:
                dumps = [
                    pltpu.make_async_copy(ga, extra_gm, stg_sem.at[0]),
                    pltpu.make_async_copy(gproj, extra_gproj, stg_sem.at[1]),
                    pltpu.make_async_copy(att, extra_att, rt_sem.at[0]),
                ]
                for c in dumps:
                    c.start()
                for c in dumps:
                    c.wait()
            for g in keys + ag2 + ag3 + ag4 + rs2 + rs4 + kgrads:
                g.drain()

        ag1[0].start()
        mask(0)
        grad_rows(0)
        clear()
        first_norm(1)
        ag1[0].step(1)
        grad_rows(1)
        load_up.start()
        ag1[0].step(2)
        ag1[1].start()
        ag1[0].step(3)
        keys_out(0)
        queries(0)
        ag1[1].step(1)
        load_down.start()
        ag1[1].step(2)
        keys[0].step()
        ag3[0].start()
        keys[0].finish()
        attention(0)
        ag1[1].step(3)
        keys_out(1)
        queries(1)
        ag3[0].step(1)
        save_g1.start()
        keys[1].step()
        rs1[0].step(0)
        ag3[0].step(2)
        rs1[0].step(1)
        keys[1].finish()
        ag3[0].step(3)
        rs1[0].step(2)
        ag3[1].start()
        trade_grad(0)
        mask(1)
        sum_one(0)
        attention(1)
        ag2[0].step(1)
        rs1[1].step(0)
        ag2[0].step(2)
        ag2[0].step(3)
        before_ffn()
        up_a(0)
        back_a(0)
        rs1[1].step(1)
        rs1[1].step(2)
        trade_act(0, 0)
        up_b(0)
        ag3[1].step(1)
        trade_act(1, 0)
        sum_one(1)
        back_b(0)
        ffn_c(0)
        ag2[1].step(1)
        ffn_out(0)
        ag2[1].step(2)
        ag2[1].step(3)
        rs3[0].step(0)
        up_a(1)
        trade_act(0, 1)
        rs2[0].start()
        up_b(1)
        ag3[1].step(2)
        rs3[0].step(1)
        ag3[1].step(3)
        trade_grad(1)
        back_a(1)
        rs3[0].step(2)
        trade_act(1, 1)
        grads_down(0)
        push(0)
        back_b(1)
        sum_three(0)
        ffn_c(1)
        offer()
        pass_y(0)
        rs2[0].step(0)
        trade_one()
        grads_down(1)
        push(1)
        pass_x(0)
        ffn_out(1)
        ag4[0].step(1)
        grads_up(0)
        push(2)
        rs3[1].step(0)
        ag4[0].step(2)
        load_g1.start()
        pass_y(1)
        grads_up(1)
        rs3[1].step(1)
        rs3[1].step(2)
        ag4[0].step(3)
        grad_attended(0)
        offer_two()
        attention_back(0)
        sum_three(1)
        keys_back(0)
        trade_two()
        rs2[1].start()
        push(3)
        pass_x(2)
        pass_y(2)
        pass_x(1)
        ag4[1].step(1)
        rs2[0].step(1)
        keys_sum(0)
        ag4[1].step(2)
        back_c(0)
        rs2[0].step(2)
        ag4[1].step(3)
        grad_attended(1)
        rs2[1].step(0)
        attention_back(1)
        keys_back(1)
        trade_four()
        trade_three()
        rs2[1].step(1)
        rs2[1].step(2)
        pass_y(3)
        rs4[0].step(0)
        grads_q()
        grads_out()
        rs4[0].step(1)
        push(5)
        push(4)
        pass_x(3)
        keys_sum(1)
        trade_five()
        back_c(1)
        sum_two(1)
        grads_kv()
        push(6)
        rs4[0].step(2)
        norms_at(0)
        rs4[1].step(0)
        sum_two(0)
        pass_y(4)
        pass_x(4)
        rs4[1].step(1)
        pass_x(5)
        sum_four(0)
        pass_y(5)
        rs4[1].step(2)
        norms_at(1)
        pass_y(6)
        norms_at(2)
        pass_x(6)
        norms_at(3)
        sum_four(1)
        the_end()

    return kernel, w_lanes


def layer(z, tokens, out_grad, lengths, self_flags, episode_weight, g1, b1, g2, b2, w_qkv, w_out, w_up, w_down):
    S, R, D, LW, F, T, SEQ, H = z.S, z.R, z.D, z.LW, z.F, z.T, z.SEQ, z.H
    RT, PD = R * T, D // 8
    kernel, w_lanes = make_kernel(z)
    sds = jax.ShapeDtypeStruct
    any_, vmem, smem = (pl.BlockSpec(memory_space=m) for m in (pl.ANY, pltpu.VMEM, pltpu.SMEM))
    extra = (lambda *s: sds(s, bf16)) if not z.pairs else (lambda *s: sds((16, 128), bf16))
    pairs = (lambda *s: sds(s, bf16)) if z.pairs else (lambda *s: sds((16, 128), bf16))
    out_shape = [
        sds((R, S, D), bf16),
        sds((R, S, D), f32),
        sds((16, D // 4), f32),
        pairs(PD, w_lanes),
        pairs(PD, w_lanes),
        pairs(PD, w_lanes),
        pairs(3, PD, w_lanes),
        pairs(PD, w_lanes),
        pairs(PD, w_lanes),
        sds((R, RT, D), bf16),
        sds((RT, D), bf16),
        extra(RT, D),
        extra(RT, D),
        extra(RT, D),
        extra(RT, F),
        extra(RT, F),
        extra(RT, 3 * LW),
        extra(RT, LW),
    ]
    dma = pltpu.SemaphoreType.DMA
    reg = pltpu.SemaphoreType.REGULAR
    v = lambda *s: pltpu.VMEM(s, bf16)
    vf = lambda *s: pltpu.VMEM(s, f32)
    scratch = [
        v(D + F, D), v(RT, F), v(RT, D // 2), v(D, 3 * LW), v(LW, D), v(RT, D), v(RT, D), v(RT, D),
        v(RT, LW), v(R, SEQ, 2 * LW), v(RT, F), v(RT, F), v(RT, 3 * LW), v(RT, LW),
        v(RT, D), v(RT, D), v(R, 5, S, D), v(R, 5, S, D),
        vf(R, S, D), v(T, SEQ), v(2, PD, max(F, D) // 2), vf(3, 4, 16, D // 4), vf(S, D),
        dma((4, R, 6, 2)), dma((4, R, 4, 2)), dma((4, R, 6, 2)), dma((4, R, 6, 2)),
        dma((R, 3)), dma((R, 4)), dma((R, 3)), dma((R, 3)),
        dma((30,)), dma((30,)), dma((7, 6)), dma((7, 6)), dma((3, 3)), dma((3, 3)),
        dma((6,)), dma((3,)), dma((2,)), dma((4,)), reg, reg, reg,
    ]
    return pl.pallas_call(
        kernel,
        out_shape=out_shape,
        in_specs=[vmem] * 2 + [smem] * 3 + [vmem] * 4 + [any_] * 4,
        out_specs=[vmem] * 3 + [any_] * 15,
        scratch_shapes=scratch,
        compiler_params=pltpu.CompilerParams(
            collective_id=0, has_side_effects=True, vmem_limit_bytes=64 * 2**20 - 2**16
        ),
        cost_estimate=pl.CostEstimate(flops=42 * 10**9, bytes_accessed=10**8, transcendentals=10**7),
    )(tokens, out_grad, lengths, self_flags, episode_weight, g1, b1, g2, b2, w_qkv, w_out, w_up, w_down)


def last_step(z, y, gin, norms, ro, rx, ry):
    S, R, D, LW, F, PD = z.S, z.R, z.D, z.LW, z.F, z.D // 8
    steps = 4
    wide, slim = F // steps, LW // steps
    offsets = [(wide, 0), (wide, steps)]
    base = 2 * F // slim
    offsets += [(slim, base + k * steps) for k in range(4)]

    def kernel(*refs):
        y_in, gin_in, norms_in = refs[:3]
        parts = refs[3:21]
        out, gout, qkv, proj, up, down, one, two = refs[21:]

        def total(k):
            return parts[k][...].astype(f32) + parts[6 + k][...].astype(f32) + parts[12 + k][...].astype(f32)

        down[...] = total(0).T
        up[...] = total(1)
        proj[...] = total(2).T
        for j in range(3):
            qkv[j] = total(3 + j)
        for r in range(R):
            gout[:, r, :] = gin_in[r]
        out[...] = jnp.stack([y_in[r].astype(f32) for r in range(R)], axis=1).astype(bf16)
        for k, ref in enumerate((one, two)):
            for i in range(8):
                ref[i // 4 : i // 4 + 1, (i % 4) * (D // 4) : (i % 4 + 1) * (D // 4)] = norms_in[k * 8 + i : k * 8 + i + 1, :]

    spec = pl.BlockSpec
    rows = spec((R, S // steps, D), lambda i: (0, i, 0))
    in_specs = [rows, rows, spec((16, D // 4), lambda i: (0, 0))]
    for _ in range(3):
        in_specs += [spec((PD, w), lambda i, o=o: (0, o + i)) for w, o in offsets]
    sds = jax.ShapeDtypeStruct
    return pl.pallas_call(
        kernel,
        grid=(steps,),
        out_shape=[
            sds((S, R, D), bf16), sds((S, R, D), f32), sds((3, PD, LW), f32), sds((LW, PD), f32), sds((PD, F), f32),
            sds((F, PD), f32), sds((2, D), f32), sds((2, D), f32),
        ],
        in_specs=in_specs,
        out_specs=[
            spec((S // steps, R, D), lambda i: (i, 0, 0)), spec((S // steps, R, D), lambda i: (i, 0, 0)),
            spec((3, PD, slim), lambda i: (0, 0, i)), spec((slim, PD), lambda i: (i, 0)),
            spec((PD, wide), lambda i: (0, i)), spec((wide, PD), lambda i: (i, 0)), spec((2, D), lambda i: (0, 0)),
            spec((2, D), lambda i: (0, 0)),
        ],
        compiler_params=pltpu.CompilerParams(vmem_limit_bytes=64 * 2**20 - 2**16),
    )(y, gin, norms, *([ro] * 6 + [rx] * 6 + [ry] * 6))


def solution(mesh):
    shape = dict(mesh.shape)

    def on_device(
        tokens, lengths, self_flags, episode_weight, ln1_gain, ln1_bias, w_qkv, w_out, ln2_gain, ln2_bias, w_up,
        w_down, out_grad,
    ):
        z = Sizes(shape, tokens.shape, w_qkv.shape, w_up.shape, lengths.shape)
        row = lambda a: a.reshape(1, -1)
        results = layer(
            z, tokens, out_grad, lengths, self_flags, episode_weight, row(ln1_gain), row(ln1_bias), row(ln2_gain),
            row(ln2_bias), jnp.transpose(w_qkv, (1, 0, 2)), w_out, w_up, w_down,
        )
        y, gin, norms, ro, rx, ry = results[:6]
        if z.pairs:
            output, grad_input, qkv, grad_out, grad_up, grad_down, one, two = last_step(z, y, gin, norms, ro, rx, ry)
            return output, grad_input, jnp.transpose(qkv, (1, 0, 2)), grad_out, grad_up, grad_down, one, two
        output = jnp.transpose(y, (1, 0, 2))
        grad_input = jnp.transpose(gin, (1, 0, 2))
        g1_all, g2_all, gy_all, gm_all, act, gpre, gproj, att = results[10:]

        def over_tokens(a, b, dim):
            value = jnp.einsum("ta,tb->ab", a, b, preferred_element_type=f32).astype(bf16)
            return lax.psum_scatter(value, ("dp", "sp"), scatter_dimension=dim, tiled=True).astype(f32)

        grad_down = over_tokens(act, gy_all, 1)
        grad_up = over_tokens(g2_all, gpre, 0)
        grad_out = over_tokens(att, gm_all, 1)
        grad_qkv = over_tokens(g1_all, gproj, 0).reshape(-1, 3, z.LW)
        both = lax.psum(norms, ("dp", "sp", "tp"))
        both = both.reshape(2, 2, -1)
        return output, grad_input, grad_qkv, grad_out, grad_up, grad_down, both[0], both[1]

    return jax.shard_map(
        on_device,
        mesh=mesh,
        in_specs=(
            P(("sp", "tp"), "dp", None), P("dp", None), P("dp", None), P("dp", None), P(), P(), P(None, None, "tp"),
            P("tp", None), P(), P(), P(None, "tp"), P("tp", None), P(("sp", "tp"), "dp", None),
        ),
        out_specs=(
            P(("sp", "tp"), "dp", None), P(("sp", "tp"), "dp", None), P(("dp", "sp"), None, "tp"),
            P("tp", ("dp", "sp")), P(("dp", "sp"), "tp"), P("tp", ("dp", "sp")), P(), P(),
        ),
        check_vma=False,
    )
```

```python
import jax
import jax.numpy as jnp
from jax import lax
from jax.experimental import pallas as pl
from jax.experimental.pallas import tpu as pltpu
from jax.sharding import PartitionSpec as P

DH = 128
EPSILON = 1e-05
NEG = -1e30
f32 = jnp.float32
bf16 = jnp.bfloat16
MESH = pl.DeviceIdType.MESH


def dot(a, b, ca, cb):
    return lax.dot_general(a, b, (((ca,), (cb,)), ((), ())), preferred_element_type=f32)


def lanes(start, size):
    if isinstance(start, int):
        return pl.ds(start, size)
    return pl.ds(pl.multiple_of(start, 128), size)


def rows_at(start, size):
    if isinstance(start, int):
        return pl.ds(start, size)
    return pl.ds(pl.multiple_of(start, 64), size)


def norm_parts(values):
    average = jnp.mean(values, axis=-1, keepdims=True)
    centred = values - average
    variance = jnp.mean(centred * centred, axis=-1, keepdims=True)
    inverse = lax.rsqrt(variance + EPSILON)
    return centred * inverse, inverse


def norm_back(unit, inverse, gain, grad):
    scaled = grad * gain
    first = jnp.mean(scaled, axis=-1, keepdims=True)
    second = jnp.mean(scaled * unit, axis=-1, keepdims=True)
    return inverse * (scaled - first - unit * second)


class Sizes:
    def __init__(self, mesh_shape, tokens, w_qkv, w_up, lengths):
        self.n_dp = mesh_shape["dp"]
        self.n_sp = mesh_shape["sp"]
        self.n_tp = mesh_shape["tp"]
        self.S = tokens[0]
        self.R = tokens[1]
        self.D = tokens[2]
        self.LW = w_qkv[2]
        self.F = w_up[1]
        self.E = lengths[1]
        self.T = self.S * self.n_tp
        self.SEQ = self.T * self.n_sp
        self.H = self.LW // DH
        self.pairs = self.n_dp == 2 and self.n_sp == 4


def wgrad_kinds(z):
    half = z.F // 2
    out, offset = {}, 0
    for name, n, along in (
        ("d0", half, 5), ("d1", half, 5), ("u0", half, 6), ("u1", half, 6), ("out", z.LW, 6), ("q", z.LW, 4),
        ("kv", 2 * z.LW, 6),
    ):
        out[name] = (n, offset, n * along // 8)
        offset += n
    return out, offset


def make_kernel(z):
    S, R, D, LW, F, T, SEQ, H = z.S, z.R, z.D, z.LW, z.F, z.T, z.SEQ, z.H
    RT = R * T
    kinds, w_lanes = wgrad_kinds(z)
    scale = DH ** (-0.5)
    PD = D // 8

    def kernel(
        tok_hbm, og_hbm, lens, flags, eweight, g1, b1, g2, b2, wqkv_hbm, wout_hbm, wup_hbm, wdn_hbm,
        y_hbm, gin_hbm, norms_hbm, ro, rx, ry, sw, tx, ty, ph, g1h, extra_g2, extra_gy, extra_gm, extra_act, extra_gpre,
        extra_gproj, extra_att,
        arena, xact, xgy, wqkv, wout, ga, g2b, gyb, q, kv, act, gpre, gproj, att, part, part2, slots, slots2,
        mid, ds, stage, nr, total,
        ag_s, ag_r, rs_s, rs_r, kv_s, kv_r, dk_s, dk_r, x_s, x_r, w_s, w_r, n_s, n_r, loc, raw_sem, stg_sem,
        rt_sem, free_x, free_c, free_y,
        tok, og, y_out, gin, norms, io,
    ):
        dp = lax.axis_index("dp")
        sp = lax.axis_index("sp")
        tp = lax.axis_index("tp")
        par = lax.rem(sp, 2)
        yy = lax.div(sp, 2)
        mate = sp + 1 - 2 * par
        far = lax.rem(sp + 2, 4)
        odp = 1 - dp
        kv_row = sp * T
        own = tp * S

        def remote(src, dst, ssem, rsem, device):
            return pltpu.make_async_remote_copy(
                src_ref=src, dst_ref=dst, send_sem=ssem, recv_sem=rsem, device_id=device, device_id_type=MESH
            )

        HS = S // 2

        class Gather:
            def __init__(self, buf, i, r):
                self.buf, self.i, self.r = buf, i, r

            def copy(self, shard, way, hop, h):
                sl = self.buf.at[pl.ds(pl.multiple_of(self.r * T + shard * S + h * HS, HS), HS), :]
                to = tp + 1 if way == 0 else tp - 1
                return remote(
                    sl,
                    sl,
                    ag_s.at[self.i, self.r, way * 3 + hop, h],
                    ag_r.at[self.i, self.r, shard, h],
                    (dp, sp, to),
                )

            def start(self):
                for h in range(2):

                    @pl.when(tp < 3)
                    def _(h=h):
                        self.copy(tp, 0, 0, h).start()

                    @pl.when(tp > 0)
                    def _(h=h):
                        self.copy(tp, 1, 0, h).start()

            def step(self, hop):
                for h in range(2):

                    @pl.when(tp >= hop)
                    def _(h=h):
                        self.copy(tp - hop, 0, 0, h).wait_recv()

                    if hop < 3:

                        @pl.when((tp >= hop) & (tp < 3))
                        def _(h=h):
                            self.copy(tp - hop, 0, hop, h).start()

                    @pl.when(tp <= 3 - hop)
                    def _(h=h):
                        self.copy(tp + hop, 1, 0, h).wait_recv()

                    if hop < 3:

                        @pl.when((tp <= 3 - hop) & (tp > 0))
                        def _(h=h):
                            self.copy(tp + hop, 1, hop, h).start()

            def drain(self):
                for hop in range(3):

                    @pl.when((tp >= hop) & (tp < 3))
                    def _(hop=hop):
                        for h in range(2):
                            self.copy(tp - hop, 0, hop, h).wait_send()

                    @pl.when((tp <= 3 - hop) & (tp > 0))
                    def _(hop=hop):
                        for h in range(2):
                            self.copy(tp + hop, 1, hop, h).wait_send()

        class Scatter:
            def __init__(self, buf, box, i, r):
                self.buf, self.box, self.i, self.r = buf, box, i, r

            def place(self, way, k, h):
                o = 3 - k if way == 0 else k
                return pl.ds(self.r * T + o * S + h * HS, HS)

            def slot(self, way, k):
                return k if way == 0 else 4 - k

            def copy(self, way, k, h):
                to = tp + 1 if way == 0 else tp - 1
                n = way * 3 + k
                return remote(
                    self.buf.at[self.place(way, k, h), :],
                    self.box.at[self.r, self.slot(way, k), pl.ds(h * HS, HS), :],
                    rs_s.at[self.i, self.r, n, h],
                    rs_r.at[self.i, self.r, n, h],
                    (dp, sp, to),
                )

            def start(self):
                for k in range(3):

                    @pl.when(tp == 0)
                    def _(k=k):
                        for h in range(2):
                            self.copy(0, k, h).start()

                    @pl.when(tp == 3)
                    def _(k=k):
                        for h in range(2):
                            self.copy(1, k, h).start()

            def relay(self, way, k):
                for h in range(2):
                    sl = self.place(way, k, h)
                    self.copy(way, k, h).wait_recv()
                    self.buf[sl, :] = (
                        self.buf[sl, :].astype(f32)
                        + self.box[self.r, self.slot(way, k), h * HS : (h + 1) * HS].astype(f32)
                    ).astype(bf16)
                    self.copy(way, k, h).start()

            def step(self, k):
                first, second, n = (0, 1, k) if k < 2 else (1, 0, 0)

                @pl.when(tp == 1)
                def _():
                    self.relay(first, n)

                @pl.when(tp == 2)
                def _():
                    self.relay(second, n)

            def finish(self):
                total[...] = self.buf[rows_at(self.r * T + own, S), :].astype(f32)
                for way in range(2):
                    for k in range(3):

                        @pl.when(tp == (3 - k if way == 0 else k))
                        def _(way=way, k=k):
                            for h in range(2):
                                self.copy(way, k, h).wait_recv()
                            total[...] += self.box[self.r, self.slot(way, k)].astype(f32)

            def drain(self):
                for k in range(3):

                    @pl.when(tp < 3 - k)
                    def _(k=k):
                        for h in range(2):
                            self.copy(0, k, h).wait_send()

                    @pl.when(tp > k)
                    def _(k=k):
                        for h in range(2):
                            self.copy(1, k, h).wait_send()

        class Keys:
            def __init__(self, r):
                self.r = r

            def copy(self, block, to, n):
                sl = kv.at[self.r, rows_at(block * T, T), :]
                return remote(sl, sl, kv_s.at[self.r, n], kv_r.at[self.r, block], (dp, to, tp))

            def start(self):
                @pl.when(sp < 2)
                def _():
                    self.copy(sp, sp + 2, 0).start()

                @pl.when(par == 0)
                def _():
                    self.copy(sp, sp + 1, 1).start()

            def step(self):
                for me, block, to in ((2, 0, 3), (3, 1, 2)):

                    @pl.when(sp == me)
                    def _(block=block, to=to):
                        self.copy(block, to, 0).wait_recv()
                        self.copy(block, to, 2).start()

            def finish(self):
                for me, block in ((1, 0), (2, 1), (3, 0), (3, 2)):

                    @pl.when(sp == me)
                    def _(block=block):
                        self.copy(block, 0, 0).wait_recv()

            def drain(self):
                @pl.when(sp < 2)
                def _():
                    self.copy(sp, sp + 2, 0).wait_send()

                @pl.when(par == 0)
                def _():
                    self.copy(sp, sp + 1, 1).wait_send()

                for me, block, to in ((2, 0, 3), (3, 1, 2)):

                    @pl.when(sp == me)
                    def _(block=block, to=to):
                        self.copy(block, to, 2).wait_send()

        KW = 2 * LW
        DK0 = 5 * RT
        DR0 = RT

        class KeyGrads:
            def __init__(self, r):
                self.r = r

            def src(self, block):
                return arena.at[pl.ds(DK0 + block * T, T), pl.ds(self.r * KW, KW)]

            def dst(self, box):
                return arena.at[pl.ds(DR0 + box * T, T), pl.ds(self.r * KW, KW)]

            def copy(self, block, to, box, n):
                return remote(
                    self.src(block), self.dst(box), dk_s.at[self.r, n], dk_r.at[self.r, box], (dp, to, tp)
                )

            def start(self):
                for me, block, to, box, n in ((3, 0, 2, 0, 0), (3, 2, 2, 1, 1), (2, 1, 3, 0, 0), (1, 0, 0, 1, 0)):

                    @pl.when(sp == me)
                    def _(block=block, to=to, box=box, n=n):
                        self.copy(block, to, box, n).start()

            def step(self):
                for me, block, to in ((2, 0, 0), (3, 1, 1)):

                    @pl.when(sp == me)
                    def _(block=block, to=to):
                        self.copy(block, to, 0, 2).wait_recv()
                        mine = pl.ds(DK0 + block * T, T)
                        col = pl.ds(self.r * KW, KW)
                        arena[mine, col] = (
                            arena[mine, col].astype(f32) + arena[pl.ds(DR0, T), col].astype(f32)
                        ).astype(bf16)
                        self.copy(block, to, 2, 2).start()

            def finish(self):
                col = pl.ds(self.r * KW, KW)
                there = pl.ds(self.r * T, T)
                to = pl.ds(LW, KW)
                for me, boxes in ((0, (1, 2)), (1, (2,)), (2, (1,)), (3, ())):

                    @pl.when(sp == me)
                    def _(me=me, boxes=boxes):
                        value = arena[pl.ds(DK0 + me * T, T), col].astype(f32)
                        for box in boxes:
                            self.copy(0, 0, box, 0).wait_recv()
                            value += arena[pl.ds(DR0 + box * T, T), col].astype(f32)
                        gproj[there, to] = value.astype(bf16)

            def drain(self):
                for me, block, to, box, n in (
                    (3, 0, 2, 0, 0), (3, 2, 2, 1, 1), (2, 1, 3, 0, 0), (1, 0, 0, 1, 0), (2, 0, 0, 2, 2), (3, 1, 1, 2, 2),
                ):

                    @pl.when(sp == me)
                    def _(block=block, to=to, box=box, n=n):
                        self.copy(block, to, box, n).wait_send()

        ends = []
        for r in range(R):
            run, row = 0, []
            for e in range(z.E):
                run = run + lens[r, e]
                row.append(run)
            ends.append(row)

        def first_norm(r):
            unit, _ = norm_parts(tok[:, r, :].astype(f32))
            ga[rows_at(r * T + own, S), :] = (unit * g1[...] + b1[...]).astype(bf16)

        def weighted_grad(r):
            place = sp * T + own + lax.broadcasted_iota(jnp.int32, (S, 1), 0)
            factor = jnp.full((S, 1), eweight[r, 0] * (1.0 + flags[r, 0].astype(f32)), f32)
            for e in range(1, z.E):
                factor = jnp.where(
                    place >= ends[r][e - 1], eweight[r, e] * (1.0 + flags[r, e].astype(f32)), factor
                )
            return og[:, r, :].astype(f32) * factor

        def project(r, j):
            value = dot(ga[r * T : (r + 1) * T, :], wqkv[:, j * LW : (j + 1) * LW], 1, 0).astype(bf16)
            if j == 0:
                q[r * T : (r + 1) * T, :] = value
            else:
                kv[r, rows_at(kv_row, T), (j - 1) * LW : j * LW] = value

        def mask(r):
            here = kv_row + lax.broadcasted_iota(jnp.int32, (T, 1), 0)
            begin = jnp.zeros((T, 1), jnp.int32)
            for e in range(z.E):
                begin = jnp.where(here >= ends[r][e], jnp.maximum(begin, ends[r][e]), begin)
            there = lax.broadcasted_iota(jnp.int32, (T, SEQ), 1)
            ds[...] = jnp.where((there <= here) & (there >= begin), 0.0, NEG).astype(bf16)

        half = T // 2
        ppl = D // SEQ
        keep = [act, gpre]

        def attend(r):
            def one(i, carry):
                rs = rows_at(i * half, half)
                qs = rows_at(r * T + i * half, half)
                for h in range(H):
                    hs = slice(h * DH, (h + 1) * DH)
                    s = dot(q[qs, hs], kv[r, :, hs], 1, 1) * scale + ds[rs, :].astype(f32)
                    peak = jnp.max(s, axis=1, keepdims=True)
                    e = jnp.exp(s - peak)
                    p = (e * (1.0 / jnp.sum(e, axis=1, keepdims=True))).astype(bf16)
                    keep[r][rows_at((h // ppl) * T + i * half, half), (h % ppl) * SEQ : (h % ppl + 1) * SEQ] = p
                    att[qs, hs] = dot(p, kv[r, :, LW + h * DH : LW + (h + 1) * DH], 1, 0).astype(bf16)
                return carry

            lax.fori_loop(0, 2, one, 0)

        def times(lhs, r, weight, out, transposed):
            width = 512
            n = out.shape[1] // width

            def one(j, carry):
                cs = lanes(j * width, width)
                w = weight(j, width)
                out[r * T : (r + 1) * T, cs] = dot(lhs, w, 1, 1 if transposed else 0).astype(bf16)
                return carry

            lax.fori_loop(0, n, one, 0)

        def project_out(r):
            def one(j, carry):
                cs = lanes(j * 512, 512)
                part[r * T : (r + 1) * T, cs] = dot(att[r * T : (r + 1) * T, :], wout[:, cs], 1, 0).astype(bf16)
                return carry

            lax.fori_loop(0, D // 512, one, 0)

        def ffn_up(r, low, high):
            rs = slice(r * T, (r + 1) * T)

            def one(j, carry):
                cs = lanes(j * 256, 256)
                pre = dot(g2b[rs, :], arena[0:D, cs], 1, 0)
                e = 0.5 * (1.0 + lax.erf(pre * 0.7071067811865476))
                act[rs, cs] = (pre * e).astype(bf16)
                gpre[rs, cs] = (e + pre * (jnp.exp(-0.5 * pre * pre) * 0.3989422804014327)).astype(bf16)
                return carry

            lax.fori_loop(low, high, one, 0)

        def ffn_slope(r, low, high):
            rs = slice(r * T, (r + 1) * T)

            def one(j, carry):
                cs = lanes(j * 256, 256)
                back = dot(gyb[rs, :], arena[rows_at(D + j * 256, 256), :], 1, 1)
                gpre[rs, cs] = (back * gpre[rs, cs].astype(f32)).astype(bf16)
                return carry

            lax.fori_loop(low, high, one, 0)

        def ffn_back(r):
            rs = slice(r * T, (r + 1) * T)

            def one(j, carry):
                part[rs, lanes(j * 512, 512)] = dot(gpre[rs, :], arena[rows_at(j * 512, 512), :], 1, 1).astype(bf16)
                return carry

            lax.fori_loop(0, D // 512, one, 0)

        def ffn_out(r):
            rs = slice(r * T, (r + 1) * T)

            def one(j, carry):
                cs = lanes(j * 512, 512)
                part2[rs, cs] = dot(act[rs, :], arena[D : D + F, cs], 1, 0).astype(bf16)
                return carry

            lax.fori_loop(0, D // 512, one, 0)

        def second_norm(r):
            value = tok[:, r, :].astype(f32) + total[...]
            mid[r] = value
            unit, _ = norm_parts(value)
            g2b[rows_at(r * T + own, S), :] = (unit * g2[...] + b2[...]).astype(bf16)

        def add_norms(grad, unit):
            sums = (jnp.sum(grad * unit, axis=0, keepdims=True), jnp.sum(grad, axis=0, keepdims=True))
            for i in range(8):
                piece = sums[i // 4][:, (i % 4) * (D // 4) : (i % 4 + 1) * (D // 4)]
                nr[0, pl.ds(tp, 1), 8 + i : 9 + i, :] += piece[None]

        def second_norm_back(r):
            unit, inverse = norm_parts(mid[r])
            grad = total[...]
            add_norms(grad, unit)
            value = weighted_grad(r) + norm_back(unit, inverse, g2[...], grad)
            gin[r] = value
            ga[rows_at(r * T + own, S), :] = value.astype(bf16)

        def first_norm_back(r):
            unit, inverse = norm_parts(tok[:, r, :].astype(f32))
            grad = total[...]
            gin[r] = gin[r] + norm_back(unit, inverse, g1[...], grad)

        def attend_back(r):
            rows = slice(r * T, (r + 1) * T)

            def one(h, carry):
                hs, vs = lanes(h * DH, DH), lanes(LW + h * DH, DH)
                top = lax.div(h, ppl) * T
                pc = lanes(lax.rem(h, ppl) * SEQ, SEQ)
                for t in range(2):
                    gp = dot(gproj[r * T + t * half : r * T + (t + 1) * half, hs], kv[r, :, vs], 1, 1)
                    p = keep[r][rows_at(top + t * half, half), pc].astype(f32)
                    x = p * gp
                    delta = jnp.sum(x, axis=1, keepdims=True)
                    ds[t * half : (t + 1) * half, :] = ((x - p * delta) * scale).astype(bf16)
                arena[DK0 : DK0 + SEQ, lanes(r * KW + h * DH, DH)] = dot(ds[...], q[rows, hs], 0, 0).astype(bf16)
                arena[DK0 : DK0 + SEQ, lanes(r * KW + LW + h * DH, DH)] = dot(
                    keep[r][rows_at(top, T), pc], gproj[rows, hs], 0, 0
                ).astype(bf16)
                gproj[rows, hs] = dot(ds[...], kv[r, :, hs], 1, 0).astype(bf16)
                return carry

            lax.fori_loop(0, H, one, 0)

        def grad_attended(r):
            rows = slice(r * T, (r + 1) * T)
            gproj[rows, 0:LW] = dot(ga[rows, :], wout[...], 1, 1).astype(bf16)

        def qkv_back(r):
            rs = slice(r * T, (r + 1) * T)
            ns = slice(7 * RT + r * T, 7 * RT + (r + 1) * T)
            width = D // 4

            def one(j, carry):
                cs = lanes(j * width, width)
                value = dot(gproj[rs, :], wqkv[rows_at(j * width, width), :], 1, 1)
                part[rs, cs] = value.astype(bf16)
                normed = arena[ns, cs].astype(f32)
                nr[0, pl.ds(tp, 1), pl.ds(j, 1), :] += jnp.sum(value * normed, axis=0, keepdims=True)[None]
                nr[0, pl.ds(tp, 1), pl.ds(4 + j, 1), :] += jnp.sum(value, axis=0, keepdims=True)[None]
                return carry

            lax.fori_loop(0, 4, one, 0)

        load_tok = pltpu.make_async_copy(tok_hbm, tok, io.at[0])
        load_og = pltpu.make_async_copy(og_hbm, og, io.at[1])
        store_y = [pltpu.make_async_copy(y_out.at[r], y_hbm.at[r], io.at[2 + r]) for r in range(R)]
        store_gin = [pltpu.make_async_copy(gin.at[r], gin_hbm.at[r], io.at[4 + r]) for r in range(R)]
        store_norms = pltpu.make_async_copy(norms, norms_hbm, io.at[6])
        og_waits = [load_og]
        load_out = pltpu.make_async_copy(wout_hbm, wout, loc.at[0])
        load_qkv = [
            pltpu.make_async_copy(wqkv_hbm.at[j], wqkv.at[:, pl.ds(j * LW, LW)], raw_sem.at[j]) for j in range(3)
        ]
        load_up = pltpu.make_async_copy(wup_hbm, arena.at[pl.ds(0, D), :], loc.at[1])
        load_down = pltpu.make_async_copy(wdn_hbm, arena.at[pl.ds(D, F), :], loc.at[2])
        save_p = [pltpu.make_async_copy(keep[r], ph.at[r], loc.at[3 + r]) for r in range(R)]
        load_p = [pltpu.make_async_copy(ph.at[r], keep[r], loc.at[3 + r]) for r in range(R)]
        save_g1 = pltpu.make_async_copy(ga, g1h, loc.at[5])
        load_g1 = pltpu.make_async_copy(g1h, arena.at[pl.ds(7 * RT, RT), :], loc.at[5])

        XP, XG, XH, XJ = RT, 2 * RT, 3 * RT, 4 * RT
        there = (dp, mate, tp)
        oth = 1 - par

        def halves(buf, buf_row, size, box, box_row, box_lane, n):
            return [
                remote(
                    buf.at[pl.ds(buf_row, size), lanes(b * 2 * PD + oth * PD, PD)],
                    box.at[pl.ds(box_row, size), pl.ds(box_lane + b * PD, PD)],
                    x_s.at[n + b],
                    x_r.at[n + b],
                    there,
                )
                for b in range(4)
            ]

        def piece(buf, row, size, lane, width, box, box_row, box_lane, n):
            return [
                remote(
                    buf.at[pl.ds(row, size), pl.ds(lane, width)],
                    box.at[pl.ds(box_row, size), pl.ds(box_lane, width)],
                    x_s.at[n],
                    x_r.at[n],
                    there,
                )
            ]

        trade_rows = [[piece(act, r * T, T, h * F // 2, F // 2, xact, r * T, h * F // 2, 2 * h + r) for r in range(R)] for h in range(2)]
        trade_gy = [halves(gyb, r * T, T, xgy, r * T, 0, 22 + 4 * r) for r in range(R)]
        trade_up = piece(gpre, 0, RT, 0, F, arena, XP, 0, 21) + halves(g2b, 0, RT, arena, XG, 0, 6)
        trade_g1 = halves(arena, 7 * RT, RT, arena, XH, 0, 10)
        trade_out = piece(att, 0, RT, 0, LW, arena, XJ, 3 * LW, 18) + halves(ga, 0, RT, arena, XH, D // 2, 14)
        trade_q = piece(gproj, 0, RT, 0, LW, arena, XJ, 0, 19)
        trade_kv = piece(gproj, 0, RT, LW, 2 * LW, arena, XJ, LW, 20)

        names = list(kinds)
        operands = {
            "d0": ((gyb, 0), (act, 0), (xgy, 0, 0), (xact, 0, 0)),
            "d1": ((gyb, 0), (act, F // 2), (xgy, 0, 0), (xact, 0, F // 2)),
            "u0": ((g2b, 0), (gpre, 0), (arena, XG, 0), (arena, XP, 0)),
            "u1": ((g2b, 0), (gpre, F // 2), (arena, XG, 0), (arena, XP, F // 2)),
            "out": ((ga, 0), (att, 0), (arena, XH, D // 2), (arena, XJ, 3 * LW)),
            "q": ((arena, 7 * RT), (gproj, 0), (arena, XH, 0), (arena, XJ, 0)),
            "kv": ((arena, 7 * RT), (gproj, LW), (arena, XH, 0), (arena, XJ, LW)),
        }

        def tile(t, way, size):
            if way == 0:
                return arena.at[pl.ds(0, PD), pl.ds((t % 2) * (D // 2), size)]
            return arena.at[pl.ds(XG + PD, PD), pl.ds(D // 2 + (t % 2) * (D // 4), size)]

        def w_copy(name, which):
            t = names.index(name)
            n, off, a = kinds[name]
            ca, cb = pl.ds(off, a), pl.ds(off + a, n - a)
            x_to, y_to = (odp, sp, tp), (dp, far, tp)
            src, dst, to = {
                "S2": (sw.at[0, :, ca], tx.at[:, ca], x_to),
                "S4": (sw.at[0, :, cb], ty.at[:, cb], y_to),
                "S1": (sw.at[1, :, ca], rx.at[:, ca], x_to),
                "S3": (sw.at[2, :, cb], ry.at[:, cb], y_to),
                "R1": (tile(t, 0, a), ry.at[:, ca], y_to),
                "R2": (tile(t, 1, n - a), rx.at[:, cb], x_to),
            }[which]
            k = ("S1", "S2", "S3", "S4", "R1", "R2").index(which)
            return remote(src, dst, w_s.at[t, k], w_r.at[t, k], to)

        def weight_grad(name):
            (own_d, own_row), (own_r, own_lane), (mate_d, d_row, d_lane), (mate_r, r_row, r_lane) = operands[name]
            n, off, _ = kinds[name]
            own_r = own_r.at[:, pl.ds(own_lane, n)]
            mate_r = mate_r.at[pl.ds(r_row, RT), pl.ds(r_lane, n)]

            def staged(i, dst):
                slot = lax.rem(i, 2)
                return pltpu.make_async_copy(
                    stage.at[slot, :, pl.ds(0, n)], dst.at[:, pl.ds(off, n)], stg_sem.at[slot]
                )

            def one(i, carry):
                b4 = jnp.where(i < 2, odp, dp) * 2 + jnp.where(lax.rem(i, 2) == 0, 1 - yy, yy)
                value = dot(own_d[own_row : own_row + RT, lanes(b4 * 2 * PD + par * PD, PD)], own_r[...], 0, 0)
                value += dot(mate_d[d_row : d_row + RT, lanes(d_lane + b4 * PD, PD)], mate_r[...], 0, 0)
                stage[lax.rem(i, 2), :, 0:n] = value.astype(bf16)

                @pl.when(i < 3)
                def _():
                    staged(i, sw.at[i]).start()

                @pl.when(i == 3)
                def _():
                    staged(i, ro).start()

                @pl.when(i > 0)
                def _():
                    staged(i - 1, sw.at[i - 1]).wait()

                for k, which in ((1, "S2"), (2, "S1")):

                    @pl.when(i == k)
                    def _(which=which):
                        w_copy(name, which).start()

                return carry

            lax.fori_loop(0, 4, one, 0)
            staged(3, ro).wait()

        def relay_sum(name, way):
            t = names.index(name)
            n, off, a = kinds[name]
            first, size, box, block, need, send = (
                (0, a, tx, 2, "S2", "R1") if way == 0 else (a, n - a, ty, 1, "S4", "R2")
            )
            if t > 1:
                w_copy(names[t - 2], send).wait_send()
            there_l = pl.ds(off + first, size)
            mine, met = tile(t, way, size), arena.at[pl.ds(PD, PD), pl.ds(0, size)]
            own_c = pltpu.make_async_copy(sw.at[block, :, there_l], mine, rt_sem.at[way])
            got_c = pltpu.make_async_copy(box.at[:, there_l], met, rt_sem.at[2 + way])
            own_c.start()
            w_copy(name, need).wait_recv()
            got_c.start()
            own_c.wait()
            got_c.wait()
            mine[...] = (mine[...].astype(f32) + met[...].astype(f32)).astype(bf16)
            w_copy(name, send).start()

        def finish_sums(name):
            for which in ("S1", "S3", "R1", "R2"):
                w_copy(name, which).wait_recv()
            for which in ("S1", "S2", "S3", "S4"):
                w_copy(name, which).wait_send()
            if names.index(name) >= len(names) - 2:
                w_copy(name, "R1").wait_send()
                w_copy(name, "R2").wait_send()

        norm_axes = ((4, tp), (4, sp), (z.n_dp, dp))

        def norm_copies(i):
            axis_n, index = norm_axes[i]
            slot = nr.at[i, pl.ds(index, 1)]
            copies = []
            for d in range(1, axis_n):
                to = lax.rem(index + d, axis_n)
                device = ((dp, sp, to), (dp, to, tp), (to, sp, tp))[i]
                copies.append(remote(slot, slot, n_s.at[i, d - 1], n_r.at[i, d - 1], device))
            return copies

        def norm_result(value):
            norms[4:16, :] = value[4:16, :]
            for i in range(4):
                cs = slice(i * (D // 4), (i + 1) * (D // 4))
                norms[i : i + 1, :] = (value[i : i + 1, :] - b1[:, cs] * value[4 + i : 5 + i, :]) / g1[:, cs]
            store_norms.start()

        def norm_add(i):
            for c in norm_copies(i):
                c.wait_send()
                c.wait_recv()
            value = nr[i, 0]
            for n in range(1, norm_axes[i][0]):
                value = value + nr[i, n]
            return value

        load_tok.start()
        load_og.start()
        load_out.start()
        for c in load_qkv:
            c.start()
        barrier = pltpu.get_barrier_semaphore()
        greet = [(dp, sp, lax.rem(tp + d, 4)) for d in (1, 2, 3)]
        greet += [(dp, lax.rem(sp + d, 4), tp) for d in (1, 2, 3)]
        if z.pairs:
            greet += [(odp, sp, tp)]
        for device in greet:
            pl.semaphore_signal(barrier, inc=1, device_id=device, device_id_type=MESH)
        load_tok.wait()
        first_norm(0)
        pl.semaphore_wait(barrier, len(greet))

        ag1 = [Gather(ga, 0, r) for r in range(R)]
        ag2 = [Gather(g2b, 1, r) for r in range(R)]
        ag3 = [Gather(gyb, 2, r) for r in range(R)]
        ag4 = [Gather(ga, 3, r) for r in range(R)]
        rs1 = [Scatter(part, slots, 0, r) for r in range(R)]
        rs3 = [Scatter(part, slots, 1, r) for r in range(R)]
        rs4 = [Scatter(part, slots, 2, r) for r in range(R)]
        rs2 = [Scatter(part2, slots2, 3, r) for r in range(R)]
        keys = [Keys(r) for r in range(R)]
        kgrads = [KeyGrads(r) for r in range(R)]

        def grad_rows(r):
            while og_waits:
                og_waits.pop().wait()
            gyb[rows_at(r * T + own, S), :] = weighted_grad(r).astype(bf16)

        def clear():
            nr[0, pl.ds(tp, 1)] = jnp.zeros((1,) + nr.shape[2:], f32)
            for b in range(1, 4):

                @pl.when(b > sp)
                def _(b=b):
                    kv[:, b * T : (b + 1) * T, :] = jnp.zeros((R, T, KW), bf16)

        def keys_out(r):
            if r == 0:
                for c in load_qkv:
                    c.wait()
            project(r, 1)
            project(r, 2)
            keys[r].start()

        def queries(r):
            project(r, 0)

        def attention(r):
            attend(r)
            save_p[r].start()
            if r == 0:
                load_out.wait()
            project_out(r)
            rs1[r].start()

        def sum_one(r):
            rs1[r].finish()
            second_norm(r)
            ag2[r].start()

        def before_ffn():
            load_up.wait()
            load_down.wait()
            save_g1.wait()
            for c in save_p:
                c.wait()
            for g in ag1:
                g.drain()

        def up_a(r):
            ffn_up(r, 0, F // 512)

        def up_b(r):
            ffn_up(r, F // 512, F // 256)

        def back_a(r):
            ffn_slope(r, 0, F // 512)

        def back_b(r):
            ffn_slope(r, F // 512, F // 256)

        def ffn_c(r):
            rs1[r].drain()
            ffn_back(r)
            rs3[r].start()

        def sum_three(r):
            rs3[r].finish()
            second_norm_back(r)
            ag4[r].start()

        def sum_two(r):
            rs2[r].finish()
            y_out[r] = (mid[r] + total[...]).astype(bf16)
            store_y[r].start()

        def sum_four(r):
            rs4[r].finish()
            first_norm_back(r)
            store_gin[r].start()

        def offer():
            if z.pairs:
                pl.semaphore_signal(free_x, inc=1, device_id=there, device_id_type=MESH)

        def trade_act(h, r):
            if z.pairs:
                for c in trade_rows[h][r]:
                    c.start()

        def trade_grad(r):
            if z.pairs:
                for c in trade_gy[r]:
                    c.start()

        def trade_one():
            if z.pairs:
                pl.semaphore_wait(free_x, 1)
                for c in trade_up:
                    c.start()

        def grads_down(h):
            if z.pairs:
                for c in trade_rows[h][0] + trade_rows[h][1] + (trade_gy[0] + trade_gy[1] if h == 0 else []):
                    c.wait_recv()
                weight_grad(names[h])

        def grads_up(h):
            if z.pairs:
                if h == 0:
                    for c in trade_up:
                        c.wait_recv()
                weight_grad(names[2 + h])

        def offer_two():
            if z.pairs:
                for c in trade_rows[0][0] + trade_rows[0][1] + trade_rows[1][0] + trade_rows[1][1] + trade_gy[0] + trade_gy[1] + trade_up:
                    c.wait_send()
            else:
                dumps = [
                    pltpu.make_async_copy(act, extra_act, stg_sem.at[0]),
                    pltpu.make_async_copy(gpre, extra_gpre, stg_sem.at[1]),
                    pltpu.make_async_copy(g2b, extra_g2, rt_sem.at[0]),
                    pltpu.make_async_copy(gyb, extra_gy, rt_sem.at[1]),
                ]
                for c in dumps:
                    c.start()
                for c in dumps:
                    c.wait()
            pl.semaphore_signal(free_c, inc=1, device_id=there, device_id_type=MESH)
            pl.semaphore_signal(free_y, inc=1, device_id=(dp, far, tp), device_id_type=MESH)
            for c in load_p:
                c.start()

        def trade_two():
            load_g1.wait()
            if z.pairs:
                for c in trade_g1:
                    c.start()

        def attention_back(r):
            load_p[r].wait()
            attend_back(r)
            if r == 0:
                pl.semaphore_wait(free_c, 1)
            kgrads[r].start()

        def keys_back(r):
            if r == 0:
                pl.semaphore_wait(free_y, 1)
            kgrads[r].step()

        def keys_sum(r):
            kgrads[r].finish()

        def trade_three():
            if z.pairs:
                for c in trade_out:
                    c.start()

        def grads_out():
            if z.pairs:
                for c in trade_out:
                    c.wait_recv()
                weight_grad("out")

        def trade_four():
            if z.pairs:
                for c in trade_q:
                    c.start()

        def trade_five():
            if z.pairs:
                for c in trade_kv:
                    c.start()

        def grads_q():
            if z.pairs:
                for c in trade_g1 + trade_q:
                    c.wait_recv()
                weight_grad("q")

        def grads_kv():
            if z.pairs:
                for c in trade_kv:
                    c.wait_recv()
                weight_grad("kv")

        def push(i):
            if z.pairs:
                w_copy(names[i], "S4").start()
                w_copy(names[i], "S3").start()

        def pass_y(i):
            if z.pairs:
                relay_sum(names[i], 0)

        def pass_x(i):
            if z.pairs:
                relay_sum(names[i], 1)

        def back_c(r):
            rs3[r].drain()
            qkv_back(r)
            rs4[r].start()

        def norms_at(i):
            if not z.pairs:
                if i == 3:
                    norm_result(nr[0, pl.ds(tp, 1)][0])
                return
            if i:
                value = norm_add(i - 1)
                if i == 3:
                    norm_result(value)
                    return
                nr[i, pl.ds((sp, dp)[i - 1], 1)] = value[None]
            for c in norm_copies(i):
                c.start()

        def the_end():
            for c in store_y + store_gin + [store_norms]:
                c.wait()
            if z.pairs:
                for name in names:
                    finish_sums(name)
                for c in trade_g1 + trade_out + trade_q + trade_kv:
                    c.wait_send()
            else:
                dumps = [
                    pltpu.make_async_copy(ga, extra_gm, stg_sem.at[0]),
                    pltpu.make_async_copy(gproj, extra_gproj, stg_sem.at[1]),
                    pltpu.make_async_copy(att, extra_att, rt_sem.at[0]),
                ]
                for c in dumps:
                    c.start()
                for c in dumps:
                    c.wait()
            for g in keys + ag2 + ag3 + ag4 + rs2 + rs4 + kgrads:
                g.drain()

        ag1[0].start()
        mask(0)
        grad_rows(0)
        clear()
        first_norm(1)
        ag1[0].step(1)
        grad_rows(1)
        load_up.start()
        ag1[0].step(2)
        ag1[1].start()
        ag1[0].step(3)
        keys_out(0)
        queries(0)
        ag1[1].step(1)
        load_down.start()
        ag1[1].step(2)
        keys[0].step()
        ag3[0].start()
        keys[0].finish()
        attention(0)
        ag1[1].step(3)
        keys_out(1)
        queries(1)
        ag3[0].step(1)
        save_g1.start()
        keys[1].step()
        rs1[0].step(0)
        ag3[0].step(2)
        rs1[0].step(1)
        keys[1].finish()
        ag3[0].step(3)
        rs1[0].step(2)
        ag3[1].start()
        trade_grad(0)
        mask(1)
        sum_one(0)
        attention(1)
        ag2[0].step(1)
        rs1[1].step(0)
        ag2[0].step(2)
        ag2[0].step(3)
        before_ffn()
        up_a(0)
        back_a(0)
        rs1[1].step(1)
        rs1[1].step(2)
        trade_act(0, 0)
        up_b(0)
        ag3[1].step(1)
        trade_act(1, 0)
        sum_one(1)
        back_b(0)
        ffn_c(0)
        ag2[1].step(1)
        ffn_out(0)
        ag2[1].step(2)
        ag2[1].step(3)
        rs3[0].step(0)
        up_a(1)
        trade_act(0, 1)
        rs2[0].start()
        up_b(1)
        ag3[1].step(2)
        rs3[0].step(1)
        ag3[1].step(3)
        trade_grad(1)
        back_a(1)
        rs3[0].step(2)
        trade_act(1, 1)
        grads_down(0)
        push(0)
        back_b(1)
        sum_three(0)
        ffn_c(1)
        offer()
        pass_y(0)
        rs2[0].step(0)
        trade_one()
        grads_down(1)
        push(1)
        pass_x(0)
        ffn_out(1)
        ag4[0].step(1)
        grads_up(0)
        push(2)
        rs3[1].step(0)
        ag4[0].step(2)
        load_g1.start()
        pass_y(1)
        grads_up(1)
        rs3[1].step(1)
        rs3[1].step(2)
        ag4[0].step(3)
        grad_attended(0)
        offer_two()
        attention_back(0)
        sum_three(1)
        keys_back(0)
        trade_two()
        rs2[1].start()
        push(3)
        pass_x(2)
        pass_y(2)
        pass_x(1)
        ag4[1].step(1)
        rs2[0].step(1)
        keys_sum(0)
        ag4[1].step(2)
        back_c(0)
        rs2[0].step(2)
        ag4[1].step(3)
        grad_attended(1)
        rs2[1].step(0)
        attention_back(1)
        keys_back(1)
        trade_four()
        trade_three()
        rs2[1].step(1)
        rs2[1].step(2)
        pass_y(3)
        rs4[0].step(0)
        grads_q()
        grads_out()
        rs4[0].step(1)
        push(5)
        push(4)
        pass_x(3)
        keys_sum(1)
        trade_five()
        back_c(1)
        sum_two(1)
        grads_kv()
        push(6)
        rs4[0].step(2)
        norms_at(0)
        rs4[1].step(0)
        sum_two(0)
        pass_y(4)
        pass_x(4)
        rs4[1].step(1)
        pass_x(5)
        sum_four(0)
        pass_y(5)
        rs4[1].step(2)
        norms_at(1)
        pass_y(6)
        norms_at(2)
        pass_x(6)
        norms_at(3)
        sum_four(1)
        the_end()

    return kernel, w_lanes


def layer(z, tokens, out_grad, lengths, self_flags, episode_weight, g1, b1, g2, b2, w_qkv, w_out, w_up, w_down):
    S, R, D, LW, F, T, SEQ, H = z.S, z.R, z.D, z.LW, z.F, z.T, z.SEQ, z.H
    RT, PD = R * T, D // 8
    kernel, w_lanes = make_kernel(z)
    sds = jax.ShapeDtypeStruct
    any_, vmem, smem = (pl.BlockSpec(memory_space=m) for m in (pl.ANY, pltpu.VMEM, pltpu.SMEM))
    extra = (lambda *s: sds(s, bf16)) if not z.pairs else (lambda *s: sds((16, 128), bf16))
    pairs = (lambda *s: sds(s, bf16)) if z.pairs else (lambda *s: sds((16, 128), bf16))
    out_shape = [
        sds((R, S, D), bf16),
        sds((R, S, D), f32),
        sds((16, D // 4), f32),
        pairs(PD, w_lanes),
        pairs(PD, w_lanes),
        pairs(PD, w_lanes),
        pairs(3, PD, w_lanes),
        pairs(PD, w_lanes),
        pairs(PD, w_lanes),
        sds((R, RT, D), bf16),
        sds((RT, D), bf16),
        extra(RT, D),
        extra(RT, D),
        extra(RT, D),
        extra(RT, F),
        extra(RT, F),
        extra(RT, 3 * LW),
        extra(RT, LW),
    ]
    dma = pltpu.SemaphoreType.DMA
    reg = pltpu.SemaphoreType.REGULAR
    v = lambda *s: pltpu.VMEM(s, bf16)
    vf = lambda *s: pltpu.VMEM(s, f32)
    scratch = [
        v(D + F, D), v(RT, F), v(RT, D // 2), v(D, 3 * LW), v(LW, D), v(RT, D), v(RT, D), v(RT, D),
        v(RT, LW), v(R, SEQ, 2 * LW), v(RT, F), v(RT, F), v(RT, 3 * LW), v(RT, LW),
        v(RT, D), v(RT, D), v(R, 5, S, D), v(R, 5, S, D),
        vf(R, S, D), v(T, SEQ), v(2, PD, max(F, D) // 2), vf(3, 4, 16, D // 4), vf(S, D),
        dma((4, R, 6, 2)), dma((4, R, 4, 2)), dma((4, R, 6, 2)), dma((4, R, 6, 2)),
        dma((R, 3)), dma((R, 4)), dma((R, 3)), dma((R, 3)),
        dma((30,)), dma((30,)), dma((7, 6)), dma((7, 6)), dma((3, 3)), dma((3, 3)),
        dma((6,)), dma((3,)), dma((2,)), dma((4,)), reg, reg, reg,
        v(S, R, D), v(S, R, D), v(R, S, D), vf(R, S, D), vf(16, D // 4), dma((7,)),
    ]
    return pl.pallas_call(
        kernel,
        out_shape=out_shape,
        in_specs=[any_] * 2 + [smem] * 3 + [vmem] * 4 + [any_] * 4,
        out_specs=[any_] * 18,
        scratch_shapes=scratch,
        compiler_params=pltpu.CompilerParams(
            collective_id=0, has_side_effects=True, vmem_limit_bytes=64 * 2**20 - 2**16
        ),
        cost_estimate=pl.CostEstimate(flops=42 * 10**9, bytes_accessed=10**8, transcendentals=10**7),
    )(tokens, out_grad, lengths, self_flags, episode_weight, g1, b1, g2, b2, w_qkv, w_out, w_up, w_down)


def last_step(z, y, gin, norms, ro, rx, ry):
    S, R, D, LW, F, PD = z.S, z.R, z.D, z.LW, z.F, z.D // 8
    steps = 2
    wide, slim = F // steps, LW // steps
    offsets = [(wide, 0), (wide, steps)]
    base = 2 * F // slim
    offsets += [(slim, base + k * steps) for k in range(4)]

    def kernel(*refs):
        y_in, gin_in, norms_in = refs[:3]
        parts = refs[3:21]
        out, gout, qkv, proj, up, down, one, two = refs[21:]

        def total(k):
            return parts[k][...].astype(f32) + parts[6 + k][...].astype(f32) + parts[12 + k][...].astype(f32)

        down[...] = total(0).T
        up[...] = total(1)
        proj[...] = total(2).T
        for j in range(3):
            qkv[j] = total(3 + j)
        for r in range(R):
            gout[:, r, :] = gin_in[r]
        out[...] = jnp.stack([y_in[r].astype(f32) for r in range(R)], axis=1).astype(bf16)
        for k, ref in enumerate((one, two)):
            for i in range(8):
                ref[i // 4 : i // 4 + 1, (i % 4) * (D // 4) : (i % 4 + 1) * (D // 4)] = norms_in[k * 8 + i : k * 8 + i + 1, :]

    spec = pl.BlockSpec
    rows = spec((R, S // steps, D), lambda i: (0, i, 0))
    in_specs = [rows, rows, spec((16, D // 4), lambda i: (0, 0))]
    for _ in range(3):
        in_specs += [spec((PD, w), lambda i, o=o: (0, o + i)) for w, o in offsets]
    sds = jax.ShapeDtypeStruct
    return pl.pallas_call(
        kernel,
        grid=(steps,),
        out_shape=[
            sds((S, R, D), bf16), sds((S, R, D), f32), sds((3, PD, LW), f32), sds((LW, PD), f32), sds((PD, F), f32),
            sds((F, PD), f32), sds((2, D), f32), sds((2, D), f32),
        ],
        in_specs=in_specs,
        out_specs=[
            spec((S // steps, R, D), lambda i: (i, 0, 0)), spec((S // steps, R, D), lambda i: (i, 0, 0)),
            spec((3, PD, slim), lambda i: (0, 0, i)), spec((slim, PD), lambda i: (i, 0)),
            spec((PD, wide), lambda i: (0, i)), spec((wide, PD), lambda i: (i, 0)), spec((2, D), lambda i: (0, 0)),
            spec((2, D), lambda i: (0, 0)),
        ],
        compiler_params=pltpu.CompilerParams(vmem_limit_bytes=64 * 2**20 - 2**16),
    )(y, gin, norms, *([ro] * 6 + [rx] * 6 + [ry] * 6))


def solution(mesh):
    shape = dict(mesh.shape)

    def on_device(
        tokens, lengths, self_flags, episode_weight, ln1_gain, ln1_bias, w_qkv, w_out, ln2_gain, ln2_bias, w_up,
        w_down, out_grad,
    ):
        z = Sizes(shape, tokens.shape, w_qkv.shape, w_up.shape, lengths.shape)
        row = lambda a: a.reshape(1, -1)
        results = layer(
            z, tokens, out_grad, lengths, self_flags, episode_weight, row(ln1_gain), row(ln1_bias), row(ln2_gain),
            row(ln2_bias), jnp.transpose(w_qkv, (1, 0, 2)), w_out, w_up, w_down,
        )
        y, gin, norms, ro, rx, ry = results[:6]
        if z.pairs:
            output, grad_input, qkv, grad_out, grad_up, grad_down, one, two = last_step(z, y, gin, norms, ro, rx, ry)
            return output, grad_input, jnp.transpose(qkv, (1, 0, 2)), grad_out, grad_up, grad_down, one, two
        output = jnp.transpose(y, (1, 0, 2))
        grad_input = jnp.transpose(gin, (1, 0, 2))
        g1_all, g2_all, gy_all, gm_all, act, gpre, gproj, att = results[10:]

        def over_tokens(a, b, dim):
            value = jnp.einsum("ta,tb->ab", a, b, preferred_element_type=f32).astype(bf16)
            return lax.psum_scatter(value, ("dp", "sp"), scatter_dimension=dim, tiled=True).astype(f32)

        grad_down = over_tokens(act, gy_all, 1)
        grad_up = over_tokens(g2_all, gpre, 0)
        grad_out = over_tokens(att, gm_all, 1)
        grad_qkv = over_tokens(g1_all, gproj, 0).reshape(-1, 3, z.LW)
        both = lax.psum(norms, ("dp", "sp", "tp"))
        both = both.reshape(2, 2, -1)
        return output, grad_input, grad_qkv, grad_out, grad_up, grad_down, both[0], both[1]

    return jax.shard_map(
        on_device,
        mesh=mesh,
        in_specs=(
            P(("sp", "tp"), "dp", None), P("dp", None), P("dp", None), P("dp", None), P(), P(), P(None, None, "tp"),
            P("tp", None), P(), P(), P(None, "tp"), P("tp", None), P(("sp", "tp"), "dp", None),
        ),
        out_specs=(
            P(("sp", "tp"), "dp", None), P(("sp", "tp"), "dp", None), P(("dp", "sp"), None, "tp"),
            P("tp", ("dp", "sp")), P(("dp", "sp"), "tp"), P("tp", ("dp", "sp")), P(), P(),
        ),
        check_vma=False,
    )
```

```python
import jax
import jax.numpy as jnp
from jax import lax
from jax.experimental import pallas as pl
from jax.experimental.pallas import tpu as pltpu
from jax.sharding import PartitionSpec as P

DH = 128
EPSILON = 1e-05
NEG = -1e30
f32 = jnp.float32
bf16 = jnp.bfloat16
MESH = pl.DeviceIdType.MESH


def dot(a, b, ca, cb):
    return lax.dot_general(a, b, (((ca,), (cb,)), ((), ())), preferred_element_type=f32)


def lanes(start, size):
    if isinstance(start, int):
        return pl.ds(start, size)
    return pl.ds(pl.multiple_of(start, 128), size)


def rows_at(start, size):
    if isinstance(start, int):
        return pl.ds(start, size)
    return pl.ds(pl.multiple_of(start, 64), size)


def norm_parts(values):
    average = jnp.mean(values, axis=-1, keepdims=True)
    centred = values - average
    variance = jnp.mean(centred * centred, axis=-1, keepdims=True)
    inverse = lax.rsqrt(variance + EPSILON)
    return centred * inverse, inverse


def norm_back(unit, inverse, gain, grad):
    scaled = grad * gain
    first = jnp.mean(scaled, axis=-1, keepdims=True)
    second = jnp.mean(scaled * unit, axis=-1, keepdims=True)
    return inverse * (scaled - first - unit * second)


class Sizes:
    def __init__(self, mesh_shape, tokens, w_qkv, w_up, lengths):
        self.n_dp = mesh_shape["dp"]
        self.n_sp = mesh_shape["sp"]
        self.n_tp = mesh_shape["tp"]
        self.S = tokens[0]
        self.R = tokens[1]
        self.D = tokens[2]
        self.LW = w_qkv[2]
        self.F = w_up[1]
        self.E = lengths[1]
        self.T = self.S * self.n_tp
        self.SEQ = self.T * self.n_sp
        self.H = self.LW // DH
        self.pairs = self.n_dp == 2 and self.n_sp == 4


def wgrad_kinds(z):
    half = z.F // 2
    out, offset = {}, 0
    for name, n, along in (
        ("d0", half, 5), ("d1", half, 5), ("u0", half, 6), ("u1", half, 6), ("out", z.LW, 6), ("q", z.LW, 4),
        ("kv", 2 * z.LW, 6),
    ):
        out[name] = (n, offset, n * along // 8)
        offset += n
    return out, offset


def make_kernel(z):
    S, R, D, LW, F, T, SEQ, H = z.S, z.R, z.D, z.LW, z.F, z.T, z.SEQ, z.H
    RT = R * T
    kinds, w_lanes = wgrad_kinds(z)
    scale = DH ** (-0.5)
    PD = D // 8

    def kernel(
        tok_hbm, og_hbm, lens, flags, eweight, g1, b1, g2, b2, wqkv_hbm, wout_hbm, wup_hbm, wdn_hbm,
        y_hbm, gin_hbm, norms_hbm, ro, rx, ry, sw, tx, ty, ph, g1h, extra_g2, extra_gy, extra_gm, extra_act, extra_gpre,
        extra_gproj, extra_att,
        arena, xact, xgy, wqkv, wout, ga, g2b, gyb, q, kv, act, gpre, gproj, att, part, part2, slots, slots2,
        mid, ds, stage, nr, total,
        ag_s, ag_r, rs_s, rs_r, kv_s, kv_r, dk_s, dk_r, x_s, x_r, w_s, w_r, n_s, n_r, loc, raw_sem, stg_sem,
        rt_sem, free_x, free_c, free_y,
        tok, og, y_out, gin, norms, io,
    ):
        dp = lax.axis_index("dp")
        sp = lax.axis_index("sp")
        tp = lax.axis_index("tp")
        par = lax.rem(sp, 2)
        yy = lax.div(sp, 2)
        mate = sp + 1 - 2 * par
        far = lax.rem(sp + 2, 4)
        odp = 1 - dp
        kv_row = sp * T
        own = tp * S

        def remote(src, dst, ssem, rsem, device):
            return pltpu.make_async_remote_copy(
                src_ref=src, dst_ref=dst, send_sem=ssem, recv_sem=rsem, device_id=device, device_id_type=MESH
            )

        HS = S // 2

        class Gather:
            def __init__(self, buf, i, r):
                self.buf, self.i, self.r = buf, i, r

            def copy(self, shard, way, hop, h):
                sl = self.buf.at[pl.ds(pl.multiple_of(self.r * T + shard * S + h * HS, HS), HS), :]
                to = tp + 1 if way == 0 else tp - 1
                return remote(
                    sl,
                    sl,
                    ag_s.at[self.i, self.r, way * 3 + hop, h],
                    ag_r.at[self.i, self.r, shard, h],
                    (dp, sp, to),
                )

            def start(self):
                for h in range(2):

                    @pl.when(tp < 3)
                    def _(h=h):
                        self.copy(tp, 0, 0, h).start()

                    @pl.when(tp > 0)
                    def _(h=h):
                        self.copy(tp, 1, 0, h).start()

            def step(self, hop):
                for h in range(2):

                    @pl.when(tp >= hop)
                    def _(h=h):
                        self.copy(tp - hop, 0, 0, h).wait_recv()

                    if hop < 3:

                        @pl.when((tp >= hop) & (tp < 3))
                        def _(h=h):
                            self.copy(tp - hop, 0, hop, h).start()

                    @pl.when(tp <= 3 - hop)
                    def _(h=h):
                        self.copy(tp + hop, 1, 0, h).wait_recv()

                    if hop < 3:

                        @pl.when((tp <= 3 - hop) & (tp > 0))
                        def _(h=h):
                            self.copy(tp + hop, 1, hop, h).start()

            def drain(self):
                for hop in range(3):

                    @pl.when((tp >= hop) & (tp < 3))
                    def _(hop=hop):
                        for h in range(2):
                            self.copy(tp - hop, 0, hop, h).wait_send()

                    @pl.when((tp <= 3 - hop) & (tp > 0))
                    def _(hop=hop):
                        for h in range(2):
                            self.copy(tp + hop, 1, hop, h).wait_send()

        class Scatter:
            def __init__(self, buf, box, i, r):
                self.buf, self.box, self.i, self.r = buf, box, i, r

            def place(self, way, k, h):
                o = 3 - k if way == 0 else k
                return pl.ds(self.r * T + o * S + h * HS, HS)

            def slot(self, way, k):
                return k if way == 0 else 4 - k

            def copy(self, way, k, h):
                to = tp + 1 if way == 0 else tp - 1
                n = way * 3 + k
                return remote(
                    self.buf.at[self.place(way, k, h), :],
                    self.box.at[self.r, self.slot(way, k), pl.ds(h * HS, HS), :],
                    rs_s.at[self.i, self.r, n, h],
                    rs_r.at[self.i, self.r, n, h],
                    (dp, sp, to),
                )

            def start(self):
                for k in range(3):

                    @pl.when(tp == 0)
                    def _(k=k):
                        for h in range(2):
                            self.copy(0, k, h).start()

                    @pl.when(tp == 3)
                    def _(k=k):
                        for h in range(2):
                            self.copy(1, k, h).start()

            def relay(self, way, k):
                for h in range(2):
                    sl = self.place(way, k, h)
                    self.copy(way, k, h).wait_recv()
                    self.buf[sl, :] = (
                        self.buf[sl, :].astype(f32)
                        + self.box[self.r, self.slot(way, k), h * HS : (h + 1) * HS].astype(f32)
                    ).astype(bf16)
                    self.copy(way, k, h).start()

            def step(self, k):
                first, second, n = (0, 1, k) if k < 2 else (1, 0, 0)

                @pl.when(tp == 1)
                def _():
                    self.relay(first, n)

                @pl.when(tp == 2)
                def _():
                    self.relay(second, n)

            def finish(self):
                total[...] = self.buf[rows_at(self.r * T + own, S), :].astype(f32)
                for way in range(2):
                    for k in range(3):

                        @pl.when(tp == (3 - k if way == 0 else k))
                        def _(way=way, k=k):
                            for h in range(2):
                                self.copy(way, k, h).wait_recv()
                            total[...] += self.box[self.r, self.slot(way, k)].astype(f32)

            def drain(self):
                for k in range(3):

                    @pl.when(tp < 3 - k)
                    def _(k=k):
                        for h in range(2):
                            self.copy(0, k, h).wait_send()

                    @pl.when(tp > k)
                    def _(k=k):
                        for h in range(2):
                            self.copy(1, k, h).wait_send()

        class Keys:
            def __init__(self, r):
                self.r = r

            def copy(self, block, to, n):
                sl = kv.at[self.r, rows_at(block * T, T), :]
                return remote(sl, sl, kv_s.at[self.r, n], kv_r.at[self.r, block], (dp, to, tp))

            def start(self):
                @pl.when(sp < 2)
                def _():
                    self.copy(sp, sp + 2, 0).start()

                @pl.when(par == 0)
                def _():
                    self.copy(sp, sp + 1, 1).start()

            def step(self):
                for me, block, to in ((2, 0, 3), (3, 1, 2)):

                    @pl.when(sp == me)
                    def _(block=block, to=to):
                        self.copy(block, to, 0).wait_recv()
                        self.copy(block, to, 2).start()

            def finish(self):
                for me, block in ((1, 0), (2, 1), (3, 0), (3, 2)):

                    @pl.when(sp == me)
                    def _(block=block):
                        self.copy(block, 0, 0).wait_recv()

            def drain(self):
                @pl.when(sp < 2)
                def _():
                    self.copy(sp, sp + 2, 0).wait_send()

                @pl.when(par == 0)
                def _():
                    self.copy(sp, sp + 1, 1).wait_send()

                for me, block, to in ((2, 0, 3), (3, 1, 2)):

                    @pl.when(sp == me)
                    def _(block=block, to=to):
                        self.copy(block, to, 2).wait_send()

        KW = 2 * LW
        DK0 = 5 * RT
        DR0 = RT

        class KeyGrads:
            def __init__(self, r):
                self.r = r

            def src(self, block):
                return arena.at[pl.ds(DK0 + block * T, T), pl.ds(self.r * KW, KW)]

            def dst(self, box):
                return arena.at[pl.ds(DR0 + box * T, T), pl.ds(self.r * KW, KW)]

            def copy(self, block, to, box, n):
                return remote(
                    self.src(block), self.dst(box), dk_s.at[self.r, n], dk_r.at[self.r, box], (dp, to, tp)
                )

            def start(self):
                for me, block, to, box, n in ((3, 0, 2, 0, 0), (3, 2, 2, 1, 1), (2, 1, 3, 0, 0), (1, 0, 0, 1, 0)):

                    @pl.when(sp == me)
                    def _(block=block, to=to, box=box, n=n):
                        self.copy(block, to, box, n).start()

            def step(self):
                for me, block, to in ((2, 0, 0), (3, 1, 1)):

                    @pl.when(sp == me)
                    def _(block=block, to=to):
                        self.copy(block, to, 0, 2).wait_recv()
                        mine = pl.ds(DK0 + block * T, T)
                        col = pl.ds(self.r * KW, KW)
                        arena[mine, col] = (
                            arena[mine, col].astype(f32) + arena[pl.ds(DR0, T), col].astype(f32)
                        ).astype(bf16)
                        self.copy(block, to, 2, 2).start()

            def finish(self):
                col = pl.ds(self.r * KW, KW)
                there = pl.ds(self.r * T, T)
                to = pl.ds(LW, KW)
                for me, boxes in ((0, (1, 2)), (1, (2,)), (2, (1,)), (3, ())):

                    @pl.when(sp == me)
                    def _(me=me, boxes=boxes):
                        value = arena[pl.ds(DK0 + me * T, T), col].astype(f32)
                        for box in boxes:
                            self.copy(0, 0, box, 0).wait_recv()
                            value += arena[pl.ds(DR0 + box * T, T), col].astype(f32)
                        gproj[there, to] = value.astype(bf16)

            def drain(self):
                for me, block, to, box, n in (
                    (3, 0, 2, 0, 0), (3, 2, 2, 1, 1), (2, 1, 3, 0, 0), (1, 0, 0, 1, 0), (2, 0, 0, 2, 2), (3, 1, 1, 2, 2),
                ):

                    @pl.when(sp == me)
                    def _(block=block, to=to, box=box, n=n):
                        self.copy(block, to, box, n).wait_send()

        ends = []
        for r in range(R):
            run, row = 0, []
            for e in range(z.E):
                run = run + lens[r, e]
                row.append(run)
            ends.append(row)

        def first_norm(r):
            unit, _ = norm_parts(tok[:, r, :].astype(f32))
            ga[rows_at(r * T + own, S), :] = (unit * g1[...] + b1[...]).astype(bf16)

        def weighted_grad(r):
            place = sp * T + own + lax.broadcasted_iota(jnp.int32, (S, 1), 0)
            factor = jnp.full((S, 1), eweight[r, 0] * (1.0 + flags[r, 0].astype(f32)), f32)
            for e in range(1, z.E):
                factor = jnp.where(
                    place >= ends[r][e - 1], eweight[r, e] * (1.0 + flags[r, e].astype(f32)), factor
                )
            return og[:, r, :].astype(f32) * factor

        def project(r, j):
            value = dot(ga[r * T : (r + 1) * T, :], wqkv[:, j * LW : (j + 1) * LW], 1, 0).astype(bf16)
            if j == 0:
                q[r * T : (r + 1) * T, :] = value
            else:
                kv[r, rows_at(kv_row, T), (j - 1) * LW : j * LW] = value

        def mask(r):
            here = kv_row + lax.broadcasted_iota(jnp.int32, (T, 1), 0)
            begin = jnp.zeros((T, 1), jnp.int32)
            for e in range(z.E):
                begin = jnp.where(here >= ends[r][e], jnp.maximum(begin, ends[r][e]), begin)
            there = lax.broadcasted_iota(jnp.int32, (T, SEQ), 1)
            ds[...] = jnp.where((there <= here) & (there >= begin), 0.0, NEG).astype(bf16)

        half = T // 2
        ppl = D // SEQ
        keep = [act, gpre]

        def attend(r):
            def one(i, carry):
                rs = rows_at(i * half, half)
                qs = rows_at(r * T + i * half, half)
                for h in range(H):
                    hs = slice(h * DH, (h + 1) * DH)
                    s = dot(q[qs, hs], kv[r, :, hs], 1, 1) * scale + ds[rs, :].astype(f32)
                    peak = jnp.max(s, axis=1, keepdims=True)
                    e = jnp.exp(s - peak)
                    p = (e * (1.0 / jnp.sum(e, axis=1, keepdims=True))).astype(bf16)
                    keep[r][rows_at((h // ppl) * T + i * half, half), (h % ppl) * SEQ : (h % ppl + 1) * SEQ] = p
                    att[qs, hs] = dot(p, kv[r, :, LW + h * DH : LW + (h + 1) * DH], 1, 0).astype(bf16)
                return carry

            lax.fori_loop(0, 2, one, 0)

        def times(lhs, r, weight, out, transposed):
            width = 512
            n = out.shape[1] // width

            def one(j, carry):
                cs = lanes(j * width, width)
                w = weight(j, width)
                out[r * T : (r + 1) * T, cs] = dot(lhs, w, 1, 1 if transposed else 0).astype(bf16)
                return carry

            lax.fori_loop(0, n, one, 0)

        def project_out(r):
            def one(j, carry):
                cs = lanes(j * 512, 512)
                part[r * T : (r + 1) * T, cs] = dot(att[r * T : (r + 1) * T, :], wout[:, cs], 1, 0).astype(bf16)
                return carry

            lax.fori_loop(0, D // 512, one, 0)

        def ffn_up(r, low, high):
            rs = slice(r * T, (r + 1) * T)

            def one(j, carry):
                cs = lanes(j * 256, 256)
                pre = dot(g2b[rs, :], arena[0:D, cs], 1, 0)
                e = 0.5 * (1.0 + lax.erf(pre * 0.7071067811865476))
                act[rs, cs] = (pre * e).astype(bf16)
                gpre[rs, cs] = (e + pre * (jnp.exp(-0.5 * pre * pre) * 0.3989422804014327)).astype(bf16)
                return carry

            lax.fori_loop(low, high, one, 0)

        def ffn_slope(r, low, high):
            rs = slice(r * T, (r + 1) * T)

            def one(j, carry):
                cs = lanes(j * 256, 256)
                back = dot(gyb[rs, :], arena[rows_at(D + j * 256, 256), :], 1, 1)
                gpre[rs, cs] = (back * gpre[rs, cs].astype(f32)).astype(bf16)
                return carry

            lax.fori_loop(low, high, one, 0)

        def ffn_back(r):
            rs = slice(r * T, (r + 1) * T)

            def one(j, carry):
                part[rs, lanes(j * 512, 512)] = dot(gpre[rs, :], arena[rows_at(j * 512, 512), :], 1, 1).astype(bf16)
                return carry

            lax.fori_loop(0, D // 512, one, 0)

        def ffn_out(r):
            rs = slice(r * T, (r + 1) * T)

            def one(j, carry):
                cs = lanes(j * 512, 512)
                part2[rs, cs] = dot(act[rs, :], arena[D : D + F, cs], 1, 0).astype(bf16)
                return carry

            lax.fori_loop(0, D // 512, one, 0)

        def second_norm(r):
            value = tok[:, r, :].astype(f32) + total[...]
            mid[r] = value
            unit, _ = norm_parts(value)
            g2b[rows_at(r * T + own, S), :] = (unit * g2[...] + b2[...]).astype(bf16)

        def add_norms(grad, unit):
            sums = (jnp.sum(grad * unit, axis=0, keepdims=True), jnp.sum(grad, axis=0, keepdims=True))
            for i in range(8):
                piece = sums[i // 4][:, (i % 4) * (D // 4) : (i % 4 + 1) * (D // 4)]
                nr[0, pl.ds(tp, 1), 8 + i : 9 + i, :] += piece[None]

        def second_norm_back(r):
            unit, inverse = norm_parts(mid[r])
            grad = total[...]
            add_norms(grad, unit)
            value = weighted_grad(r) + norm_back(unit, inverse, g2[...], grad)
            gin[r] = value
            ga[rows_at(r * T + own, S), :] = value.astype(bf16)

        def first_norm_back(r):
            unit, inverse = norm_parts(tok[:, r, :].astype(f32))
            grad = total[...]
            gin[r] = gin[r] + norm_back(unit, inverse, g1[...], grad)

        def attend_back(r):
            rows = slice(r * T, (r + 1) * T)

            def one(h, carry):
                hs, vs = lanes(h * DH, DH), lanes(LW + h * DH, DH)
                top = lax.div(h, ppl) * T
                pc = lanes(lax.rem(h, ppl) * SEQ, SEQ)
                for t in range(2):
                    gp = dot(gproj[r * T + t * half : r * T + (t + 1) * half, hs], kv[r, :, vs], 1, 1)
                    p = keep[r][rows_at(top + t * half, half), pc].astype(f32)
                    x = p * gp
                    delta = jnp.sum(x, axis=1, keepdims=True)
                    ds[t * half : (t + 1) * half, :] = ((x - p * delta) * scale).astype(bf16)
                arena[DK0 : DK0 + SEQ, lanes(r * KW + h * DH, DH)] = dot(ds[...], q[rows, hs], 0, 0).astype(bf16)
                arena[DK0 : DK0 + SEQ, lanes(r * KW + LW + h * DH, DH)] = dot(
                    keep[r][rows_at(top, T), pc], gproj[rows, hs], 0, 0
                ).astype(bf16)
                gproj[rows, hs] = dot(ds[...], kv[r, :, hs], 1, 0).astype(bf16)
                return carry

            lax.fori_loop(0, H, one, 0)

        def grad_attended(r):
            rows = slice(r * T, (r + 1) * T)
            gproj[rows, 0:LW] = dot(ga[rows, :], wout[...], 1, 1).astype(bf16)

        def qkv_back(r):
            rs = slice(r * T, (r + 1) * T)
            ns = slice(7 * RT + r * T, 7 * RT + (r + 1) * T)
            width = D // 4

            def one(j, carry):
                cs = lanes(j * width, width)
                value = dot(gproj[rs, :], wqkv[rows_at(j * width, width), :], 1, 1)
                part[rs, cs] = value.astype(bf16)
                normed = arena[ns, cs].astype(f32)
                nr[0, pl.ds(tp, 1), pl.ds(j, 1), :] += jnp.sum(value * normed, axis=0, keepdims=True)[None]
                nr[0, pl.ds(tp, 1), pl.ds(4 + j, 1), :] += jnp.sum(value, axis=0, keepdims=True)[None]
                return carry

            lax.fori_loop(0, 4, one, 0)

        load_tok = pltpu.make_async_copy(tok_hbm, tok, io.at[0])
        load_og = pltpu.make_async_copy(og_hbm, og, io.at[1])
        store_y = [pltpu.make_async_copy(y_out.at[r], y_hbm.at[r], io.at[2 + r]) for r in range(R)]
        store_gin = [pltpu.make_async_copy(gin.at[r], gin_hbm.at[r], io.at[4 + r]) for r in range(R)]
        store_norms = pltpu.make_async_copy(norms, norms_hbm, io.at[6])
        og_waits = [load_og]
        load_out = pltpu.make_async_copy(wout_hbm, wout, loc.at[0])
        load_qkv = [
            pltpu.make_async_copy(wqkv_hbm.at[j], wqkv.at[:, pl.ds(j * LW, LW)], raw_sem.at[j]) for j in range(3)
        ]
        load_up = pltpu.make_async_copy(wup_hbm, arena.at[pl.ds(0, D), :], loc.at[1])
        load_down = pltpu.make_async_copy(wdn_hbm, arena.at[pl.ds(D, F), :], loc.at[2])
        save_p = [pltpu.make_async_copy(keep[r], ph.at[r], loc.at[3 + r]) for r in range(R)]
        load_p = [pltpu.make_async_copy(ph.at[r], keep[r], loc.at[3 + r]) for r in range(R)]
        save_g1 = pltpu.make_async_copy(ga, g1h, loc.at[5])
        load_g1 = pltpu.make_async_copy(g1h, arena.at[pl.ds(7 * RT, RT), :], loc.at[5])

        XP, XG, XH, XJ = RT, 2 * RT, 3 * RT, 4 * RT
        there = (dp, mate, tp)
        oth = 1 - par

        def halves(buf, buf_row, size, box, box_row, box_lane, n):
            return [
                remote(
                    buf.at[pl.ds(buf_row, size), lanes(b * 2 * PD + oth * PD, PD)],
                    box.at[pl.ds(box_row, size), pl.ds(box_lane + b * PD, PD)],
                    x_s.at[n + b],
                    x_r.at[n + b],
                    there,
                )
                for b in range(4)
            ]

        def piece(buf, row, size, lane, width, box, box_row, box_lane, n):
            return [
                remote(
                    buf.at[pl.ds(row, size), pl.ds(lane, width)],
                    box.at[pl.ds(box_row, size), pl.ds(box_lane, width)],
                    x_s.at[n],
                    x_r.at[n],
                    there,
                )
            ]

        trade_rows = [[piece(act, r * T, T, h * F // 2, F // 2, xact, r * T, h * F // 2, 2 * h + r) for r in range(R)] for h in range(2)]
        trade_gy = [halves(gyb, r * T, T, xgy, r * T, 0, 22 + 4 * r) for r in range(R)]
        trade_up = piece(gpre, 0, RT, 0, F, arena, XP, 0, 21) + halves(g2b, 0, RT, arena, XG, 0, 6)
        trade_g1 = halves(arena, 7 * RT, RT, arena, XH, 0, 10)
        trade_out = piece(att, 0, RT, 0, LW, arena, XJ, 3 * LW, 18) + halves(ga, 0, RT, arena, XH, D // 2, 14)
        trade_q = piece(gproj, 0, RT, 0, LW, arena, XJ, 0, 19)
        trade_kv = piece(gproj, 0, RT, LW, 2 * LW, arena, XJ, LW, 20)

        names = list(kinds)
        operands = {
            "d0": ((gyb, 0), (act, 0), (xgy, 0, 0), (xact, 0, 0)),
            "d1": ((gyb, 0), (act, F // 2), (xgy, 0, 0), (xact, 0, F // 2)),
            "u0": ((g2b, 0), (gpre, 0), (arena, XG, 0), (arena, XP, 0)),
            "u1": ((g2b, 0), (gpre, F // 2), (arena, XG, 0), (arena, XP, F // 2)),
            "out": ((ga, 0), (att, 0), (arena, XH, D // 2), (arena, XJ, 3 * LW)),
            "q": ((arena, 7 * RT), (gproj, 0), (arena, XH, 0), (arena, XJ, 0)),
            "kv": ((arena, 7 * RT), (gproj, LW), (arena, XH, 0), (arena, XJ, LW)),
        }

        def tile(t, way, size):
            if way == 0:
                return arena.at[pl.ds(0, PD), pl.ds((t % 2) * (D // 2), size)]
            return arena.at[pl.ds(XG + PD, PD), pl.ds(D // 2 + (t % 2) * (D // 4), size)]

        def w_copy(name, which):
            t = names.index(name)
            n, off, a = kinds[name]
            ca, cb = pl.ds(off, a), pl.ds(off + a, n - a)
            x_to, y_to = (odp, sp, tp), (dp, far, tp)
            src, dst, to = {
                "S2": (sw.at[0, :, ca], tx.at[:, ca], x_to),
                "S4": (sw.at[0, :, cb], ty.at[:, cb], y_to),
                "S1": (sw.at[1, :, ca], rx.at[:, ca], x_to),
                "S3": (sw.at[2, :, cb], ry.at[:, cb], y_to),
                "R1": (tile(t, 0, a), ry.at[:, ca], y_to),
                "R2": (tile(t, 1, n - a), rx.at[:, cb], x_to),
            }[which]
            k = ("S1", "S2", "S3", "S4", "R1", "R2").index(which)
            return remote(src, dst, w_s.at[t, k], w_r.at[t, k], to)

        def weight_grad(name):
            (own_d, own_row), (own_r, own_lane), (mate_d, d_row, d_lane), (mate_r, r_row, r_lane) = operands[name]
            n, off, _ = kinds[name]
            own_r = own_r.at[:, pl.ds(own_lane, n)]
            mate_r = mate_r.at[pl.ds(r_row, RT), pl.ds(r_lane, n)]

            def staged(i, dst):
                slot = lax.rem(i, 2)
                return pltpu.make_async_copy(
                    stage.at[slot, :, pl.ds(0, n)], dst.at[:, pl.ds(off, n)], stg_sem.at[slot]
                )

            def one(i, carry):
                b4 = jnp.where(i < 2, odp, dp) * 2 + jnp.where(lax.rem(i, 2) == 0, 1 - yy, yy)
                value = dot(own_d[own_row : own_row + RT, lanes(b4 * 2 * PD + par * PD, PD)], own_r[...], 0, 0)
                value += dot(mate_d[d_row : d_row + RT, lanes(d_lane + b4 * PD, PD)], mate_r[...], 0, 0)
                stage[lax.rem(i, 2), :, 0:n] = value.astype(bf16)

                @pl.when(i < 3)
                def _():
                    staged(i, sw.at[i]).start()

                @pl.when(i == 3)
                def _():
                    staged(i, ro).start()

                @pl.when(i > 0)
                def _():
                    staged(i - 1, sw.at[i - 1]).wait()

                for k, which in ((1, "S2"), (2, "S1")):

                    @pl.when(i == k)
                    def _(which=which):
                        w_copy(name, which).start()

                return carry

            lax.fori_loop(0, 4, one, 0)
            staged(3, ro).wait()

        def relay_sum(name, way):
            t = names.index(name)
            n, off, a = kinds[name]
            first, size, box, block, need, send = (
                (0, a, tx, 2, "S2", "R1") if way == 0 else (a, n - a, ty, 1, "S4", "R2")
            )
            if t > 1:
                w_copy(names[t - 2], send).wait_send()
            there_l = pl.ds(off + first, size)
            mine, met = tile(t, way, size), arena.at[pl.ds(PD, PD), pl.ds(0, size)]
            own_c = pltpu.make_async_copy(sw.at[block, :, there_l], mine, rt_sem.at[way])
            got_c = pltpu.make_async_copy(box.at[:, there_l], met, rt_sem.at[2 + way])
            own_c.start()
            w_copy(name, need).wait_recv()
            got_c.start()
            own_c.wait()
            got_c.wait()
            mine[...] = (mine[...].astype(f32) + met[...].astype(f32)).astype(bf16)
            w_copy(name, send).start()

        def finish_sums(name):
            for which in ("S1", "S3", "R1", "R2"):
                w_copy(name, which).wait_recv()
            for which in ("S1", "S2", "S3", "S4"):
                w_copy(name, which).wait_send()
            if names.index(name) >= len(names) - 2:
                w_copy(name, "R1").wait_send()
                w_copy(name, "R2").wait_send()

        norm_axes = ((4, tp), (4, sp), (z.n_dp, dp))

        def norm_copies(i):
            axis_n, index = norm_axes[i]
            slot = nr.at[i, pl.ds(index, 1)]
            copies = []
            for d in range(1, axis_n):
                to = lax.rem(index + d, axis_n)
                device = ((dp, sp, to), (dp, to, tp), (to, sp, tp))[i]
                copies.append(remote(slot, slot, n_s.at[i, d - 1], n_r.at[i, d - 1], device))
            return copies

        def norm_result(value):
            norms[4:16, :] = value[4:16, :]
            for i in range(4):
                cs = slice(i * (D // 4), (i + 1) * (D // 4))
                norms[i : i + 1, :] = (value[i : i + 1, :] - b1[:, cs] * value[4 + i : 5 + i, :]) / g1[:, cs]
            store_norms.start()

        def norm_add(i):
            for c in norm_copies(i):
                c.wait_send()
                c.wait_recv()
            value = nr[i, 0]
            for n in range(1, norm_axes[i][0]):
                value = value + nr[i, n]
            return value

        load_tok.start()
        load_og.start()
        barrier = pltpu.get_barrier_semaphore()
        greet = [(dp, sp, lax.rem(tp + d, 4)) for d in (1, 2, 3)]
        greet += [(dp, lax.rem(sp + d, 4), tp) for d in (1, 2, 3)]
        if z.pairs:
            greet += [(odp, sp, tp)]
        for device in greet:
            pl.semaphore_signal(barrier, inc=1, device_id=device, device_id_type=MESH)
        load_out.start()
        for c in load_qkv:
            c.start()
        load_tok.wait()
        first_norm(0)
        pl.semaphore_wait(barrier, len(greet))

        ag1 = [Gather(ga, 0, r) for r in range(R)]
        ag2 = [Gather(g2b, 1, r) for r in range(R)]
        ag3 = [Gather(gyb, 2, r) for r in range(R)]
        ag4 = [Gather(ga, 3, r) for r in range(R)]
        rs1 = [Scatter(part, slots, 0, r) for r in range(R)]
        rs3 = [Scatter(part, slots, 1, r) for r in range(R)]
        rs4 = [Scatter(part, slots, 2, r) for r in range(R)]
        rs2 = [Scatter(part2, slots2, 3, r) for r in range(R)]
        keys = [Keys(r) for r in range(R)]
        kgrads = [KeyGrads(r) for r in range(R)]

        def grad_rows(r):
            while og_waits:
                og_waits.pop().wait()
            gyb[rows_at(r * T + own, S), :] = weighted_grad(r).astype(bf16)

        def clear():
            nr[0, pl.ds(tp, 1)] = jnp.zeros((1,) + nr.shape[2:], f32)
            for b in range(1, 4):

                @pl.when(b > sp)
                def _(b=b):
                    kv[:, b * T : (b + 1) * T, :] = jnp.zeros((R, T, KW), bf16)

        def keys_out(r):
            if r == 0:
                for c in load_qkv:
                    c.wait()
            project(r, 1)
            project(r, 2)
            keys[r].start()

        def queries(r):
            project(r, 0)

        def attention(r):
            attend(r)
            save_p[r].start()
            if r == 0:
                load_out.wait()
            project_out(r)
            rs1[r].start()

        def sum_one(r):
            rs1[r].finish()
            second_norm(r)
            ag2[r].start()

        def before_ffn():
            load_up.wait()
            load_down.wait()
            save_g1.wait()
            for c in save_p:
                c.wait()
            for g in ag1:
                g.drain()

        def up_a(r):
            ffn_up(r, 0, F // 512)

        def up_b(r):
            ffn_up(r, F // 512, F // 256)

        def back_a(r):
            ffn_slope(r, 0, F // 512)

        def back_b(r):
            ffn_slope(r, F // 512, F // 256)

        def ffn_c(r):
            rs1[r].drain()
            ffn_back(r)
            rs3[r].start()

        def sum_three(r):
            rs3[r].finish()
            second_norm_back(r)
            ag4[r].start()

        def sum_two(r):
            rs2[r].finish()
            y_out[r] = (mid[r] + total[...]).astype(bf16)
            store_y[r].start()

        def sum_four(r):
            rs4[r].finish()
            first_norm_back(r)
            store_gin[r].start()

        def offer():
            if z.pairs:
                pl.semaphore_signal(free_x, inc=1, device_id=there, device_id_type=MESH)

        def trade_act(h, r):
            if z.pairs:
                for c in trade_rows[h][r]:
                    c.start()

        def trade_grad(r):
            if z.pairs:
                for c in trade_gy[r]:
                    c.start()

        def trade_one():
            if z.pairs:
                pl.semaphore_wait(free_x, 1)
                for c in trade_up:
                    c.start()

        def grads_down(h):
            if z.pairs:
                for c in trade_rows[h][0] + trade_rows[h][1] + (trade_gy[0] + trade_gy[1] if h == 0 else []):
                    c.wait_recv()
                weight_grad(names[h])

        def grads_up(h):
            if z.pairs:
                if h == 0:
                    for c in trade_up:
                        c.wait_recv()
                weight_grad(names[2 + h])

        def offer_two():
            if z.pairs:
                for c in trade_rows[0][0] + trade_rows[0][1] + trade_rows[1][0] + trade_rows[1][1] + trade_gy[0] + trade_gy[1] + trade_up:
                    c.wait_send()
            else:
                dumps = [
                    pltpu.make_async_copy(act, extra_act, stg_sem.at[0]),
                    pltpu.make_async_copy(gpre, extra_gpre, stg_sem.at[1]),
                    pltpu.make_async_copy(g2b, extra_g2, rt_sem.at[0]),
                    pltpu.make_async_copy(gyb, extra_gy, rt_sem.at[1]),
                ]
                for c in dumps:
                    c.start()
                for c in dumps:
                    c.wait()
            pl.semaphore_signal(free_c, inc=1, device_id=there, device_id_type=MESH)
            pl.semaphore_signal(free_y, inc=1, device_id=(dp, far, tp), device_id_type=MESH)
            for c in load_p:
                c.start()

        def trade_two():
            load_g1.wait()
            if z.pairs:
                for c in trade_g1:
                    c.start()

        def attention_back(r):
            load_p[r].wait()
            attend_back(r)
            if r == 0:
                pl.semaphore_wait(free_c, 1)
            kgrads[r].start()

        def keys_back(r):
            if r == 0:
                pl.semaphore_wait(free_y, 1)
            kgrads[r].step()

        def keys_sum(r):
            kgrads[r].finish()

        def trade_three():
            if z.pairs:
                for c in trade_out:
                    c.start()

        def grads_out():
            if z.pairs:
                for c in trade_out:
                    c.wait_recv()
                weight_grad("out")

        def trade_four():
            if z.pairs:
                for c in trade_q:
                    c.start()

        def trade_five():
            if z.pairs:
                for c in trade_kv:
                    c.start()

        def grads_q():
            if z.pairs:
                for c in trade_g1 + trade_q:
                    c.wait_recv()
                weight_grad("q")

        def grads_kv():
            if z.pairs:
                for c in trade_kv:
                    c.wait_recv()
                weight_grad("kv")

        def push(i):
            if z.pairs:
                w_copy(names[i], "S4").start()
                w_copy(names[i], "S3").start()

        def pass_y(i):
            if z.pairs:
                relay_sum(names[i], 0)

        def pass_x(i):
            if z.pairs:
                relay_sum(names[i], 1)

        def back_c(r):
            rs3[r].drain()
            qkv_back(r)
            rs4[r].start()

        def norms_at(i):
            if not z.pairs:
                if i == 3:
                    norm_result(nr[0, pl.ds(tp, 1)][0])
                return
            if i:
                value = norm_add(i - 1)
                if i == 3:
                    norm_result(value)
                    return
                nr[i, pl.ds((sp, dp)[i - 1], 1)] = value[None]
            for c in norm_copies(i):
                c.start()

        def the_end():
            for c in store_y + store_gin + [store_norms]:
                c.wait()
            if z.pairs:
                for name in names:
                    finish_sums(name)
                for c in trade_g1 + trade_out + trade_q + trade_kv:
                    c.wait_send()
            else:
                dumps = [
                    pltpu.make_async_copy(ga, extra_gm, stg_sem.at[0]),
                    pltpu.make_async_copy(gproj, extra_gproj, stg_sem.at[1]),
                    pltpu.make_async_copy(att, extra_att, rt_sem.at[0]),
                ]
                for c in dumps:
                    c.start()
                for c in dumps:
                    c.wait()
            for g in keys + ag2 + ag3 + ag4 + rs2 + rs4 + kgrads:
                g.drain()

        ag1[0].start()
        mask(0)
        grad_rows(0)
        clear()
        first_norm(1)
        ag1[0].step(1)
        grad_rows(1)
        load_up.start()
        ag1[0].step(2)
        ag1[1].start()
        ag1[0].step(3)
        keys_out(0)
        queries(0)
        ag1[1].step(1)
        load_down.start()
        ag1[1].step(2)
        keys[0].step()
        ag3[0].start()
        keys[0].finish()
        attention(0)
        ag1[1].step(3)
        keys_out(1)
        queries(1)
        ag3[0].step(1)
        save_g1.start()
        keys[1].step()
        rs1[0].step(0)
        ag3[0].step(2)
        rs1[0].step(1)
        keys[1].finish()
        ag3[0].step(3)
        rs1[0].step(2)
        ag3[1].start()
        trade_grad(0)
        mask(1)
        sum_one(0)
        attention(1)
        ag2[0].step(1)
        rs1[1].step(0)
        ag2[0].step(2)
        ag2[0].step(3)
        before_ffn()
        up_a(0)
        back_a(0)
        rs1[1].step(1)
        rs1[1].step(2)
        trade_act(0, 0)
        up_b(0)
        ag3[1].step(1)
        trade_act(1, 0)
        sum_one(1)
        back_b(0)
        ffn_c(0)
        ag2[1].step(1)
        ffn_out(0)
        ag2[1].step(2)
        ag2[1].step(3)
        rs3[0].step(0)
        up_a(1)
        trade_act(0, 1)
        rs2[0].start()
        up_b(1)
        ag3[1].step(2)
        rs3[0].step(1)
        ag3[1].step(3)
        trade_grad(1)
        back_a(1)
        rs3[0].step(2)
        trade_act(1, 1)
        grads_down(0)
        push(0)
        back_b(1)
        sum_three(0)
        ffn_c(1)
        offer()
        pass_y(0)
        rs2[0].step(0)
        trade_one()
        grads_down(1)
        push(1)
        pass_x(0)
        ffn_out(1)
        ag4[0].step(1)
        grads_up(0)
        push(2)
        rs3[1].step(0)
        ag4[0].step(2)
        load_g1.start()
        pass_y(1)
        grads_up(1)
        rs3[1].step(1)
        rs3[1].step(2)
        ag4[0].step(3)
        grad_attended(0)
        offer_two()
        attention_back(0)
        sum_three(1)
        keys_back(0)
        trade_two()
        rs2[1].start()
        push(3)
        pass_x(2)
        pass_y(2)
        pass_x(1)
        ag4[1].step(1)
        rs2[0].step(1)
        keys_sum(0)
        ag4[1].step(2)
        back_c(0)
        rs2[0].step(2)
        ag4[1].step(3)
        grad_attended(1)
        rs2[1].step(0)
        attention_back(1)
        keys_back(1)
        trade_four()
        trade_three()
        rs2[1].step(1)
        rs2[1].step(2)
        pass_y(3)
        rs4[0].step(0)
        grads_q()
        grads_out()
        rs4[0].step(1)
        push(5)
        push(4)
        pass_x(3)
        keys_sum(1)
        trade_five()
        back_c(1)
        sum_two(1)
        grads_kv()
        push(6)
        rs4[0].step(2)
        norms_at(0)
        rs4[1].step(0)
        sum_two(0)
        pass_y(4)
        pass_x(4)
        rs4[1].step(1)
        pass_x(5)
        sum_four(0)
        pass_y(5)
        rs4[1].step(2)
        norms_at(1)
        pass_y(6)
        norms_at(2)
        pass_x(6)
        norms_at(3)
        sum_four(1)
        the_end()

    return kernel, w_lanes


def layer(z, tokens, out_grad, lengths, self_flags, episode_weight, g1, b1, g2, b2, w_qkv, w_out, w_up, w_down):
    S, R, D, LW, F, T, SEQ, H = z.S, z.R, z.D, z.LW, z.F, z.T, z.SEQ, z.H
    RT, PD = R * T, D // 8
    kernel, w_lanes = make_kernel(z)
    sds = jax.ShapeDtypeStruct
    any_, vmem, smem = (pl.BlockSpec(memory_space=m) for m in (pl.ANY, pltpu.VMEM, pltpu.SMEM))
    extra = (lambda *s: sds(s, bf16)) if not z.pairs else (lambda *s: sds((16, 128), bf16))
    pairs = (lambda *s: sds(s, bf16)) if z.pairs else (lambda *s: sds((16, 128), bf16))
    out_shape = [
        sds((R, S, D), bf16),
        sds((R, S, D), f32),
        sds((16, D // 4), f32),
        pairs(PD, w_lanes),
        pairs(PD, w_lanes),
        pairs(PD, w_lanes),
        pairs(3, PD, w_lanes),
        pairs(PD, w_lanes),
        pairs(PD, w_lanes),
        sds((R, RT, D), bf16),
        sds((RT, D), bf16),
        extra(RT, D),
        extra(RT, D),
        extra(RT, D),
        extra(RT, F),
        extra(RT, F),
        extra(RT, 3 * LW),
        extra(RT, LW),
    ]
    dma = pltpu.SemaphoreType.DMA
    reg = pltpu.SemaphoreType.REGULAR
    v = lambda *s: pltpu.VMEM(s, bf16)
    vf = lambda *s: pltpu.VMEM(s, f32)
    scratch = [
        v(D + F, D), v(RT, F), v(RT, D // 2), v(D, 3 * LW), v(LW, D), v(RT, D), v(RT, D), v(RT, D),
        v(RT, LW), v(R, SEQ, 2 * LW), v(RT, F), v(RT, F), v(RT, 3 * LW), v(RT, LW),
        v(RT, D), v(RT, D), v(R, 5, S, D), v(R, 5, S, D),
        vf(R, S, D), v(T, SEQ), v(2, PD, max(F, D) // 2), vf(3, 4, 16, D // 4), vf(S, D),
        dma((4, R, 6, 2)), dma((4, R, 4, 2)), dma((4, R, 6, 2)), dma((4, R, 6, 2)),
        dma((R, 3)), dma((R, 4)), dma((R, 3)), dma((R, 3)),
        dma((30,)), dma((30,)), dma((7, 6)), dma((7, 6)), dma((3, 3)), dma((3, 3)),
        dma((6,)), dma((3,)), dma((2,)), dma((4,)), reg, reg, reg,
        v(S, R, D), v(S, R, D), v(R, S, D), vf(R, S, D), vf(16, D // 4), dma((7,)),
    ]
    return pl.pallas_call(
        kernel,
        out_shape=out_shape,
        in_specs=[any_] * 2 + [smem] * 3 + [vmem] * 4 + [any_] * 4,
        out_specs=[any_] * 18,
        scratch_shapes=scratch,
        compiler_params=pltpu.CompilerParams(
            collective_id=0, has_side_effects=True, vmem_limit_bytes=64 * 2**20 - 2**16
        ),
        cost_estimate=pl.CostEstimate(flops=42 * 10**9, bytes_accessed=10**8, transcendentals=10**7),
    )(tokens, out_grad, lengths, self_flags, episode_weight, g1, b1, g2, b2, w_qkv, w_out, w_up, w_down)


def last_step(z, y, gin, norms, ro, rx, ry):
    S, R, D, LW, F, PD = z.S, z.R, z.D, z.LW, z.F, z.D // 8
    steps = 2
    wide, slim = F // steps, LW // steps
    offsets = [(wide, 0), (wide, steps)]
    base = 2 * F // slim
    offsets += [(slim, base + k * steps) for k in range(4)]

    def kernel(*refs):
        y_in, gin_in, norms_in = refs[:3]
        parts = refs[3:21]
        out, gout, qkv, proj, up, down, one, two = refs[21:]

        def total(k):
            return parts[k][...].astype(f32) + parts[6 + k][...].astype(f32) + parts[12 + k][...].astype(f32)

        down[...] = total(0).T
        up[...] = total(1)
        proj[...] = total(2).T
        for j in range(3):
            qkv[j] = total(3 + j)
        for r in range(R):
            gout[:, r, :] = gin_in[r]
        out[...] = jnp.stack([y_in[r].astype(f32) for r in range(R)], axis=1).astype(bf16)
        for k, ref in enumerate((one, two)):
            for i in range(8):
                ref[i // 4 : i // 4 + 1, (i % 4) * (D // 4) : (i % 4 + 1) * (D // 4)] = norms_in[k * 8 + i : k * 8 + i + 1, :]

    spec = pl.BlockSpec
    rows = spec((R, S // steps, D), lambda i: (0, i, 0))
    in_specs = [rows, rows, spec((16, D // 4), lambda i: (0, 0))]
    for _ in range(3):
        in_specs += [spec((PD, w), lambda i, o=o: (0, o + i)) for w, o in offsets]
    sds = jax.ShapeDtypeStruct
    return pl.pallas_call(
        kernel,
        grid=(steps,),
        out_shape=[
            sds((S, R, D), bf16), sds((S, R, D), f32), sds((3, PD, LW), f32), sds((LW, PD), f32), sds((PD, F), f32),
            sds((F, PD), f32), sds((2, D), f32), sds((2, D), f32),
        ],
        in_specs=in_specs,
        out_specs=[
            spec((S // steps, R, D), lambda i: (i, 0, 0)), spec((S // steps, R, D), lambda i: (i, 0, 0)),
            spec((3, PD, slim), lambda i: (0, 0, i)), spec((slim, PD), lambda i: (i, 0)),
            spec((PD, wide), lambda i: (0, i)), spec((wide, PD), lambda i: (i, 0)), spec((2, D), lambda i: (0, 0)),
            spec((2, D), lambda i: (0, 0)),
        ],
        compiler_params=pltpu.CompilerParams(vmem_limit_bytes=64 * 2**20 - 2**16),
    )(y, gin, norms, *([ro] * 6 + [rx] * 6 + [ry] * 6))


def solution(mesh):
    shape = dict(mesh.shape)

    def on_device(
        tokens, lengths, self_flags, episode_weight, ln1_gain, ln1_bias, w_qkv, w_out, ln2_gain, ln2_bias, w_up,
        w_down, out_grad,
    ):
        z = Sizes(shape, tokens.shape, w_qkv.shape, w_up.shape, lengths.shape)
        row = lambda a: a.reshape(1, -1)
        results = layer(
            z, tokens, out_grad, lengths, self_flags, episode_weight, row(ln1_gain), row(ln1_bias), row(ln2_gain),
            row(ln2_bias), jnp.transpose(w_qkv, (1, 0, 2)), w_out, w_up, w_down,
        )
        y, gin, norms, ro, rx, ry = results[:6]
        if z.pairs:
            output, grad_input, qkv, grad_out, grad_up, grad_down, one, two = last_step(z, y, gin, norms, ro, rx, ry)
            return output, grad_input, jnp.transpose(qkv, (1, 0, 2)), grad_out, grad_up, grad_down, one, two
        output = jnp.transpose(y, (1, 0, 2))
        grad_input = jnp.transpose(gin, (1, 0, 2))
        g1_all, g2_all, gy_all, gm_all, act, gpre, gproj, att = results[10:]

        def over_tokens(a, b, dim):
            value = jnp.einsum("ta,tb->ab", a, b, preferred_element_type=f32).astype(bf16)
            return lax.psum_scatter(value, ("dp", "sp"), scatter_dimension=dim, tiled=True).astype(f32)

        grad_down = over_tokens(act, gy_all, 1)
        grad_up = over_tokens(g2_all, gpre, 0)
        grad_out = over_tokens(att, gm_all, 1)
        grad_qkv = over_tokens(g1_all, gproj, 0).reshape(-1, 3, z.LW)
        both = lax.psum(norms, ("dp", "sp", "tp"))
        both = both.reshape(2, 2, -1)
        return output, grad_input, grad_qkv, grad_out, grad_up, grad_down, both[0], both[1]

    return jax.shard_map(
        on_device,
        mesh=mesh,
        in_specs=(
            P(("sp", "tp"), "dp", None), P("dp", None), P("dp", None), P("dp", None), P(), P(), P(None, None, "tp"),
            P("tp", None), P(), P(), P(None, "tp"), P("tp", None), P(("sp", "tp"), "dp", None),
        ),
        out_specs=(
            P(("sp", "tp"), "dp", None), P(("sp", "tp"), "dp", None), P(("dp", "sp"), None, "tp"),
            P("tp", ("dp", "sp")), P(("dp", "sp"), "tp"), P("tp", ("dp", "sp")), P(), P(),
        ),
        check_vma=False,
    )
```
